32 devices in a mesh: kv: 2 (over y), blk: 16 (over z, x, core).
Axes of the slice: x: 2, y: 2, z: 4, core: 2. Of those that a mesh axis runs over, the one named last changes fastest.
Arguments:
- hidden_in: bfloat16 [8192, 1280], P('blk'), may hold values from -6 to 6
- w_query: bfloat16 [1280, 1280], P(None, 'kv'), may hold values from -0.15625 to 0.15625
- w_key: bfloat16 [1280, 1280], P(None, 'kv'), may hold values from -0.15625 to 0.15625
- w_value: bfloat16 [1280, 1280], P(None, 'kv'), may hold values from -0.15625 to 0.15625
- w_out: bfloat16 [1280, 1280], P('kv'), may hold values from -0.15625 to 0.15625
- head_gain: float32 [1280], P('kv'), may hold values from 1 to 2.5
- eigen_rate: float32 [1280], replicated, may hold values from 0.15 to 0.6
- pool_keys: bfloat16 [64, 256, 1280], P('blk', None, 'kv'), may hold values from -2 to 2
- pool_values: bfloat16 [64, 256, 1280], P('blk', None, 'kv'), may hold values from -6 to 6
- req_len: int32 [16], P('blk'), may hold values from 1 to 512, as said below
- prefix_len: int32 [16], P('blk'), may hold values from 0 to 4, as said below
- prefix_pages: int32 [16, 4], replicated, may hold values from 0 to 63, as said below
- placement: int32 [32], replicated, may hold values from 0 to 31, as said below
Outputs:
- layer_out: bfloat16 [8192, 1280], P('blk')
- new_keys: bfloat16 [32, 256, 1280], P('blk', None, 'kv')
- new_values: bfloat16 [32, 256, 1280], P('blk', None, 'kv')
The draws below stay inside these ranges and needn't reach their ends.
Inputs may be any that keep to these rules, and one draw needn't show every extreme that they name: `req_len`: some request has all 512 tokens live. `prefix_len`: some request has 4 cached pages. Page prefix_pages[r, s] lies among pages h * 4 to (h + 1) * 4 - 1 with h = (r + 1 + s * 4) mod 16, for every slot s. Each page once; placement[b] lies among pages e * 2 to (e + 1) * 2 - 1 with e = (b // 2 + (2 * (b mod 2) + 1) * 4) mod 16.
All inputs are finite; a program needn't handle non-finite values.
Results may differ from the reference program's by a relative error of at most 0.0067.
Values may be sent and summed in bfloat16 or wider, within the bound.
No kernel may reach another device: no remote copies, remote signals or barrier semaphores. Data moves between devices by JAX's collectives and lax.ppermute only.
A program may use at most 128 MiB of HBM per device.

```python
import math
import jax
import jax.numpy as jnp
from jax import lax

D = 1280
HEADS = 20
HD = 64
PAGE = 256
TOK_DEV = 512
PMAX = 4
POOL_REQ = 4
REQS = 16
TOKENS = 8192
NEWPAGES = 32
POOL = 64


def draw_req_len(key, part):
    counts = jax.random.randint(key, (REQS,), 1, TOK_DEV + 1)
    chosen = jax.random.randint(jax.random.fold_in(key, 7), (), 0, REQS)
    return jnp.where(jnp.arange(REQS) == chosen, TOK_DEV, counts).astype(jnp.int32)


def draw_prefix_len(key, part):
    counts = jax.random.randint(key, (REQS,), 0, PMAX + 1)
    chosen = jax.random.randint(jax.random.fold_in(key, 11), (), 0, REQS)
    return jnp.where(jnp.arange(REQS) == chosen, PMAX, counts).astype(jnp.int32)


def draw_prefix_pages(key, part):
    request = jnp.arange(REQS, dtype=jnp.int32)[:, None]
    slot = jnp.arange(PMAX, dtype=jnp.int32)[None, :]
    holder = (request + 1 + slot * REQS // PMAX) % REQS
    local = jax.random.randint(jax.random.fold_in(key, 13), (REQS, PMAX), 0, POOL_REQ)
    local = jnp.where((request == REQS - 1) & (slot == 0), 0, local)
    local = jnp.where((request == REQS - 2) & (slot == 0), POOL_REQ - 1, local)
    return (holder * POOL_REQ + local).astype(jnp.int32)


def draw_placement(key, part):
    per_dev = TOK_DEV // PAGE
    scores = jax.random.randint(jax.random.fold_in(key, 17), (REQS, per_dev), 0, 1 << 20)
    scores = scores * per_dev + jnp.arange(per_dev, dtype=jnp.int32)[None, :]
    order = jnp.argsort(scores, axis=1).astype(jnp.int32)
    source = jnp.arange(REQS, dtype=jnp.int32)[:, None]
    block = jnp.arange(per_dev, dtype=jnp.int32)[None, :]
    target = (source + (2 * block + 1) * REQS // (2 * per_dev)) % REQS
    slot = order[target, block]
    return (target * per_dev + slot).reshape(-1).astype(jnp.int32)


def levels(stream_key, dims, pieces, smallest, high):
    factor_of, own = 1.0, jax.random.fold_in(stream_key, 6)
    for position, shards_of in pieces:
        heights = jnp.exp(jax.random.uniform(jax.random.fold_in(own, position), (shards_of,), jnp.float32, smallest / len(pieces), high / len(pieces)))
        factor_of = factor_of * jnp.repeat(heights, dims[position] // shards_of).reshape([-1 if axis == position else 1 for axis in range(len(dims))])
    return factor_of


def noise(rng, dims, scale, reach, split=(), held_as=jnp.bfloat16):
    factor_of = levels(rng, dims, split, -0.22, 0.18) if split else 1.0
    entries = jax.random.normal(rng, dims, jnp.float32) * scale * factor_of
    return jnp.minimum(jnp.maximum(entries, -reach), reach).astype(held_as)


def setup_inputs(seed: int = 0) -> dict:
    key_list = jax.random.split(jax.random.key(seed), 14)
    return {
        "hidden_in": noise(key_list[0], (TOKENS, D), 1.0, 6.0, ((0, 16),)),
        "w_query": noise(key_list[1], (D, D), D ** -0.5, 0.15625, ((1, 2),)),
        "w_key": noise(key_list[2], (D, D), D ** -0.5, 0.15625, ((1, 2),)),
        "w_value": noise(key_list[3], (D, D), D ** -0.5, 0.15625, ((1, 2),)),
        "w_out": noise(key_list[4], (D, D), D ** -0.5, 0.15625, ((0, 2),)),
        "head_gain": jnp.clip(jnp.exp(math.log(2.5) - 0.916290732 * jax.random.uniform(key_list[5], (D,), jnp.float32) ** levels(key_list[5], (D,), ((0, 2),), -0.2, 0.2)), 1.0, 2.5),
        "eigen_rate": jnp.clip(jnp.exp(jax.random.uniform(key_list[6], (D,), jnp.float32, math.log(0.15), math.log(0.6))), 0.15, 0.6),
        "pool_keys": jnp.clip(jax.random.uniform(key_list[7], (POOL, PAGE, D), jnp.float32, -2.0, 2.0) * levels(key_list[7], (POOL, PAGE, D), ((0, 16), (2, 2)), -0.4, 0.0), -2.0, 2.0).astype(jnp.bfloat16),
        "pool_values": noise(key_list[8], (POOL, PAGE, D), 1.0, 6.0, ((0, 16), (2, 2))),
        "req_len": draw_req_len(jax.random.fold_in(key_list[13], 71), 0),
        "prefix_len": draw_prefix_len(jax.random.fold_in(key_list[13], 71), 0),
        "prefix_pages": draw_prefix_pages(jax.random.fold_in(key_list[13], 71), 0),
        "placement": draw_placement(jax.random.fold_in(key_list[13], 71), 0),
    }


epsilon = 1e-06

def rms_scale(values):
    return values * lax.rsqrt(lax.optimization_barrier(jnp.mean(values * values, axis=-1, keepdims=True)) + epsilon)

def head_normed(projected, head_gain):
    count = projected.shape[0]
    split_heads = projected.reshape(count, -1, HD)
    return (rms_scale(split_heads).reshape(count, -1) * head_gain).astype(jnp.bfloat16)

def reference(hidden_in, w_query, w_key, w_value, w_out, head_gain, eigen_rate, pool_keys, pool_values, req_len, prefix_len, prefix_pages, placement):
    hidden_f = hidden_in.astype(jnp.float32)
    row_scale = lax.rsqrt(lax.optimization_barrier(jnp.mean(hidden_f * hidden_f, axis=-1, keepdims=True)) + epsilon)
    anchor = hidden_f * row_scale
    queries = head_normed(jnp.dot(hidden_in, w_query, preferred_element_type=jnp.float32), head_gain)
    key_rows = head_normed(jnp.dot(hidden_in, w_key, preferred_element_type=jnp.float32), head_gain)
    value_rows = (jnp.dot(hidden_in, w_value, preferred_element_type=jnp.float32) * row_scale).astype(jnp.bfloat16)

    def one_request(items):
        query_block, key_block, value_block, live_count, depth, pages = items
        cached_keys = pool_keys[pages].reshape(PMAX * PAGE, D)
        cached_values = pool_values[pages].reshape(PMAX * PAGE, D)
        all_keys = jnp.concatenate([key_block, cached_keys], axis=0)
        all_values = jnp.concatenate([value_block, cached_values], axis=0)
        row_index = jnp.arange(TOK_DEV, dtype=jnp.int32)[:, None]
        col_index = jnp.arange(TOK_DEV + PMAX * PAGE, dtype=jnp.int32)[None, :]
        own_part = (col_index <= row_index) & (col_index < live_count)
        cached_part = (col_index >= TOK_DEV) & ((col_index - TOK_DEV) // PAGE < depth)
        visible = own_part | cached_part
        query_heads = query_block.astype(jnp.float32).reshape(TOK_DEV, HEADS, HD)
        key_heads = all_keys.astype(jnp.float32).reshape(-1, HEADS, HD)
        value_heads = all_values.astype(jnp.float32).reshape(-1, HEADS, HD)
        scores = jnp.einsum('qhd,khd->hqk', query_heads, key_heads) / math.sqrt(HD)
        weights = jnp.where(visible[None], jnp.exp(scores), 0.0)
        totals = lax.optimization_barrier(jnp.sum(weights, axis=-1))
        rounded = lax.optimization_barrier(weights.astype(jnp.bfloat16)).astype(jnp.float32)
        mixed = jnp.einsum('hqk,khd->qhd', rounded, value_heads)
        return (mixed / totals.T[:, :, None]).astype(jnp.bfloat16).reshape(TOK_DEV, D)
    attended = lax.map(one_request, (queries.reshape(REQS, TOK_DEV, D), key_rows.reshape(REQS, TOK_DEV, D), value_rows.reshape(REQS, TOK_DEV, D), req_len, prefix_len, prefix_pages))
    attended = attended.reshape(TOKENS, D)
    branch = jnp.dot(attended, w_out, preferred_element_type=jnp.float32)
    updated = anchor + eigen_rate * (rms_scale(branch) - anchor)
    layer_out = rms_scale(updated).astype(jnp.bfloat16)
    key_pages = key_rows.reshape(NEWPAGES, PAGE, D)
    value_pages = value_rows.reshape(NEWPAGES, PAGE, D)
    new_keys = jnp.zeros_like(key_pages).at[placement].set(key_pages)
    new_values = jnp.zeros_like(value_pages).at[placement].set(value_pages)
    return (layer_out, new_keys, new_values)
```

```python
import functools
import math

import jax
import jax.numpy as jnp
from jax import lax
from jax.experimental import pallas as pl
from jax.experimental.pallas import tpu as pltpu
from jax.sharding import PartitionSpec as P

HD = 64
PAGE = 256
PMAX = 4
LANES = 128
GROUPS = (256, 256, 128)
VMEM_LIMIT = 48 * 1024 * 1024

epsilon = 1e-06

f32 = jnp.float32
bf16 = jnp.bfloat16


def from_behind(block, axis, distance):
    devices = range(lax.axis_size(axis))
    route = [((i - distance) % len(devices), i) for i in devices]
    return lax.ppermute(block, axis, route)


def group_slices(width):
    slices, start = [], 0
    for size in GROUPS:
        slices.append((start, size))
        start += size
    assert start == width
    return slices


def params():
    return pltpu.CompilerParams(vmem_limit_bytes=VMEM_LIMIT)


def cost(flops, bytes_accessed, transcendentals=0):
    return pl.CostEstimate(
        flops=flops, bytes_accessed=bytes_accessed, transcendentals=transcendentals
    )


def pack_kernel(slices, blocks, local_ref, kv_ref, hidden, keys, values, *rest):
    outs, sem = rest[:-1], rest[-1]
    half = PAGE // 2
    copies = []
    for block in range(blocks):
        rows = pl.ds(pl.multiple_of(block * PAGE + kv_ref[0] * half, half), half)
        copies.append((hidden.at[rows], outs[block]))
    place = blocks
    for start, size in slices:
        for slot in range(PMAX):
            local = local_ref[slot]
            columns = pl.ds(start, size)
            copies.append((keys.at[local, :, columns], outs[place].at[0]))
            copies.append((values.at[local, :, columns], outs[place].at[1]))
            place += 1
    started = []
    for index, (source, target) in enumerate(copies):
        copy = pltpu.make_async_copy(source, target, sem.at[index])
        copy.start()
        started.append(copy)
    for copy in started:
        copy.wait()


def pack(hidden_in, pool_keys, pool_values, local, kv_index, blocks):
    width = pool_keys.shape[2]
    slices = group_slices(width)
    outs = [jax.ShapeDtypeStruct((PAGE // 2, hidden_in.shape[1]), bf16)] * blocks
    for _, size in slices:
        outs += [jax.ShapeDtypeStruct((2, PAGE, size), bf16)] * PMAX
    count = blocks + 2 * PMAX * len(slices)
    result = pl.pallas_call(
        functools.partial(pack_kernel, slices, blocks),
        grid_spec=pltpu.PrefetchScalarGridSpec(
            num_scalar_prefetch=2,
            grid=(1,),
            in_specs=[pl.BlockSpec(memory_space=pl.ANY)] * 3,
            out_specs=[pl.BlockSpec(memory_space=pl.ANY)] * len(outs),
            scratch_shapes=[pltpu.SemaphoreType.DMA((count,))],
        ),
        out_shape=outs,
        compiler_params=params(),
        name="pack",
    )(local, kv_index, hidden_in, pool_keys, pool_values)
    relays = result[:blocks]
    pages = [result[blocks + PMAX * g : blocks + PMAX * (g + 1)] for g in range(len(slices))]
    return relays, pages


def head_sum_matrix():
    rows = lax.broadcasted_iota(jnp.int32, (LANES, LANES), 0) // HD
    cols = lax.broadcasted_iota(jnp.int32, (LANES, LANES), 1) // HD
    return jnp.where(rows == cols, 1.0 / HD, 0.0).astype(bf16)


def head_norm(projected, gain, matrix):
    parts = []
    for start in range(0, projected.shape[1], LANES):
        part = projected[:, start : start + LANES]
        squares = part * part
        high = squares.astype(bf16)
        low = (squares - high.astype(f32)).astype(bf16)
        mean = jnp.dot(high, matrix, preferred_element_type=f32)
        mean += jnp.dot(low, matrix, preferred_element_type=f32)
        parts.append(part * lax.rsqrt(mean + epsilon) * gain[:, start : start + LANES])
    return jnp.concatenate(parts, axis=1) if len(parts) > 1 else parts[0]


def row_scale_of(hidden):
    hidden_f = hidden.astype(f32)
    return lax.rsqrt(jnp.mean(hidden_f * hidden_f, axis=-1, keepdims=True) + epsilon)


def project_kernel(slices, hidden, wq, wk, wv, gain, *outs):
    matrix = head_sum_matrix()
    rows_all = hidden.shape[0]
    for low in range(0, rows_all, PAGE):
        rows = slice(low, low + PAGE)
        x = hidden[rows, :]
        scale = row_scale_of(x)
        for g, (start, size) in enumerate(slices):
            cols = slice(start, start + size)
            q = jnp.dot(x, wq[:, cols], preferred_element_type=f32)
            q = head_norm(q, gain[:, cols], matrix).astype(bf16)
            outs[3 * g][rows, :] = q * jnp.asarray(1.0 / math.sqrt(HD), bf16)
            k = jnp.dot(x, wk[:, cols], preferred_element_type=f32)
            outs[3 * g + 1][rows, :] = head_norm(k, gain[:, cols], matrix).astype(bf16)
            v = jnp.dot(x, wv[:, cols], preferred_element_type=f32)
            outs[3 * g + 2][rows, :] = (v * scale).astype(bf16)


def project(hidden_in, wq, wk, wv, gain):
    tokens, depth = hidden_in.shape
    width = wq.shape[1]
    slices = group_slices(width)
    outs = []
    for _, size in slices:
        outs += [jax.ShapeDtypeStruct((tokens, size), bf16)] * 3
    flat = pl.pallas_call(
        functools.partial(project_kernel, slices),
        out_shape=outs,
        compiler_params=params(),
        cost_estimate=cost(6 * tokens * depth * width, 8 * 1024 * 1024),
        name="project",
    )(hidden_in, wq, wk, wv, gain)
    return [flat[3 * g : 3 * g + 3] for g in range(len(slices))]


def relay_kernel(slices, blocks, kv_ref, slot_ref, *refs):
    mine = refs[:blocks]
    theirs = refs[blocks : 2 * blocks]
    wk, wv, gain, key_out, value_out, rows_buf = refs[2 * blocks :]
    matrix = head_sum_matrix()
    half = PAGE // 2
    for block in range(blocks):
        near = pl.multiple_of(kv_ref[0] * half, half)
        far = pl.multiple_of((1 - kv_ref[0]) * half, half)
        rows_buf[pl.ds(near, half), :] = mine[block][...]
        rows_buf[pl.ds(far, half), :] = theirs[block][...]
        x = rows_buf[...]
        scale = row_scale_of(x)
        slot = slot_ref[block]
        for start, size in slices:
            cols = slice(start, start + size)
            k = jnp.dot(x, wk[:, cols], preferred_element_type=f32)
            key_out[slot, :, cols] = head_norm(k, gain[:, cols], matrix).astype(bf16)
            v = jnp.dot(x, wv[:, cols], preferred_element_type=f32)
            value_out[slot, :, cols] = (v * scale).astype(bf16)


def relay_project(mine, theirs, wk, wv, gain, kv_index, slots):
    blocks = len(mine)
    depth, width = wk.shape
    out = jax.ShapeDtypeStruct((blocks, PAGE, width), bf16)
    smem = pl.BlockSpec(memory_space=pltpu.SMEM)
    vmem = pl.BlockSpec(memory_space=pltpu.VMEM)
    return pl.pallas_call(
        functools.partial(relay_kernel, group_slices(width), blocks),
        in_specs=[smem, smem] + [vmem] * (2 * blocks + 3),
        out_specs=[vmem, vmem],
        out_shape=[out, out],
        scratch_shapes=[pltpu.VMEM((PAGE, depth), bf16)],
        compiler_params=params(),
        cost_estimate=cost(4 * blocks * PAGE * depth * width, 8 * 1024 * 1024),
        name="relay_project",
    )(kv_index, slots, *mine, *theirs, wk, wv, gain)


def attend_kernel(live_ref, depth_ref, q_ref, k_ref, v_ref, p0, p1, p2, p3, out):
    pages = (p0, p1, p2, p3)
    tokens, width = q_ref.shape
    live, depth = live_ref[0], depth_ref[0]
    lane = lax.broadcasted_iota(jnp.int32, (1, LANES), 1)
    row = lax.broadcasted_iota(jnp.int32, (PAGE, PAGE), 0)
    col = lax.broadcasted_iota(jnp.int32, (PAGE, PAGE), 1)
    causal = col <= row
    key_row = lax.broadcasted_iota(jnp.int32, (PAGE, LANES), 0)
    blocks = tokens // PAGE
    for start in range(0, width, LANES):
        cols = slice(start, start + LANES)
        keys, values = [], []
        for b in range(blocks):
            rows = slice(b * PAGE, (b + 1) * PAGE)
            keep = (key_row + b * PAGE) < live
            keys.append(k_ref[rows, cols])
            shown = jnp.where(keep, v_ref[rows, cols].astype(f32), 0.0).astype(bf16)
            ones = jnp.where(keep, 1.0, 0.0).astype(bf16)
            values.append(jnp.concatenate([shown, ones], axis=1))
        for p in range(PMAX):
            keep = jnp.where(p < depth, 1.0, 0.0).astype(bf16)
            keys.append(pages[p][0, :, cols])
            ones = jnp.full((PAGE, LANES), 1.0, bf16) * keep
            values.append(jnp.concatenate([pages[p][1, :, cols] * keep, ones], axis=1))
        for b in range(blocks):
            rows = slice(b * PAGE, (b + 1) * PAGE)
            q = q_ref[rows, cols]
            ratios = []
            for side in range(2):
                q_side = jnp.where((lane // HD) == side, q, jnp.zeros_like(q))
                acc = jnp.zeros((PAGE, 2 * LANES), f32)
                for j in list(range(b + 1)) + list(range(blocks, blocks + PMAX)):
                    scores = lax.dot_general(
                        q_side, keys[j], (((1,), (1,)), ((), ())), preferred_element_type=f32
                    )
                    weights = jnp.exp(scores)
                    if j == b:
                        weights = jnp.where(causal, weights, 0.0)
                    acc += jnp.dot(weights.astype(bf16), values[j], preferred_element_type=f32)
                ratios.append(acc[:, :LANES] / acc[:, LANES:])
            out[rows, cols] = jnp.where((lane // HD) == 0, ratios[0], ratios[1]).astype(bf16)


def attend(live, depth, q, k, v, pages):
    tokens, width = q.shape
    heads = width // HD
    smem = pl.BlockSpec(memory_space=pltpu.SMEM)
    vmem = pl.BlockSpec(memory_space=pltpu.VMEM)
    keys = tokens + PMAX * PAGE
    return pl.pallas_call(
        attend_kernel,
        in_specs=[smem, smem] + [vmem] * 7,
        out_specs=vmem,
        out_shape=jax.ShapeDtypeStruct((tokens, width), bf16),
        compiler_params=params(),
        cost_estimate=cost(
            16 * heads * tokens * keys * HD, 2 * 1024 * 1024, heads * tokens * keys
        ),
        name="attend",
    )(live, depth, q, k, v, *pages)


def finish_kernel(slices, count, *refs):
    hidden, w_mine, w_theirs, rate = refs[:4]
    mine = refs[4 : 4 + count]
    theirs = refs[4 + count : 4 + 2 * count]
    out = refs[4 + 2 * count]

    def half(parts, weights):
        total = None
        for part, (start, size) in zip(parts, slices):
            term = jnp.dot(part[...], weights[start : start + size, :], preferred_element_type=f32)
            total = term if total is None else total + term
        return total

    branch = half(mine, w_mine) + half(theirs, w_theirs)
    hidden_f = hidden[...].astype(f32)
    anchor = hidden_f * lax.rsqrt(jnp.mean(hidden_f * hidden_f, axis=-1, keepdims=True) + epsilon)
    normed = branch * lax.rsqrt(jnp.mean(branch * branch, axis=-1, keepdims=True) + epsilon)
    updated = anchor + rate[...] * (normed - anchor)
    scale = lax.rsqrt(jnp.mean(updated * updated, axis=-1, keepdims=True) + epsilon)
    out[...] = (updated * scale).astype(bf16)


def finish(hidden_in, w_mine, w_theirs, rate, mine, theirs):
    tokens, depth = hidden_in.shape
    width = w_mine.shape[0]
    slices = group_slices(width)
    step = 256
    by_rows = lambda size: pl.BlockSpec((step, size), lambda i: (i, 0))
    whole = lambda shape: pl.BlockSpec(shape, lambda i: (0, 0))
    return pl.pallas_call(
        functools.partial(finish_kernel, slices, len(slices)),
        grid=(tokens // step,),
        in_specs=[by_rows(depth), whole(w_mine.shape), whole(w_theirs.shape), whole(rate.shape)]
        + [by_rows(size) for _, size in slices] * 2,
        out_specs=by_rows(depth),
        out_shape=jax.ShapeDtypeStruct((tokens, depth), bf16),
        compiler_params=params(),
        cost_estimate=cost(4 * tokens * depth * width, 8 * 1024 * 1024),
        name="finish",
    )(hidden_in, w_mine, w_theirs, rate, *mine, *theirs)


def body(
    hidden_in,
    w_query,
    w_key,
    w_value,
    w_out,
    head_gain,
    eigen_rate,
    pool_keys,
    pool_values,
    req_len,
    prefix_len,
    prefix_pages,
    placement,
):
    devices = lax.axis_size("blk")
    here = lax.axis_index("blk")
    kv_index = lax.axis_index("kv").astype(jnp.int32).reshape(1)
    blocks = hidden_in.shape[0] // PAGE
    gain = head_gain.reshape(1, -1)
    rate = eigen_rate.reshape(1, -1)

    page_offsets = [slot * devices // PMAX + 1 for slot in range(PMAX)]
    askers = (here - jnp.asarray(page_offsets, jnp.int32)) % devices
    local = prefix_pages[askers, jnp.arange(PMAX)] % pool_keys.shape[0]
    block_offsets = [(2 * b + 1) * devices // (2 * blocks) for b in range(blocks)]
    sources = (here - jnp.asarray(block_offsets, jnp.int32)) % devices
    slots = placement[sources * blocks + jnp.arange(blocks)] % blocks

    relay_send, page_send = pack(hidden_in, pool_keys, pool_values, local, kv_index, blocks)
    relay_mine = [from_behind(relay_send[b], "blk", block_offsets[b]) for b in range(blocks)]
    pages = [
        [from_behind(sent[s], "blk", devices - page_offsets[s]) for s in range(PMAX)]
        for sent in page_send
    ]
    w_theirs = from_behind(w_out, "kv", 1)
    projected = project(hidden_in, w_query, w_key, w_value, gain)
    relay_theirs = [from_behind(rows, "kv", 1) for rows in relay_mine]

    mine, theirs = [], []
    for g, (q, k, v) in enumerate(projected):
        attended = attend(req_len, prefix_len, q, k, v, pages[g])
        mine.append(attended)
        theirs.append(from_behind(attended, "kv", 1))
    new_keys, new_values = relay_project(
        relay_mine, relay_theirs, w_key, w_value, gain, kv_index, slots
    )
    layer_out = finish(hidden_in, w_out, w_theirs, rate, mine, theirs)
    return (layer_out, new_keys, new_values)


def solution(mesh):
    in_specs = (
        P("blk", None),
        P(None, "kv"),
        P(None, "kv"),
        P(None, "kv"),
        P("kv", None),
        P("kv"),
        P(),
        P("blk", None, "kv"),
        P("blk", None, "kv"),
        P("blk"),
        P("blk"),
        P(),
        P(),
    )
    out_specs = (P("blk", None), P("blk", None, "kv"), P("blk", None, "kv"))
    return jax.shard_map(body, mesh=mesh, in_specs=in_specs, out_specs=out_specs, check_vma=False)
```

```python
import functools
import math

import jax
import jax.numpy as jnp
from jax import lax
from jax.experimental import pallas as pl
from jax.experimental.pallas import tpu as pltpu
from jax.sharding import PartitionSpec as P

HD = 64
PAGE = 256
PMAX = 4
LANES = 128
GROUPS = (256, 256, 128)
WINDOW = 4
SLOT_ORDER = (2, 1, 3, 0)
VMEM_LIMIT = 16 * 1024 * 1024

epsilon = 1e-06

f32 = jnp.float32
bf16 = jnp.bfloat16


def from_behind(block, axis, distance):
    devices = range(lax.axis_size(axis))
    route = [((i - distance) % len(devices), i) for i in devices]
    return lax.ppermute(block, axis, route)


def after(block, *others):
    return lax.optimization_barrier((block, *others))[0]


def group_slices(width):
    slices, start = [], 0
    for size in GROUPS:
        slices.append((start, size))
        start += size
    assert start == width
    return slices


def params():
    return pltpu.CompilerParams(vmem_limit_bytes=VMEM_LIMIT)


def cost(flops, bytes_accessed, transcendentals=0):
    return pl.CostEstimate(
        flops=flops, bytes_accessed=bytes_accessed, transcendentals=transcendentals
    )


def split_kernel(blocks, kv_ref, hidden, *rest):
    outs, sem = rest[:-1], rest[-1]
    half = PAGE // 2
    copies = []
    for block in range(blocks):
        rows = pl.ds(pl.multiple_of(block * PAGE + kv_ref[0] * half, half), half)
        copies.append(pltpu.make_async_copy(hidden.at[rows], outs[block], sem.at[block]))
    for copy in copies:
        copy.start()
    for copy in copies:
        copy.wait()


def split_rows(hidden_in, kv_index, blocks):
    out = jax.ShapeDtypeStruct((PAGE // 2, hidden_in.shape[1]), bf16)
    return pl.pallas_call(
        functools.partial(split_kernel, blocks),
        in_specs=[pl.BlockSpec(memory_space=pltpu.SMEM), pl.BlockSpec(memory_space=pl.ANY)],
        out_specs=[pl.BlockSpec(memory_space=pltpu.VMEM)] * blocks,
        out_shape=[out] * blocks,
        scratch_shapes=[pltpu.SemaphoreType.DMA((blocks,))],
        compiler_params=params(),
        name="split_rows",
    )(kv_index, hidden_in)


def pack_kernel(slices, devices, offsets, here_ref, table, keys, values, _, *rest):
    outs, (buf, sem) = rest[:-2], rest[-2:]
    copies = []
    for slot in range(PMAX):
        asker = lax.rem(here_ref[0] + (devices - offsets[slot]), devices)
        local = lax.rem(table[asker * PMAX + slot], keys.shape[0])
        for side, pool in enumerate((keys, values)):
            index = 2 * slot + side
            copies.append(pltpu.make_async_copy(pool.at[local], buf.at[index], sem.at[index]))
    for copy in copies:
        copy.start()
    for slot in range(PMAX):
        for side in range(2):
            index = 2 * slot + side
            copies[index].wait()
            for g, (start, size) in enumerate(slices):
                outs[g * PMAX + slot][side] = buf[index, :, start : start + size]


def pack(pool_keys, pool_values, table, here, devices, offsets, first):
    width = pool_keys.shape[2]
    slices = group_slices(width)
    outs = []
    for _, size in slices:
        outs += [jax.ShapeDtypeStruct((2, PAGE, size), bf16)] * PMAX
    smem = pl.BlockSpec(memory_space=pltpu.SMEM)
    hbm = pl.BlockSpec(memory_space=pl.ANY)
    result = pl.pallas_call(
        functools.partial(pack_kernel, slices, devices, offsets),
        in_specs=[smem, smem, hbm, hbm, hbm],
        out_specs=[pl.BlockSpec(memory_space=pltpu.VMEM)] * len(outs),
        out_shape=outs,
        scratch_shapes=[
            pltpu.VMEM((2 * PMAX, PAGE, width), bf16),
            pltpu.SemaphoreType.DMA((2 * PMAX,)),
        ],
        compiler_params=params(),
        name="pack",
    )(here, table, pool_keys, pool_values, first)
    return [result[PMAX * g : PMAX * (g + 1)] for g in range(len(slices))]


def head_sum_matrix():
    rows = (lax.broadcasted_iota(jnp.int32, (2 * LANES, LANES), 0) % LANES) // HD
    cols = lax.broadcasted_iota(jnp.int32, (2 * LANES, LANES), 1) // HD
    return jnp.where(rows == cols, 1.0 / HD, 0.0).astype(bf16)


def head_norm(projected, gain, matrix):
    parts = []
    for start in range(0, projected.shape[1], LANES):
        part = projected[:, start : start + LANES]
        squares = part * part
        high = squares.astype(bf16)
        low = (squares - high.astype(f32)).astype(bf16)
        both = jnp.concatenate([high, low], axis=1)
        mean = jnp.dot(both, matrix, preferred_element_type=f32)
        parts.append(part * lax.rsqrt(mean + epsilon) * gain[:, start : start + LANES])
    return jnp.concatenate(parts, axis=1) if len(parts) > 1 else parts[0]


def row_scale_of(hidden):
    hidden_f = hidden.astype(f32)
    return lax.rsqrt(jnp.mean(hidden_f * hidden_f, axis=-1, keepdims=True) + epsilon)


def project_kernel(slices, hidden, wq, wk, wv, gain, *outs):
    matrix = head_sum_matrix()
    rows_all = hidden.shape[0]
    for low in range(0, rows_all, PAGE):
        rows = slice(low, low + PAGE)
        x = hidden[rows, :]
        scale = row_scale_of(x)
        for g, (start, size) in enumerate(slices):
            cols = slice(start, start + size)
            q = jnp.dot(x, wq[:, cols], preferred_element_type=f32)
            q = head_norm(q, gain[:, cols], matrix).astype(bf16)
            outs[3 * g][rows, :] = q * jnp.asarray(1.0 / math.sqrt(HD), bf16)
            k = jnp.dot(x, wk[:, cols], preferred_element_type=f32)
            outs[3 * g + 1][rows, :] = head_norm(k, gain[:, cols], matrix).astype(bf16)
            v = jnp.dot(x, wv[:, cols], preferred_element_type=f32)
            outs[3 * g + 2][rows, :] = (v * scale).astype(bf16)


def project(hidden_in, wq, wk, wv, gain):
    tokens, depth = hidden_in.shape
    width = wq.shape[1]
    slices = group_slices(width)
    outs = []
    for _, size in slices:
        outs += [jax.ShapeDtypeStruct((tokens, size), bf16)] * 3
    flat = pl.pallas_call(
        functools.partial(project_kernel, slices),
        out_shape=outs,
        compiler_params=params(),
        cost_estimate=cost(6 * tokens * depth * width, 8 * 1024 * 1024),
        name="project",
    )(hidden_in, wq, wk, wv, gain)
    return [flat[3 * g : 3 * g + 3] for g in range(len(slices))]


def relay_kernel(slices, blocks, devices, offsets, kv_ref, here_ref, placement, *refs):
    mine = refs[:blocks]
    theirs = refs[blocks : 2 * blocks]
    wk, wv, gain, key_out, value_out, rows_buf = refs[2 * blocks :]
    matrix = head_sum_matrix()
    half = PAGE // 2
    for block in range(blocks):
        near = pl.multiple_of(kv_ref[0] * half, half)
        far = pl.multiple_of((1 - kv_ref[0]) * half, half)
        rows_buf[pl.ds(near, half), :] = mine[block][...]
        rows_buf[pl.ds(far, half), :] = theirs[block][...]
        x = rows_buf[...]
        scale = row_scale_of(x)
        source = lax.rem(here_ref[0] + (devices - offsets[block]), devices)
        slot = lax.rem(placement[source * blocks + block], blocks)
        for start, size in slices:
            cols = slice(start, start + size)
            k = jnp.dot(x, wk[:, cols], preferred_element_type=f32)
            key_out[slot, :, cols] = head_norm(k, gain[:, cols], matrix).astype(bf16)
            v = jnp.dot(x, wv[:, cols], preferred_element_type=f32)
            value_out[slot, :, cols] = (v * scale).astype(bf16)


def relay_project(mine, theirs, wk, wv, gain, kv_index, here, placement, offsets):
    blocks = len(mine)
    depth, width = wk.shape
    out = jax.ShapeDtypeStruct((blocks, PAGE, width), bf16)
    smem = pl.BlockSpec(memory_space=pltpu.SMEM)
    vmem = pl.BlockSpec(memory_space=pltpu.VMEM)
    return pl.pallas_call(
        functools.partial(
            relay_kernel, group_slices(width), blocks, lax.axis_size("blk"), offsets
        ),
        in_specs=[smem] * 3 + [vmem] * (2 * blocks + 3),
        out_specs=[vmem, vmem],
        out_shape=[out, out],
        scratch_shapes=[pltpu.VMEM((PAGE, depth), bf16)],
        compiler_params=params(),
        cost_estimate=cost(4 * blocks * PAGE * depth * width, 8 * 1024 * 1024),
        name="relay_project",
    )(kv_index, here, placement, *mine, *theirs, wk, wv, gain)


def attend_kernel(live_ref, depth_ref, q_ref, k_ref, v_ref, p0, p1, p2, p3, out):
    pages = (p0, p1, p2, p3)
    tokens, width = q_ref.shape
    live, depth = live_ref[0], depth_ref[0]
    lane = lax.broadcasted_iota(jnp.int32, (1, LANES), 1)
    row = lax.broadcasted_iota(jnp.int32, (PAGE, PAGE), 0)
    col = lax.broadcasted_iota(jnp.int32, (PAGE, PAGE), 1)
    causal = col <= row
    key_row = lax.broadcasted_iota(jnp.int32, (PAGE, LANES), 0)
    blocks = tokens // PAGE
    for start in range(0, width, LANES):
        cols = slice(start, start + LANES)
        keys, values = [], []
        for b in range(blocks):
            rows = slice(b * PAGE, (b + 1) * PAGE)
            keep = (key_row + b * PAGE) < live
            keys.append(k_ref[rows, cols])
            shown = jnp.where(keep, v_ref[rows, cols].astype(f32), 0.0).astype(bf16)
            ones = jnp.where(keep, 1.0, 0.0).astype(bf16)
            values.append(jnp.concatenate([shown, ones], axis=1))
        for p in range(PMAX):
            keep = jnp.where(p < depth, 1.0, 0.0).astype(bf16)
            keys.append(pages[p][0, :, cols])
            ones = jnp.full((PAGE, LANES), 1.0, bf16) * keep
            values.append(jnp.concatenate([pages[p][1, :, cols] * keep, ones], axis=1))
        for b in range(blocks):
            rows = slice(b * PAGE, (b + 1) * PAGE)
            q = q_ref[rows, cols]
            ratios = []
            for side in range(2):
                q_side = jnp.where((lane // HD) == side, q, jnp.zeros_like(q))
                acc = jnp.zeros((PAGE, 2 * LANES), f32)
                for j in list(range(b + 1)) + list(range(blocks, blocks + PMAX)):
                    scores = lax.dot_general(
                        q_side, keys[j], (((1,), (1,)), ((), ())), preferred_element_type=f32
                    )
                    weights = jnp.exp(scores)
                    if j == b:
                        weights = jnp.where(causal, weights, 0.0)
                    acc += jnp.dot(weights.astype(bf16), values[j], preferred_element_type=f32)
                ratios.append(acc[:, :LANES] / acc[:, LANES:])
            out[rows, cols] = jnp.where((lane // HD) == 0, ratios[0], ratios[1]).astype(bf16)


def attend(live, depth, q, k, v, pages):
    tokens, width = q.shape
    heads = width // HD
    smem = pl.BlockSpec(memory_space=pltpu.SMEM)
    vmem = pl.BlockSpec(memory_space=pltpu.VMEM)
    keys = tokens + PMAX * PAGE
    return pl.pallas_call(
        attend_kernel,
        in_specs=[smem, smem] + [vmem] * 7,
        out_specs=vmem,
        out_shape=jax.ShapeDtypeStruct((tokens, width), bf16),
        compiler_params=params(),
        cost_estimate=cost(
            16 * heads * tokens * keys * HD, 2 * 1024 * 1024, heads * tokens * keys
        ),
        name="attend",
    )(live, depth, q, k, v, *pages)


def finish_kernel(slices, count, *refs):
    hidden, w_mine, w_theirs, rate = refs[:4]
    mine = refs[4 : 4 + count]
    theirs = refs[4 + count : 4 + 2 * count]
    out = refs[4 + 2 * count]

    def half(parts, weights):
        total = None
        for part, (start, size) in zip(parts, slices):
            term = jnp.dot(part[...], weights[start : start + size, :], preferred_element_type=f32)
            total = term if total is None else total + term
        return total

    branch = half(mine, w_mine) + half(theirs, w_theirs)
    hidden_f = hidden[...].astype(f32)
    anchor = hidden_f * lax.rsqrt(jnp.mean(hidden_f * hidden_f, axis=-1, keepdims=True) + epsilon)
    normed = branch * lax.rsqrt(jnp.mean(branch * branch, axis=-1, keepdims=True) + epsilon)
    updated = anchor + rate[...] * (normed - anchor)
    scale = lax.rsqrt(jnp.mean(updated * updated, axis=-1, keepdims=True) + epsilon)
    out[...] = (updated * scale).astype(bf16)


def finish(hidden_in, w_mine, w_theirs, rate, mine, theirs):
    tokens, depth = hidden_in.shape
    width = w_mine.shape[0]
    slices = group_slices(width)
    step = 256
    by_rows = lambda size: pl.BlockSpec((step, size), lambda i: (i, 0))
    whole = lambda shape: pl.BlockSpec(shape, lambda i: (0, 0))
    return pl.pallas_call(
        functools.partial(finish_kernel, slices, len(slices)),
        grid=(tokens // step,),
        in_specs=[by_rows(depth), whole(w_mine.shape), whole(w_theirs.shape), whole(rate.shape)]
        + [by_rows(size) for _, size in slices] * 2,
        out_specs=by_rows(depth),
        out_shape=jax.ShapeDtypeStruct((tokens, depth), bf16),
        compiler_params=params(),
        cost_estimate=cost(4 * tokens * depth * width, 8 * 1024 * 1024),
        name="finish",
    )(hidden_in, w_mine, w_theirs, rate, *mine, *theirs)


def body(
    hidden_in,
    w_query,
    w_key,
    w_value,
    w_out,
    head_gain,
    eigen_rate,
    pool_keys,
    pool_values,
    req_len,
    prefix_len,
    prefix_pages,
    placement,
):
    devices = lax.axis_size("blk")
    here = lax.axis_index("blk").astype(jnp.int32).reshape(1)
    kv_index = lax.axis_index("kv").astype(jnp.int32).reshape(1)
    blocks = hidden_in.shape[0] // PAGE
    gain = head_gain.reshape(1, -1)
    rate = eigen_rate.reshape(1, -1)
    page_offsets = [slot * devices // PMAX + 1 for slot in range(PMAX)]
    block_offsets = [(2 * b + 1) * devices // (2 * blocks) for b in range(blocks)]

    relay_send = split_rows(hidden_in, kv_index, blocks)
    page_send = pack(
        pool_keys, pool_values, prefix_pages.reshape(-1), here, devices, page_offsets, relay_send[0]
    )

    projected = project(hidden_in, w_query, w_key, w_value, gain)

    sends = [(relay_send[b], block_offsets[b]) for b in range(blocks)]
    for sent in page_send:
        sends += [(sent[slot], devices - page_offsets[slot]) for slot in SLOT_ORDER]
    arrived = []
    for index, (block, distance) in enumerate(sends):
        if index >= WINDOW:
            block = after(block, projected[0][0], *arrived[: index - WINDOW + 1])
        arrived.append(from_behind(block, "blk", distance))
    relay_mine = arrived[:blocks]
    pages = []
    for g in range(len(page_send)):
        first = blocks + g * PMAX
        got = dict(zip(SLOT_ORDER, arrived[first : first + PMAX]))
        pages.append([got[slot] for slot in range(PMAX)])
    w_theirs = from_behind(w_out, "kv", 1)
    relay_theirs = [from_behind(rows, "kv", 1) for rows in relay_mine]

    mine, theirs = [], []
    for g, (q, k, v) in enumerate(projected):
        attended = attend(req_len, prefix_len, q, k, v, pages[g])
        mine.append(attended)
        theirs.append(from_behind(attended, "kv", 1))
    new_keys, new_values = relay_project(
        relay_mine, relay_theirs, w_key, w_value, gain, kv_index, here, placement, block_offsets
    )
    layer_out = finish(hidden_in, w_out, w_theirs, rate, mine, theirs)
    return (layer_out, new_keys, new_values)


def solution(mesh):
    in_specs = (
        P("blk", None),
        P(None, "kv"),
        P(None, "kv"),
        P(None, "kv"),
        P("kv", None),
        P("kv"),
        P(),
        P("blk", None, "kv"),
        P("blk", None, "kv"),
        P("blk"),
        P("blk"),
        P(),
        P(),
    )
    out_specs = (P("blk", None), P("blk", None, "kv"), P("blk", None, "kv"))
    return jax.shard_map(body, mesh=mesh, in_specs=in_specs, out_specs=out_specs, check_vma=False)
```

```python
import functools
import math

import jax
import jax.numpy as jnp
from jax import lax
from jax.experimental import pallas as pl
from jax.experimental.pallas import tpu as pltpu
from jax.sharding import PartitionSpec as P

HD = 64
PAGE = 256
PMAX = 4
LANES = 128
GROUPS = (256, 384)
UNITS = ((256,), (128, 128, 128))
WINDOW = 4
SLOT_ORDER = (2, 1, 3, 0)
VMEM_LIMIT = 16 * 1024 * 1024
FIRST_LIMIT = 58 * 1024 * 1024

epsilon = 1e-06

f32 = jnp.float32
bf16 = jnp.bfloat16


def from_behind(block, axis, distance):
    devices = range(lax.axis_size(axis))
    route = [((i - distance) % len(devices), i) for i in devices]
    return lax.ppermute(block, axis, route)


def over_blk(block, distances):
    devices = lax.axis_size("blk")
    route = []
    for kv in range(lax.axis_size("kv")):
        for i in range(devices):
            route.append((kv * devices + (i - distances[kv]) % devices, kv * devices + i))
    return lax.ppermute(block, ("kv", "blk"), route)


def after(block, *others):
    return lax.optimization_barrier((block, *others))[0]


def group_slices(width):
    slices, start = [], 0
    for size in GROUPS:
        slices.append((start, size))
        start += size
    assert start == width
    return slices


def unit_slices():
    units, base = [], 0
    for g, sizes in enumerate(UNITS):
        inner = 0
        for size in sizes:
            units.append((g, inner, base + inner, size))
            inner += size
        base += inner
    return units


def params(limit=VMEM_LIMIT):
    return pltpu.CompilerParams(vmem_limit_bytes=limit)


def cost():
    return pl.CostEstimate(flops=1, bytes_accessed=1, transcendentals=0)


def split_kernel(kv_ref, hidden, out, sem):
    rows = pl.ds(pl.multiple_of(kv_ref[0] * PAGE, PAGE), PAGE)
    copy = pltpu.make_async_copy(hidden.at[rows], out, sem)
    copy.start()
    copy.wait()


def split_rows(hidden_in, kv_index):
    return pl.pallas_call(
        split_kernel,
        in_specs=[pl.BlockSpec(memory_space=pltpu.SMEM), pl.BlockSpec(memory_space=pltpu.HBM)],
        out_specs=pl.BlockSpec(memory_space=pltpu.VMEM),
        out_shape=jax.ShapeDtypeStruct((PAGE, hidden_in.shape[1]), bf16),
        scratch_shapes=[pltpu.SemaphoreType.DMA],
        compiler_params=params(FIRST_LIMIT),
        cost_estimate=cost(),
        name="split_rows",
    )(kv_index, hidden_in)


def pack_kernel(slices, devices, offsets, here_ref, table, keys, values, _, *rest):
    outs, (buf, sem) = rest[:-2], rest[-2:]
    copies = []
    for slot in range(PMAX):
        asker = lax.rem(here_ref[0] + (devices - offsets[slot]), devices)
        local = lax.rem(table[slot, asker], keys.shape[0])
        for side, pool in enumerate((keys, values)):
            index = 2 * slot + side
            copies.append(pltpu.make_async_copy(pool.at[local], buf.at[index], sem.at[index]))
    for copy in copies:
        copy.start()
    for slot in range(PMAX):
        for side in range(2):
            index = 2 * slot + side
            copies[index].wait()
            for g, (start, size) in enumerate(slices):
                outs[g * PMAX + slot][side] = buf[index, :, start : start + size]


def pack(pool_keys, pool_values, table, here, devices, offsets, first):
    width = pool_keys.shape[2]
    slices = group_slices(width)
    outs = []
    for _, size in slices:
        outs += [jax.ShapeDtypeStruct((2, PAGE, size), bf16)] * PMAX
    smem = pl.BlockSpec(memory_space=pltpu.SMEM)
    hbm = pl.BlockSpec(memory_space=pltpu.HBM)
    result = pl.pallas_call(
        functools.partial(pack_kernel, slices, devices, offsets),
        in_specs=[smem, smem, hbm, hbm, pl.BlockSpec(memory_space=pl.ANY)],
        out_specs=[pl.BlockSpec(memory_space=pltpu.VMEM)] * len(outs),
        out_shape=outs,
        scratch_shapes=[
            pltpu.VMEM((2 * PMAX, PAGE, width), bf16),
            pltpu.SemaphoreType.DMA((2 * PMAX,)),
        ],
        compiler_params=params(FIRST_LIMIT),
        cost_estimate=cost(),
        name="pack",
    )(here, table, pool_keys, pool_values, first)
    return [result[PMAX * g : PMAX * (g + 1)] for g in range(len(slices))]


def head_sum_matrix():
    rows = (lax.broadcasted_iota(jnp.int32, (2 * LANES, LANES), 0) % LANES) // HD
    cols = lax.broadcasted_iota(jnp.int32, (2 * LANES, LANES), 1) // HD
    return jnp.where(rows == cols, 1.0 / HD, 0.0).astype(bf16)


def head_norm(projected, gain, matrix):
    parts = []
    for start in range(0, projected.shape[1], LANES):
        part = projected[:, start : start + LANES]
        squares = part * part
        high = squares.astype(bf16)
        low = (squares - high.astype(f32)).astype(bf16)
        both = jnp.concatenate([high, low], axis=1)
        mean = jnp.dot(both, matrix, preferred_element_type=f32)
        parts.append(part * lax.rsqrt(mean + epsilon) * gain[:, start : start + LANES])
    return jnp.concatenate(parts, axis=1) if len(parts) > 1 else parts[0]


def row_scale_of(hidden):
    hidden_f = hidden.astype(f32)
    return lax.rsqrt(jnp.mean(hidden_f * hidden_f, axis=-1, keepdims=True) + epsilon)


def project_kernel(slices, hidden, wq, wk, wv, gain, *outs):
    matrix = head_sum_matrix()
    rows_all = hidden.shape[0]
    for low in range(0, rows_all, PAGE):
        rows = slice(low, low + PAGE)
        x = hidden[rows, :]
        scale = row_scale_of(x)
        for g, (start, size) in enumerate(slices):
            cols = slice(start, start + size)
            q = jnp.dot(x, wq[:, cols], preferred_element_type=f32)
            q = head_norm(q, gain[:, cols], matrix).astype(bf16)
            outs[3 * g][rows, :] = q * jnp.asarray(1.0 / math.sqrt(HD), bf16)
            k = jnp.dot(x, wk[:, cols], preferred_element_type=f32)
            outs[3 * g + 1][rows, :] = head_norm(k, gain[:, cols], matrix).astype(bf16)
            v = jnp.dot(x, wv[:, cols], preferred_element_type=f32)
            outs[3 * g + 2][rows, :] = (v * scale).astype(bf16)


def project(hidden_in, wq, wk, wv, gain):
    tokens, depth = hidden_in.shape
    width = wq.shape[1]
    slices = [(start, size) for _, _, start, size in unit_slices()]
    outs = []
    for _, size in slices:
        outs += [jax.ShapeDtypeStruct((tokens, size), bf16)] * 3
    flat = pl.pallas_call(
        functools.partial(project_kernel, slices),
        out_shape=outs,
        compiler_params=params(),
        cost_estimate=cost(),
        name="project",
    )(hidden_in, wq, wk, wv, gain)
    return [flat[3 * g : 3 * g + 3] for g in range(len(slices))]


def relay_kernel(slices, blocks, devices, offsets, kv_ref, here_ref, placement, *refs):
    mine, theirs, wk, wv, gain, key_out, value_out = refs
    matrix = head_sum_matrix()
    for rows_ref, block in ((mine, kv_ref[0]), (theirs, 1 - kv_ref[0])):
        x = rows_ref[...]
        scale = row_scale_of(x)
        offset = jnp.where(block == 0, offsets[0], offsets[1])
        source = lax.rem(here_ref[0] + (devices - offset), devices)
        slot = lax.rem(placement[source * blocks + block], blocks)
        for start, size in slices:
            cols = slice(start, start + size)
            k = jnp.dot(x, wk[:, cols], preferred_element_type=f32)
            key_out[slot, :, cols] = head_norm(k, gain[:, cols], matrix).astype(bf16)
            v = jnp.dot(x, wv[:, cols], preferred_element_type=f32)
            value_out[slot, :, cols] = (v * scale).astype(bf16)


def relay_project(mine, theirs, wk, wv, gain, kv_index, here, placement, offsets):
    blocks = len(offsets)
    depth, width = wk.shape
    out = jax.ShapeDtypeStruct((blocks, PAGE, width), bf16)
    smem = pl.BlockSpec(memory_space=pltpu.SMEM)
    vmem = pl.BlockSpec(memory_space=pltpu.VMEM)
    return pl.pallas_call(
        functools.partial(
            relay_kernel, group_slices(width), blocks, lax.axis_size("blk"), offsets
        ),
        in_specs=[smem] * 3 + [vmem] * 5,
        out_specs=[vmem, vmem],
        out_shape=[out, out],
        compiler_params=params(),
        cost_estimate=cost(),
        name="relay_project",
    )(kv_index, here, placement, mine, theirs, wk, wv, gain)


def attend_kernel(inner, live_ref, depth_ref, q_ref, k_ref, v_ref, p0, p1, p2, p3, out):
    pages = (p0, p1, p2, p3)
    tokens, width = q_ref.shape
    live, depth = live_ref[0], depth_ref[0]
    lane = lax.broadcasted_iota(jnp.int32, (1, LANES), 1)
    row = lax.broadcasted_iota(jnp.int32, (PAGE, PAGE), 0)
    col = lax.broadcasted_iota(jnp.int32, (PAGE, PAGE), 1)
    causal = col <= row
    key_row = lax.broadcasted_iota(jnp.int32, (PAGE, LANES), 0)
    blocks = tokens // PAGE
    for start in range(0, width, LANES):
        cols = slice(start, start + LANES)
        page_cols = slice(inner + start, inner + start + LANES)
        keys, values = [], []
        for b in range(blocks):
            rows = slice(b * PAGE, (b + 1) * PAGE)
            keep = (key_row + b * PAGE) < live
            keys.append(k_ref[rows, cols])
            shown = jnp.where(keep, v_ref[rows, cols].astype(f32), 0.0).astype(bf16)
            ones = jnp.where(keep, 1.0, 0.0).astype(bf16)
            values.append(jnp.concatenate([shown, ones], axis=1))
        for p in range(PMAX):
            keep = jnp.where(p < depth, 1.0, 0.0).astype(bf16)
            keys.append(pages[p][0, :, page_cols])
            ones = jnp.full((PAGE, LANES), 1.0, bf16) * keep
            values.append(jnp.concatenate([pages[p][1, :, page_cols] * keep, ones], axis=1))
        for b in range(blocks):
            rows = slice(b * PAGE, (b + 1) * PAGE)
            q = q_ref[rows, cols]
            ratios = []
            for side in range(2):
                q_side = jnp.where((lane // HD) == side, q, jnp.zeros_like(q))
                acc = jnp.zeros((PAGE, 2 * LANES), f32)
                for j in list(range(b + 1)) + list(range(blocks, blocks + PMAX)):
                    scores = lax.dot_general(
                        q_side, keys[j], (((1,), (1,)), ((), ())), preferred_element_type=f32
                    )
                    weights = jnp.exp(scores)
                    if j == b:
                        weights = jnp.where(causal, weights, 0.0)
                    acc += jnp.dot(weights.astype(bf16), values[j], preferred_element_type=f32)
                ratios.append(acc[:, :LANES] / acc[:, LANES:])
            out[rows, cols] = jnp.where((lane // HD) == 0, ratios[0], ratios[1]).astype(bf16)


def attend(live, depth, q, k, v, pages, inner):
    tokens, width = q.shape
    heads = width // HD
    smem = pl.BlockSpec(memory_space=pltpu.SMEM)
    vmem = pl.BlockSpec(memory_space=pltpu.VMEM)
    keys = tokens + PMAX * PAGE
    return pl.pallas_call(
        functools.partial(attend_kernel, inner),
        in_specs=[smem, smem] + [vmem] * 7,
        out_specs=vmem,
        out_shape=jax.ShapeDtypeStruct((tokens, width), bf16),
        compiler_params=params(),
        cost_estimate=cost(),
        name="attend",
    )(live, depth, q, k, v, *pages)


def finish_kernel(slices, count, *refs):
    hidden, w_mine, w_theirs, rate = refs[:4]
    mine = refs[4 : 4 + count]
    theirs = refs[4 + count : 4 + 2 * count]
    out = refs[4 + 2 * count]

    def half(parts, weights):
        total = None
        for part, (start, size) in zip(parts, slices):
            term = jnp.dot(part[...], weights[start : start + size, :], preferred_element_type=f32)
            total = term if total is None else total + term
        return total

    branch = half(mine, w_mine) + half(theirs, w_theirs)
    hidden_f = hidden[...].astype(f32)
    anchor = hidden_f * lax.rsqrt(jnp.mean(hidden_f * hidden_f, axis=-1, keepdims=True) + epsilon)
    normed = branch * lax.rsqrt(jnp.mean(branch * branch, axis=-1, keepdims=True) + epsilon)
    updated = anchor + rate[...] * (normed - anchor)
    scale = lax.rsqrt(jnp.mean(updated * updated, axis=-1, keepdims=True) + epsilon)
    out[...] = (updated * scale).astype(bf16)


def finish(hidden_in, w_mine, w_theirs, rate, mine, theirs):
    tokens, depth = hidden_in.shape
    width = w_mine.shape[0]
    slices = [(start, size) for _, _, start, size in unit_slices()]
    step = 256
    by_rows = lambda size: pl.BlockSpec((step, size), lambda i: (i, 0))
    whole = lambda shape: pl.BlockSpec(shape, lambda i: (0, 0))
    return pl.pallas_call(
        functools.partial(finish_kernel, slices, len(slices)),
        grid=(tokens // step,),
        in_specs=[by_rows(depth), whole(w_mine.shape), whole(w_theirs.shape), whole(rate.shape)]
        + [by_rows(size) for _, size in slices] * 2,
        out_specs=by_rows(depth),
        out_shape=jax.ShapeDtypeStruct((tokens, depth), bf16),
        compiler_params=params(),
        cost_estimate=cost(),
        name="finish",
    )(hidden_in, w_mine, w_theirs, rate, *mine, *theirs)


def body(
    hidden_in,
    w_query,
    w_key,
    w_value,
    w_out,
    head_gain,
    eigen_rate,
    pool_keys,
    pool_values,
    req_len,
    prefix_len,
    prefix_pages,
    placement,
):
    devices = lax.axis_size("blk")
    here = lax.axis_index("blk").astype(jnp.int32).reshape(1)
    kv_index = lax.axis_index("kv").astype(jnp.int32).reshape(1)
    blocks = hidden_in.shape[0] // PAGE
    gain = head_gain.reshape(1, -1)
    rate = eigen_rate.reshape(1, -1)
    page_offsets = [slot * devices // PMAX + 1 for slot in range(PMAX)]
    block_offsets = [(2 * b + 1) * devices // (2 * blocks) for b in range(blocks)]

    assert blocks == lax.axis_size("kv") == 2
    relay_send = split_rows(hidden_in, kv_index)
    page_send = pack(
        pool_keys, pool_values, prefix_pages.T, here, devices, page_offsets, relay_send
    )

    projected = project(hidden_in, w_query, w_key, w_value, gain)

    sends = [(relay_send, block_offsets)]
    for sent in page_send:
        sends += [(sent[slot], [devices - page_offsets[slot]] * 2) for slot in SLOT_ORDER]
    arrived = []
    for index, (block, distance) in enumerate(sends):
        if index >= WINDOW:
            block = after(block, projected[0][0], *arrived[: index - WINDOW + 1])
        arrived.append(over_blk(block, distance))
    relay_mine = arrived[0]
    pages = []
    for g in range(len(page_send)):
        first = 1 + g * PMAX
        got = dict(zip(SLOT_ORDER, arrived[first : first + PMAX]))
        pages.append([got[slot] for slot in range(PMAX)])
    w_theirs = from_behind(after(w_out, page_send[0][2]), "kv", 1)
    first_pages = arrived[1 : 1 + PMAX]
    relay_theirs = from_behind(after(relay_mine, w_theirs, *first_pages), "kv", 1)
    new_keys, new_values = relay_project(
        relay_mine, relay_theirs, w_key, w_value, gain, kv_index, here, placement, block_offsets
    )

    mine, theirs = [], []
    for (g, inner, _, _), (q, k, v) in zip(unit_slices(), projected):
        q = after(q, new_keys, theirs[0]) if g else q
        attended = attend(req_len, prefix_len, q, k, v, pages[g], inner)
        mine.append(attended)
        theirs.append(from_behind(attended, "kv", 1))
    layer_out = finish(hidden_in, w_out, w_theirs, rate, mine, theirs)
    return (layer_out, new_keys, new_values)


def solution(mesh):
    in_specs = (
        P("blk", None),
        P(None, "kv"),
        P(None, "kv"),
        P(None, "kv"),
        P("kv", None),
        P("kv"),
        P(),
        P("blk", None, "kv"),
        P("blk", None, "kv"),
        P("blk"),
        P("blk"),
        P(),
        P(),
    )
    out_specs = (P("blk", None), P("blk", None, "kv"), P("blk", None, "kv"))
    return jax.shard_map(body, mesh=mesh, in_specs=in_specs, out_specs=out_specs, check_vma=False)
```

```python
import functools
import math

import jax
import jax.numpy as jnp
from jax import lax
from jax.experimental import pallas as pl
from jax.experimental.pallas import tpu as pltpu
from jax.sharding import PartitionSpec as P

HD = 64
PAGE = 256
PMAX = 4
LANES = 128
GROUPS = (256, 384)
UNITS = ((256,), (128, 128, 128))
WINDOW = 4
PARTS = 2
SLOT_ORDER = (2, 1, 3, 0)
VMEM_LIMIT = 16 * 1024 * 1024
FIRST_LIMIT = 58 * 1024 * 1024

epsilon = 1e-06

f32 = jnp.float32
bf16 = jnp.bfloat16


def from_behind(block, axis, distance):
    devices = range(lax.axis_size(axis))
    route = [((i - distance) % len(devices), i) for i in devices]
    return lax.ppermute(block, axis, route)


def over_blk(block, distances):
    devices = lax.axis_size("blk")
    route = []
    for kv in range(lax.axis_size("kv")):
        for i in range(devices):
            route.append((kv * devices + (i - distances[kv]) % devices, kv * devices + i))
    return lax.ppermute(block, ("kv", "blk"), route)


def after(block, *others):
    return lax.optimization_barrier((block, *others))[0]


def group_slices(width):
    slices, start = [], 0
    for size in GROUPS:
        slices.append((start, size))
        start += size
    assert start == width
    return slices


def unit_slices():
    units, base = [], 0
    for g, sizes in enumerate(UNITS):
        inner = 0
        for size in sizes:
            units.append((g, inner, base + inner, size))
            inner += size
        base += inner
    return units


def params(limit=VMEM_LIMIT):
    return pltpu.CompilerParams(vmem_limit_bytes=limit)


def cost():
    return pl.CostEstimate(flops=1, bytes_accessed=1, transcendentals=0)


def pack_kernel(slices, devices, offsets, kv_ref, here_ref, table, hidden, keys, values, *rest):
    outs, (buf, row_sem, sem) = rest[:-3], rest[-3:]
    part = PAGE // PARTS
    row_copies = []
    for i in range(PARTS):
        rows = pl.ds(pl.multiple_of(kv_ref[0] * PAGE + i * part, part), part)
        target = outs[0].at[pl.ds(i * part, part)]
        row_copies.append(pltpu.make_async_copy(hidden.at[rows], target, row_sem.at[i]))
    for copy in row_copies:
        copy.start()
    copies = []
    for slot in range(PMAX):
        asker = lax.rem(here_ref[0] + (devices - offsets[slot]), devices)
        local = lax.rem(table[slot, asker], keys.shape[0])
        for side, pool in enumerate((keys, values)):
            for i in range(PARTS):
                rows = pl.ds(i * part, part)
                index = (2 * slot + side) * PARTS + i
                target = buf.at[2 * slot + side, rows]
                copies.append(pltpu.make_async_copy(pool.at[local, rows], target, sem.at[index]))
    for copy in copies:
        copy.start()
    for slot in range(PMAX):
        for side in range(2):
            for i in range(PARTS):
                copies[(2 * slot + side) * PARTS + i].wait()
                rows = slice(i * part, (i + 1) * part)
                for g, (start, size) in enumerate(slices):
                    outs[1 + g * PMAX + slot][side, rows] = buf[
                        2 * slot + side, rows, start : start + size
                    ]
    for copy in row_copies:
        copy.wait()


def pack(hidden_in, pool_keys, pool_values, table, kv_index, here, devices, offsets):
    width = pool_keys.shape[2]
    slices = group_slices(width)
    outs = [jax.ShapeDtypeStruct((PAGE, hidden_in.shape[1]), bf16)]
    for _, size in slices:
        outs += [jax.ShapeDtypeStruct((2, PAGE, size), bf16)] * PMAX
    smem = pl.BlockSpec(memory_space=pltpu.SMEM)
    hbm = pl.BlockSpec(memory_space=pltpu.HBM)
    result = pl.pallas_call(
        functools.partial(pack_kernel, slices, devices, offsets),
        in_specs=[smem] * 3 + [hbm] * 3,
        out_specs=[pl.BlockSpec(memory_space=pltpu.VMEM)] * len(outs),
        out_shape=outs,
        scratch_shapes=[
            pltpu.VMEM((2 * PMAX, PAGE, width), bf16),
            pltpu.SemaphoreType.DMA((PARTS,)),
            pltpu.SemaphoreType.DMA((2 * PMAX * PARTS,)),
        ],
        compiler_params=params(FIRST_LIMIT),
        cost_estimate=cost(),
        name="pack",
    )(kv_index, here, table, hidden_in, pool_keys, pool_values)
    return result[0], [result[1 + PMAX * g : 1 + PMAX * (g + 1)] for g in range(len(slices))]


def join_kernel(w_out, rows, out, sem):
    depth, count = w_out.shape[0], rows.shape[0]
    copies = []
    for i in range(PARTS):
        part = pl.ds(i * (depth // PARTS), depth // PARTS)
        copies.append(pltpu.make_async_copy(w_out.at[part], out.at[part], sem.at[i]))
    for i in range(PARTS):
        part = pl.ds(i * (count // PARTS), count // PARTS)
        target = out.at[pl.ds(depth + i * (count // PARTS), count // PARTS)]
        copies.append(pltpu.make_async_copy(rows.at[part], target, sem.at[PARTS + i]))
    for copy in copies:
        copy.start()
    for copy in copies:
        copy.wait()


def join(w_out, rows):
    out = jax.ShapeDtypeStruct((w_out.shape[0] + rows.shape[0], w_out.shape[1]), bf16)
    return pl.pallas_call(
        join_kernel,
        in_specs=[pl.BlockSpec(memory_space=pl.ANY)] * 2,
        out_specs=pl.BlockSpec(memory_space=pltpu.VMEM),
        out_shape=out,
        scratch_shapes=[pltpu.SemaphoreType.DMA((2 * PARTS,))],
        compiler_params=params(),
        cost_estimate=cost(),
        name="join",
    )(w_out, rows)


def head_sum_matrix():
    rows = (lax.broadcasted_iota(jnp.int32, (2 * LANES, LANES), 0) % LANES) // HD
    cols = lax.broadcasted_iota(jnp.int32, (2 * LANES, LANES), 1) // HD
    return jnp.where(rows == cols, 1.0 / HD, 0.0).astype(bf16)


def head_norm(projected, gain, matrix):
    parts = []
    for start in range(0, projected.shape[1], LANES):
        part = projected[:, start : start + LANES]
        squares = part * part
        high = squares.astype(bf16)
        low = (squares - high.astype(f32)).astype(bf16)
        both = jnp.concatenate([high, low], axis=1)
        mean = jnp.dot(both, matrix, preferred_element_type=f32)
        parts.append(part * lax.rsqrt(mean + epsilon) * gain[:, start : start + LANES])
    return jnp.concatenate(parts, axis=1) if len(parts) > 1 else parts[0]


def row_scale_of(hidden):
    hidden_f = hidden.astype(f32)
    return lax.rsqrt(jnp.mean(hidden_f * hidden_f, axis=-1, keepdims=True) + epsilon)


def project_kernel(slices, hidden, wq, wk, wv, gain, *outs):
    matrix = head_sum_matrix()
    rows_all = hidden.shape[0]
    for low in range(0, rows_all, PAGE):
        rows = slice(low, low + PAGE)
        x = hidden[rows, :]
        scale = row_scale_of(x)
        for g, (start, size) in enumerate(slices):
            cols = slice(start, start + size)
            q = jnp.dot(x, wq[:, cols], preferred_element_type=f32)
            q = head_norm(q, gain[:, cols], matrix).astype(bf16)
            outs[3 * g][rows, :] = q * jnp.asarray(1.0 / math.sqrt(HD), bf16)
            k = jnp.dot(x, wk[:, cols], preferred_element_type=f32)
            outs[3 * g + 1][rows, :] = head_norm(k, gain[:, cols], matrix).astype(bf16)
            v = jnp.dot(x, wv[:, cols], preferred_element_type=f32)
            outs[3 * g + 2][rows, :] = (v * scale).astype(bf16)


def project(hidden_in, wq, wk, wv, gain):
    tokens, depth = hidden_in.shape
    width = wq.shape[1]
    slices = [(start, size) for _, _, start, size in unit_slices()]
    outs = []
    for _, size in slices:
        outs += [jax.ShapeDtypeStruct((tokens, size), bf16)] * 3
    flat = pl.pallas_call(
        functools.partial(project_kernel, slices),
        out_shape=outs,
        compiler_params=params(),
        cost_estimate=cost(),
        name="project",
    )(hidden_in, wq, wk, wv, gain)
    return [flat[3 * g : 3 * g + 3] for g in range(len(slices))]


def relay_kernel(slices, blocks, devices, offsets, kv_ref, here_ref, placement, *refs):
    mine, theirs, wk, wv, gain, key_out, value_out = refs
    matrix = head_sum_matrix()
    first = theirs.shape[0] - PAGE
    for rows, block in ((mine[...], kv_ref[0]), (theirs[first:, :], 1 - kv_ref[0])):
        x = rows
        scale = row_scale_of(x)
        offset = jnp.where(block == 0, offsets[0], offsets[1])
        source = lax.rem(here_ref[0] + (devices - offset), devices)
        slot = lax.rem(placement[source * blocks + block], blocks)
        for start, size in slices:
            cols = slice(start, start + size)
            k = jnp.dot(x, wk[:, cols], preferred_element_type=f32)
            key_out[slot, :, cols] = head_norm(k, gain[:, cols], matrix).astype(bf16)
            v = jnp.dot(x, wv[:, cols], preferred_element_type=f32)
            value_out[slot, :, cols] = (v * scale).astype(bf16)


def relay_project(mine, theirs, wk, wv, gain, kv_index, here, placement, offsets):
    blocks = len(offsets)
    depth, width = wk.shape
    out = jax.ShapeDtypeStruct((blocks, PAGE, width), bf16)
    smem = pl.BlockSpec(memory_space=pltpu.SMEM)
    vmem = pl.BlockSpec(memory_space=pltpu.VMEM)
    return pl.pallas_call(
        functools.partial(
            relay_kernel, group_slices(width), blocks, lax.axis_size("blk"), offsets
        ),
        in_specs=[smem] * 3 + [vmem] * 5,
        out_specs=[vmem, vmem],
        out_shape=[out, out],
        compiler_params=params(),
        cost_estimate=cost(),
        name="relay_project",
    )(kv_index, here, placement, mine, theirs, wk, wv, gain)


def attend_kernel(inner, live_ref, depth_ref, q_ref, k_ref, v_ref, p0, p1, p2, p3, out):
    pages = (p0, p1, p2, p3)
    tokens, width = q_ref.shape
    live, depth = live_ref[0], depth_ref[0]
    lane = lax.broadcasted_iota(jnp.int32, (1, LANES), 1)
    row = lax.broadcasted_iota(jnp.int32, (PAGE, PAGE), 0)
    col = lax.broadcasted_iota(jnp.int32, (PAGE, PAGE), 1)
    causal = col <= row
    key_row = lax.broadcasted_iota(jnp.int32, (PAGE, LANES), 0)
    blocks = tokens // PAGE
    for start in range(0, width, LANES):
        cols = slice(start, start + LANES)
        page_cols = slice(inner + start, inner + start + LANES)
        keys, values = [], []
        for b in range(blocks):
            rows = slice(b * PAGE, (b + 1) * PAGE)
            keep = (key_row + b * PAGE) < live
            keys.append(k_ref[rows, cols])
            shown = jnp.where(keep, v_ref[rows, cols].astype(f32), 0.0).astype(bf16)
            ones = jnp.where(keep, 1.0, 0.0).astype(bf16)
            values.append(jnp.concatenate([shown, ones], axis=1))
        for p in range(PMAX):
            keep = jnp.where(p < depth, 1.0, 0.0).astype(bf16)
            keys.append(pages[p][0, :, page_cols])
            ones = jnp.full((PAGE, LANES), 1.0, bf16) * keep
            values.append(jnp.concatenate([pages[p][1, :, page_cols] * keep, ones], axis=1))
        for b in range(blocks):
            rows = slice(b * PAGE, (b + 1) * PAGE)
            q = q_ref[rows, cols]
            ratios = []
            for side in range(2):
                q_side = jnp.where((lane // HD) == side, q, jnp.zeros_like(q))
                acc = jnp.zeros((PAGE, 2 * LANES), f32)
                for j in list(range(b + 1)) + list(range(blocks, blocks + PMAX)):
                    scores = lax.dot_general(
                        q_side, keys[j], (((1,), (1,)), ((), ())), preferred_element_type=f32
                    )
                    weights = jnp.exp(scores)
                    if j == b:
                        weights = jnp.where(causal, weights, 0.0)
                    acc += jnp.dot(weights.astype(bf16), values[j], preferred_element_type=f32)
                ratios.append(acc[:, :LANES] / acc[:, LANES:])
            out[rows, cols] = jnp.where((lane // HD) == 0, ratios[0], ratios[1]).astype(bf16)


def attend(live, depth, q, k, v, pages, inner):
    tokens, width = q.shape
    heads = width // HD
    smem = pl.BlockSpec(memory_space=pltpu.SMEM)
    vmem = pl.BlockSpec(memory_space=pltpu.VMEM)
    keys = tokens + PMAX * PAGE
    return pl.pallas_call(
        functools.partial(attend_kernel, inner),
        in_specs=[smem, smem] + [vmem] * 7,
        out_specs=vmem,
        out_shape=jax.ShapeDtypeStruct((tokens, width), bf16),
        compiler_params=params(),
        cost_estimate=cost(),
        name="attend",
    )(live, depth, q, k, v, *pages)


def finish_kernel(slices, count, *refs):
    hidden, w_mine, w_theirs, rate = refs[:4]
    mine = refs[4 : 4 + count]
    theirs = refs[4 + count : 4 + 2 * count]
    out = refs[4 + 2 * count]

    def half(parts, weights):
        total = None
        for part, (start, size) in zip(parts, slices):
            term = jnp.dot(part[...], weights[start : start + size, :], preferred_element_type=f32)
            total = term if total is None else total + term
        return total

    branch = half(mine, w_mine) + half(theirs, w_theirs)
    hidden_f = hidden[...].astype(f32)
    anchor = hidden_f * lax.rsqrt(jnp.mean(hidden_f * hidden_f, axis=-1, keepdims=True) + epsilon)
    normed = branch * lax.rsqrt(jnp.mean(branch * branch, axis=-1, keepdims=True) + epsilon)
    updated = anchor + rate[...] * (normed - anchor)
    scale = lax.rsqrt(jnp.mean(updated * updated, axis=-1, keepdims=True) + epsilon)
    out[...] = (updated * scale).astype(bf16)


def finish(hidden_in, w_mine, w_theirs, rate, mine, theirs):
    tokens, depth = hidden_in.shape
    width = w_mine.shape[0]
    slices = [(start, size) for _, _, start, size in unit_slices()]
    step = 256
    by_rows = lambda size: pl.BlockSpec((step, size), lambda i: (i, 0))
    whole = lambda shape: pl.BlockSpec(shape, lambda i: (0, 0))
    return pl.pallas_call(
        functools.partial(finish_kernel, slices, len(slices)),
        grid=(tokens // step,),
        in_specs=[by_rows(depth), whole(w_mine.shape), whole(w_mine.shape), whole(rate.shape)]
        + [by_rows(size) for _, size in slices] * 2,
        out_specs=by_rows(depth),
        out_shape=jax.ShapeDtypeStruct((tokens, depth), bf16),
        compiler_params=params(),
        cost_estimate=cost(),
        name="finish",
    )(hidden_in, w_mine, w_theirs, rate, *mine, *theirs)


def body(
    hidden_in,
    w_query,
    w_key,
    w_value,
    w_out,
    head_gain,
    eigen_rate,
    pool_keys,
    pool_values,
    req_len,
    prefix_len,
    prefix_pages,
    placement,
):
    devices = lax.axis_size("blk")
    here = lax.axis_index("blk").astype(jnp.int32).reshape(1)
    kv_index = lax.axis_index("kv").astype(jnp.int32).reshape(1)
    blocks = hidden_in.shape[0] // PAGE
    gain = head_gain.reshape(1, -1)
    rate = eigen_rate.reshape(1, -1)
    page_offsets = [slot * devices // PMAX + 1 for slot in range(PMAX)]
    block_offsets = [(2 * b + 1) * devices // (2 * blocks) for b in range(blocks)]

    assert blocks == lax.axis_size("kv") == 2
    relay_send, page_send = pack(
        hidden_in, pool_keys, pool_values, prefix_pages.T, kv_index, here, devices, page_offsets
    )
    projected = project(hidden_in, w_query, w_key, w_value, gain)

    sends = [(relay_send, block_offsets)]
    for sent in page_send:
        sends += [(sent[slot], [devices - page_offsets[slot]] * 2) for slot in SLOT_ORDER]
    arrived = []
    for index, (block, distance) in enumerate(sends):
        if index >= WINDOW:
            block = after(block, projected[0][0], *arrived[: index - WINDOW + 1])
        arrived.append(over_blk(block, distance))
    relay_mine = arrived[0]
    pages = []
    for g in range(len(page_send)):
        first = 1 + g * PMAX
        got = dict(zip(SLOT_ORDER, arrived[first : first + PMAX]))
        pages.append([got[slot] for slot in range(PMAX)])
    swapped = from_behind(join(w_out, relay_mine), "kv", 1)
    new_keys, new_values = relay_project(
        relay_mine, swapped, w_key, w_value, gain, kv_index, here, placement, block_offsets
    )

    mine, theirs = [], []
    for (g, inner, _, _), (q, k, v) in zip(unit_slices(), projected):
        q = after(q, new_keys) if g else q
        attended = attend(req_len, prefix_len, q, k, v, pages[g], inner)
        mine.append(attended)
        theirs.append(from_behind(attended, "kv", 1))
    layer_out = finish(hidden_in, w_out, swapped, rate, mine, theirs)
    return (layer_out, new_keys, new_values)


def solution(mesh):
    in_specs = (
        P("blk", None),
        P(None, "kv"),
        P(None, "kv"),
        P(None, "kv"),
        P("kv", None),
        P("kv"),
        P(),
        P("blk", None, "kv"),
        P("blk", None, "kv"),
        P("blk"),
        P("blk"),
        P(),
        P(),
    )
    out_specs = (P("blk", None), P("blk", None, "kv"), P("blk", None, "kv"))
    return jax.shard_map(body, mesh=mesh, in_specs=in_specs, out_specs=out_specs, check_vma=False)
```

```python
import functools
import math

import jax
import jax.numpy as jnp
from jax import lax
from jax.experimental import pallas as pl
from jax.experimental.pallas import tpu as pltpu
from jax.sharding import PartitionSpec as P

HD = 64
PAGE = 256
PMAX = 4
LANES = 128
GROUPS = (256, 384)
UNITS = ((256,), (128, 128, 128))
PARTS = 4
SLOT_ORDER = (2, 1, 3)
VMEM_LIMIT = 16 * 1024 * 1024
FIRST_LIMIT = 58 * 1024 * 1024

epsilon = 1e-06

f32 = jnp.float32
bf16 = jnp.bfloat16


def from_behind(block, axis, distance):
    devices = range(lax.axis_size(axis))
    route = [((i - distance) % len(devices), i) for i in devices]
    return lax.ppermute(block, axis, route)


def over_blk(block, distances):
    devices = lax.axis_size("blk")
    route = []
    for kv in range(lax.axis_size("kv")):
        for i in range(devices):
            route.append((kv * devices + (i - distances[kv]) % devices, kv * devices + i))
    return lax.ppermute(block, ("kv", "blk"), route)


def after(block, *others):
    return lax.optimization_barrier((block, *others))[0]


def group_slices(width):
    slices, start = [], 0
    for size in GROUPS:
        slices.append((start, size))
        start += size
    assert start == width
    return slices


def unit_slices():
    units, base = [], 0
    for g, sizes in enumerate(UNITS):
        inner = 0
        for size in sizes:
            units.append((g, inner, base + inner, size))
            inner += size
        base += inner
    return units


def params(limit=VMEM_LIMIT):
    return pltpu.CompilerParams(vmem_limit_bytes=limit)


def cost():
    return pl.CostEstimate(flops=1, bytes_accessed=1, transcendentals=0)


def split_kernel(kv_ref, hidden, out, sem):
    part = PAGE // PARTS
    copies = []
    for i in range(PARTS):
        rows = pl.ds(pl.multiple_of(kv_ref[0] * PAGE + i * part, part), part)
        target = out.at[pl.ds(i * part, part)]
        copies.append(pltpu.make_async_copy(hidden.at[rows], target, sem.at[i]))
    for copy in copies:
        copy.start()
    for copy in copies:
        copy.wait()


def split_rows(hidden_in, kv_index):
    return pl.pallas_call(
        split_kernel,
        in_specs=[pl.BlockSpec(memory_space=pltpu.SMEM), pl.BlockSpec(memory_space=pltpu.HBM)],
        out_specs=pl.BlockSpec(memory_space=pltpu.VMEM),
        out_shape=jax.ShapeDtypeStruct((PAGE, hidden_in.shape[1]), bf16),
        scratch_shapes=[pltpu.SemaphoreType.DMA((PARTS,))],
        compiler_params=params(FIRST_LIMIT),
        cost_estimate=cost(),
        name="split_rows",
    )(kv_index, hidden_in)


def pack_kernel(slices, devices, offsets, here_ref, table, keys, values, _, *rest):
    outs, (buf, sem) = rest[:-2], rest[-2:]
    copies = []
    for slot in range(PMAX):
        asker = lax.rem(here_ref[0] + (devices - offsets[slot]), devices)
        local = lax.rem(table[slot, asker], keys.shape[0])
        for side, pool in enumerate((keys, values)):
            index = 2 * slot + side
            copies.append(pltpu.make_async_copy(pool.at[local], buf.at[index], sem.at[index]))
    for copy in copies:
        copy.start()
    for slot in range(PMAX):
        for side in range(2):
            index = 2 * slot + side
            copies[index].wait()
            if slot == 0:
                outs[0][side] = buf[index]
                continue
            for g, (start, size) in enumerate(slices):
                outs[g * (PMAX - 1) + slot][side] = buf[index, :, start : start + size]


def pack(pool_keys, pool_values, table, here, devices, offsets, first):
    width = pool_keys.shape[2]
    slices = group_slices(width)
    outs = [jax.ShapeDtypeStruct((2, PAGE, width), bf16)]
    for _, size in slices:
        outs += [jax.ShapeDtypeStruct((2, PAGE, size), bf16)] * (PMAX - 1)
    smem = pl.BlockSpec(memory_space=pltpu.SMEM)
    hbm = pl.BlockSpec(memory_space=pltpu.HBM)
    result = pl.pallas_call(
        functools.partial(pack_kernel, slices, devices, offsets),
        in_specs=[smem, smem, hbm, hbm, pl.BlockSpec(memory_space=pl.ANY)],
        out_specs=[pl.BlockSpec(memory_space=pltpu.VMEM)] * len(outs),
        out_shape=outs,
        scratch_shapes=[
            pltpu.VMEM((2 * PMAX, PAGE, width), bf16),
            pltpu.SemaphoreType.DMA((2 * PMAX,)),
        ],
        compiler_params=params(FIRST_LIMIT),
        cost_estimate=cost(),
        name="pack",
    )(here, table, pool_keys, pool_values, first)
    each = PMAX - 1
    return result[0], [result[1 + each * g : 1 + each * (g + 1)] for g in range(len(slices))]


def head_sum_matrix():
    rows = (lax.broadcasted_iota(jnp.int32, (2 * LANES, LANES), 0) % LANES) // HD
    cols = lax.broadcasted_iota(jnp.int32, (2 * LANES, LANES), 1) // HD
    return jnp.where(rows == cols, 1.0 / HD, 0.0).astype(bf16)


def head_norm(projected, gain, matrix):
    parts = []
    for start in range(0, projected.shape[1], LANES):
        part = projected[:, start : start + LANES]
        squares = part * part
        high = squares.astype(bf16)
        low = (squares - high.astype(f32)).astype(bf16)
        both = jnp.concatenate([high, low], axis=1)
        mean = jnp.dot(both, matrix, preferred_element_type=f32)
        parts.append(part * lax.rsqrt(mean + epsilon) * gain[:, start : start + LANES])
    return jnp.concatenate(parts, axis=1) if len(parts) > 1 else parts[0]


def row_scale_of(hidden):
    hidden_f = hidden.astype(f32)
    return lax.rsqrt(jnp.mean(hidden_f * hidden_f, axis=-1, keepdims=True) + epsilon)


def project_kernel(slices, hidden, wq, wk, wv, gain, *outs):
    matrix = head_sum_matrix()
    rows_all = hidden.shape[0]
    for low in range(0, rows_all, PAGE):
        rows = slice(low, low + PAGE)
        x = hidden[rows, :]
        scale = row_scale_of(x)
        for g, (start, size) in enumerate(slices):
            cols = slice(start, start + size)
            q = jnp.dot(x, wq[:, cols], preferred_element_type=f32)
            q = head_norm(q, gain[:, cols], matrix).astype(bf16)
            outs[3 * g][rows, :] = q * jnp.asarray(1.0 / math.sqrt(HD), bf16)
            k = jnp.dot(x, wk[:, cols], preferred_element_type=f32)
            outs[3 * g + 1][rows, :] = head_norm(k, gain[:, cols], matrix).astype(bf16)
            v = jnp.dot(x, wv[:, cols], preferred_element_type=f32)
            outs[3 * g + 2][rows, :] = (v * scale).astype(bf16)


def project(hidden_in, wq, wk, wv, gain):
    tokens, depth = hidden_in.shape
    width = wq.shape[1]
    slices = [(start, size) for _, _, start, size in unit_slices()]
    outs = []
    for _, size in slices:
        outs += [jax.ShapeDtypeStruct((tokens, size), bf16)] * 3
    flat = pl.pallas_call(
        functools.partial(project_kernel, slices),
        out_shape=outs,
        compiler_params=params(),
        cost_estimate=cost(),
        name="project",
    )(hidden_in, wq, wk, wv, gain)
    return [flat[3 * g : 3 * g + 3] for g in range(len(slices))]


def relay_kernel(slices, blocks, devices, offsets, kv_ref, here_ref, placement, *refs):
    mine, theirs, wk, wv, gain, key_out, value_out = refs
    matrix = head_sum_matrix()
    for rows_ref, block in ((mine, kv_ref[0]), (theirs, 1 - kv_ref[0])):
        x = rows_ref[...]
        scale = row_scale_of(x)
        offset = jnp.where(block == 0, offsets[0], offsets[1])
        source = lax.rem(here_ref[0] + (devices - offset), devices)
        slot = lax.rem(placement[source * blocks + block], blocks)
        for start, size in slices:
            cols = slice(start, start + size)
            k = jnp.dot(x, wk[:, cols], preferred_element_type=f32)
            key_out[slot, :, cols] = head_norm(k, gain[:, cols], matrix).astype(bf16)
            v = jnp.dot(x, wv[:, cols], preferred_element_type=f32)
            value_out[slot, :, cols] = (v * scale).astype(bf16)


def relay_project(mine, theirs, wk, wv, gain, kv_index, here, placement, offsets):
    blocks = len(offsets)
    depth, width = wk.shape
    out = jax.ShapeDtypeStruct((blocks, PAGE, width), bf16)
    smem = pl.BlockSpec(memory_space=pltpu.SMEM)
    vmem = pl.BlockSpec(memory_space=pltpu.VMEM)
    return pl.pallas_call(
        functools.partial(
            relay_kernel, group_slices(width), blocks, lax.axis_size("blk"), offsets
        ),
        in_specs=[smem] * 3 + [vmem] * 5,
        out_specs=[vmem, vmem],
        out_shape=[out, out],
        compiler_params=params(),
        cost_estimate=cost(),
        name="relay_project",
    )(kv_index, here, placement, mine, theirs, wk, wv, gain)


def attend_kernel(inner, base, live_ref, depth_ref, q_ref, k_ref, v_ref, p0, p1, p2, p3, out):
    pages = (p0, p1, p2, p3)
    tokens, width = q_ref.shape
    live, depth = live_ref[0], depth_ref[0]
    lane = lax.broadcasted_iota(jnp.int32, (1, LANES), 1)
    row = lax.broadcasted_iota(jnp.int32, (PAGE, PAGE), 0)
    col = lax.broadcasted_iota(jnp.int32, (PAGE, PAGE), 1)
    causal = col <= row
    key_row = lax.broadcasted_iota(jnp.int32, (PAGE, LANES), 0)
    blocks = tokens // PAGE
    for start in range(0, width, LANES):
        cols = slice(start, start + LANES)
        firsts = (base,) + (inner,) * (PMAX - 1)
        page_cols = [slice(first + start, first + start + LANES) for first in firsts]
        keys, values = [], []
        for b in range(blocks):
            rows = slice(b * PAGE, (b + 1) * PAGE)
            keep = (key_row + b * PAGE) < live
            keys.append(k_ref[rows, cols])
            shown = jnp.where(keep, v_ref[rows, cols].astype(f32), 0.0).astype(bf16)
            ones = jnp.where(keep, 1.0, 0.0).astype(bf16)
            values.append(jnp.concatenate([shown, ones], axis=1))
        for p in range(PMAX):
            keep = jnp.where(p < depth, 1.0, 0.0).astype(bf16)
            keys.append(pages[p][0, :, page_cols[p]])
            ones = jnp.full((PAGE, LANES), 1.0, bf16) * keep
            values.append(jnp.concatenate([pages[p][1, :, page_cols[p]] * keep, ones], axis=1))
        for b in range(blocks):
            rows = slice(b * PAGE, (b + 1) * PAGE)
            q = q_ref[rows, cols]
            ratios = []
            for side in range(2):
                q_side = jnp.where((lane // HD) == side, q, jnp.zeros_like(q))
                acc = jnp.zeros((PAGE, 2 * LANES), f32)
                for j in list(range(b + 1)) + list(range(blocks, blocks + PMAX)):
                    scores = lax.dot_general(
                        q_side, keys[j], (((1,), (1,)), ((), ())), preferred_element_type=f32
                    )
                    weights = jnp.exp(scores)
                    if j == b:
                        weights = jnp.where(causal, weights, 0.0)
                    acc += jnp.dot(weights.astype(bf16), values[j], preferred_element_type=f32)
                ratios.append(acc[:, :LANES] / acc[:, LANES:])
            out[rows, cols] = jnp.where((lane // HD) == 0, ratios[0], ratios[1]).astype(bf16)


def attend(live, depth, q, k, v, pages, inner, base):
    tokens, width = q.shape
    heads = width // HD
    smem = pl.BlockSpec(memory_space=pltpu.SMEM)
    vmem = pl.BlockSpec(memory_space=pltpu.VMEM)
    keys = tokens + PMAX * PAGE
    return pl.pallas_call(
        functools.partial(attend_kernel, inner, base),
        in_specs=[smem, smem] + [vmem] * 7,
        out_specs=vmem,
        out_shape=jax.ShapeDtypeStruct((tokens, width), bf16),
        compiler_params=params(),
        cost_estimate=cost(),
        name="attend",
    )(live, depth, q, k, v, *pages)


def projected_heads(slices, rows, mine, theirs, w_mine, w_theirs):
    def half(parts, weights):
        total = None
        for part, (start, size) in zip(parts, slices):
            weight = weights[start : start + size, :]
            term = jnp.dot(part[rows, :], weight, preferred_element_type=f32)
            total = term if total is None else total + term
        return total

    return half(mine, w_mine) + half(theirs, w_theirs)


def partial_kernel(slices, w_mine, w_theirs, *refs):
    count = len(slices)
    mine, theirs, out = refs[:count], refs[count : 2 * count], refs[2 * count]
    for low in range(0, out.shape[0], PAGE):
        rows = slice(low, low + PAGE)
        out[rows, :] = projected_heads(slices, rows, mine, theirs, w_mine, w_theirs)


def partial_branch(slices, w_mine, w_theirs, mine, theirs):
    tokens, depth = mine[0].shape[0], w_mine.shape[1]
    vmem = pl.BlockSpec(memory_space=pltpu.VMEM)
    return pl.pallas_call(
        functools.partial(partial_kernel, slices),
        in_specs=[vmem] * (2 + 2 * len(slices)),
        out_specs=vmem,
        out_shape=jax.ShapeDtypeStruct((tokens, depth), f32),
        compiler_params=params(),
        cost_estimate=cost(),
        name="partial_branch",
    )(w_mine, w_theirs, *mine, *theirs)


def finish_kernel(slices, hidden, w_mine, w_theirs, rate, begun, *refs):
    count = len(slices)
    mine, theirs = refs[:count], refs[count : 2 * count]
    out, buf, sem = refs[2 * count :]
    step = buf.shape[1]
    copies = []
    for i in range(buf.shape[0]):
        rows = slice(i * step, (i + 1) * step)
        branch = begun[rows, :] + projected_heads(slices, rows, mine, theirs, w_mine, w_theirs)
        hidden_f = hidden[rows, :].astype(f32)
        mean = jnp.mean(hidden_f * hidden_f, axis=-1, keepdims=True)
        anchor = hidden_f * lax.rsqrt(mean + epsilon)
        mean = jnp.mean(branch * branch, axis=-1, keepdims=True)
        normed = branch * lax.rsqrt(mean + epsilon)
        updated = anchor + rate[...] * (normed - anchor)
        scale = lax.rsqrt(jnp.mean(updated * updated, axis=-1, keepdims=True) + epsilon)
        buf[i] = (updated * scale).astype(bf16)
        copy = pltpu.make_async_copy(buf.at[i], out.at[pl.ds(i * step, step)], sem.at[i])
        copy.start()
        copies.append(copy)
    for copy in copies:
        copy.wait()


def finish(slices, hidden_in, w_mine, w_theirs, rate, begun, mine, theirs):
    tokens, depth = hidden_in.shape
    steps = 4
    vmem = pl.BlockSpec(memory_space=pltpu.VMEM)
    return pl.pallas_call(
        functools.partial(finish_kernel, slices),
        in_specs=[vmem] * (5 + 2 * len(slices)),
        out_specs=pl.BlockSpec(memory_space=pltpu.HBM),
        out_shape=jax.ShapeDtypeStruct((tokens, depth), bf16),
        scratch_shapes=[
            pltpu.VMEM((steps, tokens // steps, depth), bf16),
            pltpu.SemaphoreType.DMA((steps,)),
        ],
        compiler_params=params(),
        cost_estimate=cost(),
        name="finish",
    )(hidden_in, w_mine, w_theirs, rate, begun, *mine, *theirs)


def body(
    hidden_in,
    w_query,
    w_key,
    w_value,
    w_out,
    head_gain,
    eigen_rate,
    pool_keys,
    pool_values,
    req_len,
    prefix_len,
    prefix_pages,
    placement,
):
    devices = lax.axis_size("blk")
    here = lax.axis_index("blk").astype(jnp.int32).reshape(1)
    kv_index = lax.axis_index("kv").astype(jnp.int32).reshape(1)
    blocks = hidden_in.shape[0] // PAGE
    gain = head_gain.reshape(1, -1)
    rate = eigen_rate.reshape(1, -1)
    page_offsets = [slot * devices // PMAX + 1 for slot in range(PMAX)]
    block_offsets = [(2 * b + 1) * devices // (2 * blocks) for b in range(blocks)]

    assert blocks == lax.axis_size("kv") == 2
    relay_send = split_rows(hidden_in, kv_index)
    near_send, far_send = pack(
        pool_keys, pool_values, prefix_pages.T, here, devices, page_offsets, relay_send
    )
    projected = project(hidden_in, w_query, w_key, w_value, gain)

    def fetch(block, slot):
        return over_blk(block, [devices - page_offsets[slot]] * 2)

    relay_mine = over_blk(relay_send, block_offsets)
    first = {slot: fetch(far_send[0][slot - 1], slot) for slot in SLOT_ORDER}
    arrived = [first[slot] for slot in SLOT_ORDER]
    near = fetch(after(near_send, projected[0][0], relay_mine, *arrived), 0)
    second = {}
    for i, slot in enumerate(SLOT_ORDER):
        second[slot] = fetch(after(far_send[1][slot - 1], projected[0][0], relay_mine, *arrived[: i + 1]), slot)
    pages = [[near] + [got[slot] for slot in range(1, PMAX)] for got in (first, second)]
    w_theirs = from_behind(w_out, "kv", 1)
    relay_theirs = from_behind(after(relay_mine, w_theirs, *arrived), "kv", 1)
    new_keys, new_values = relay_project(
        relay_mine, relay_theirs, w_key, w_value, gain, kv_index, here, placement, block_offsets
    )

    mine, theirs, slices = [[], []], [[], []], [[], []]
    begun = None
    for (g, inner, start, size), (q, k, v) in zip(unit_slices(), projected):
        if g and begun is None:
            begun = partial_branch(slices[0], w_out, w_theirs, mine[0], theirs[0])
        if g:
            q = after(q, new_keys, begun)
        attended = attend(req_len, prefix_len, q, k, v, pages[g], inner, start)
        mine[g].append(attended)
        theirs[g].append(from_behind(attended, "kv", 1))
        slices[g].append((start, size))
    layer_out = finish(
        slices[1], hidden_in, w_out, w_theirs, rate, begun, mine[1], theirs[1]
    )
    return (layer_out, new_keys, new_values)


def solution(mesh):
    in_specs = (
        P("blk", None),
        P(None, "kv"),
        P(None, "kv"),
        P(None, "kv"),
        P("kv", None),
        P("kv"),
        P(),
        P("blk", None, "kv"),
        P("blk", None, "kv"),
        P("blk"),
        P("blk"),
        P(),
        P(),
    )
    out_specs = (P("blk", None), P("blk", None, "kv"), P("blk", None, "kv"))
    return jax.shard_map(body, mesh=mesh, in_specs=in_specs, out_specs=out_specs, check_vma=False)
```

```python
import functools
import math

import jax
import jax.numpy as jnp
from jax import lax
from jax.experimental import pallas as pl
from jax.experimental.pallas import tpu as pltpu
from jax.sharding import PartitionSpec as P

HD = 64
PAGE = 256
PMAX = 4
LANES = 128
GROUPS = (256, 384)
UNITS = ((256,), (128, 128, 128))
PARTS = 4
SLOT_ORDER = (2, 1, 3)
VMEM_LIMIT = 16 * 1024 * 1024
FIRST_LIMIT = 58 * 1024 * 1024

epsilon = 1e-06

f32 = jnp.float32
bf16 = jnp.bfloat16


def from_behind(block, axis, distance):
    devices = range(lax.axis_size(axis))
    route = [((i - distance) % len(devices), i) for i in devices]
    return lax.ppermute(block, axis, route)


def over_blk(block, distances):
    devices = lax.axis_size("blk")
    route = []
    for kv in range(lax.axis_size("kv")):
        for i in range(devices):
            route.append((kv * devices + (i - distances[kv]) % devices, kv * devices + i))
    return lax.ppermute(block, ("kv", "blk"), route)


def after(block, *others):
    return lax.optimization_barrier((block, *others))[0]


def group_slices(width):
    slices, start = [], 0
    for size in GROUPS:
        slices.append((start, size))
        start += size
    assert start == width
    return slices


def unit_slices():
    units, base = [], 0
    for g, sizes in enumerate(UNITS):
        inner = 0
        for size in sizes:
            units.append((g, inner, base + inner, size))
            inner += size
        base += inner
    return units


def params(limit=VMEM_LIMIT):
    return pltpu.CompilerParams(vmem_limit_bytes=limit)


def cost():
    return pl.CostEstimate(flops=1, bytes_accessed=1, transcendentals=0)


def split_kernel(kv_ref, hidden, out, sem):
    part = PAGE // PARTS
    copies = []
    for i in range(PARTS):
        rows = pl.ds(pl.multiple_of(kv_ref[0] * PAGE + i * part, part), part)
        target = out.at[pl.ds(i * part, part)]
        copies.append(pltpu.make_async_copy(hidden.at[rows], target, sem.at[i]))
    for copy in copies:
        copy.start()
    for copy in copies:
        copy.wait()


def split_rows(hidden_in, kv_index):
    return pl.pallas_call(
        split_kernel,
        in_specs=[pl.BlockSpec(memory_space=pltpu.SMEM), pl.BlockSpec(memory_space=pltpu.HBM)],
        out_specs=pl.BlockSpec(memory_space=pltpu.VMEM),
        out_shape=jax.ShapeDtypeStruct((PAGE, hidden_in.shape[1]), bf16),
        scratch_shapes=[pltpu.SemaphoreType.DMA((PARTS,))],
        compiler_params=params(FIRST_LIMIT),
        cost_estimate=cost(),
        name="split_rows",
    )(kv_index, hidden_in)


def pack_kernel(slices, devices, offsets, here_ref, table, keys, values, _, *rest):
    outs, (buf, sem) = rest[:-2], rest[-2:]
    copies = []
    for slot in range(PMAX):
        asker = lax.rem(here_ref[0] + (devices - offsets[slot]), devices)
        local = lax.rem(table[slot, asker], keys.shape[0])
        for side, pool in enumerate((keys, values)):
            index = 2 * slot + side
            copies.append(pltpu.make_async_copy(pool.at[local], buf.at[index], sem.at[index]))
    for copy in copies:
        copy.start()
    for slot in range(PMAX):
        for side in range(2):
            index = 2 * slot + side
            copies[index].wait()
            if slot == 0:
                outs[0][side] = buf[index]
                continue
            for g, (start, size) in enumerate(slices):
                outs[g * (PMAX - 1) + slot][side] = buf[index, :, start : start + size]


def pack(pool_keys, pool_values, table, here, devices, offsets, first):
    width = pool_keys.shape[2]
    slices = group_slices(width)
    outs = [jax.ShapeDtypeStruct((2, PAGE, width), bf16)]
    for _, size in slices:
        outs += [jax.ShapeDtypeStruct((2, PAGE, size), bf16)] * (PMAX - 1)
    smem = pl.BlockSpec(memory_space=pltpu.SMEM)
    hbm = pl.BlockSpec(memory_space=pltpu.HBM)
    result = pl.pallas_call(
        functools.partial(pack_kernel, slices, devices, offsets),
        in_specs=[smem, smem, hbm, hbm, pl.BlockSpec(memory_space=pl.ANY)],
        out_specs=[pl.BlockSpec(memory_space=pltpu.VMEM)] * len(outs),
        out_shape=outs,
        scratch_shapes=[
            pltpu.VMEM((2 * PMAX, PAGE, width), bf16),
            pltpu.SemaphoreType.DMA((2 * PMAX,)),
        ],
        compiler_params=params(FIRST_LIMIT),
        cost_estimate=cost(),
        name="pack",
    )(here, table, pool_keys, pool_values, first)
    each = PMAX - 1
    return result[0], [result[1 + each * g : 1 + each * (g + 1)] for g in range(len(slices))]


def head_sum_matrix():
    rows = (lax.broadcasted_iota(jnp.int32, (2 * LANES, LANES), 0) % LANES) // HD
    cols = lax.broadcasted_iota(jnp.int32, (2 * LANES, LANES), 1) // HD
    return jnp.where(rows == cols, 1.0 / HD, 0.0).astype(bf16)


def head_norm(projected, gain, matrix):
    parts = []
    for start in range(0, projected.shape[1], LANES):
        part = projected[:, start : start + LANES]
        squares = part * part
        high = squares.astype(bf16)
        low = (squares - high.astype(f32)).astype(bf16)
        both = jnp.concatenate([high, low], axis=1)
        mean = jnp.dot(both, matrix, preferred_element_type=f32)
        parts.append(part * lax.rsqrt(mean + epsilon) * gain[:, start : start + LANES])
    return jnp.concatenate(parts, axis=1) if len(parts) > 1 else parts[0]


def row_scale_of(hidden):
    hidden_f = hidden.astype(f32)
    return lax.rsqrt(jnp.mean(hidden_f * hidden_f, axis=-1, keepdims=True) + epsilon)


def project_kernel(slices, hidden, wq, wk, wv, gain, *outs):
    matrix = head_sum_matrix()
    rows_all = hidden.shape[0]
    for low in range(0, rows_all, PAGE):
        rows = slice(low, low + PAGE)
        x = hidden[rows, :]
        scale = row_scale_of(x)
        for g, (start, size) in enumerate(slices):
            cols = slice(start, start + size)
            q = jnp.dot(x, wq[:, cols], preferred_element_type=f32)
            q = head_norm(q, gain[:, cols], matrix).astype(bf16)
            outs[3 * g][rows, :] = q * jnp.asarray(1.0 / math.sqrt(HD), bf16)
            k = jnp.dot(x, wk[:, cols], preferred_element_type=f32)
            outs[3 * g + 1][rows, :] = head_norm(k, gain[:, cols], matrix).astype(bf16)
            v = jnp.dot(x, wv[:, cols], preferred_element_type=f32)
            outs[3 * g + 2][rows, :] = (v * scale).astype(bf16)


def project(hidden_in, wq, wk, wv, gain):
    tokens, depth = hidden_in.shape
    width = wq.shape[1]
    slices = [(start, size) for _, _, start, size in unit_slices()]
    outs = []
    for _, size in slices:
        outs += [jax.ShapeDtypeStruct((tokens, size), bf16)] * 3
    flat = pl.pallas_call(
        functools.partial(project_kernel, slices),
        out_shape=outs,
        compiler_params=params(),
        cost_estimate=cost(),
        name="project",
    )(hidden_in, wq, wk, wv, gain)
    return [flat[3 * g : 3 * g + 3] for g in range(len(slices))]


def relay_kernel(slices, blocks, devices, offsets, kv_ref, here_ref, placement, *refs):
    mine, theirs, wk, wv, gain, key_out, value_out = refs
    matrix = head_sum_matrix()
    for rows_ref, block in ((mine, kv_ref[0]), (theirs, 1 - kv_ref[0])):
        x = rows_ref[...]
        scale = row_scale_of(x)
        offset = jnp.where(block == 0, offsets[0], offsets[1])
        source = lax.rem(here_ref[0] + (devices - offset), devices)
        slot = lax.rem(placement[source * blocks + block], blocks)
        for start, size in slices:
            cols = slice(start, start + size)
            k = jnp.dot(x, wk[:, cols], preferred_element_type=f32)
            key_out[slot, :, cols] = head_norm(k, gain[:, cols], matrix).astype(bf16)
            v = jnp.dot(x, wv[:, cols], preferred_element_type=f32)
            value_out[slot, :, cols] = (v * scale).astype(bf16)


def relay_project(mine, theirs, wk, wv, gain, kv_index, here, placement, offsets):
    blocks = len(offsets)
    depth, width = wk.shape
    out = jax.ShapeDtypeStruct((blocks, PAGE, width), bf16)
    smem = pl.BlockSpec(memory_space=pltpu.SMEM)
    vmem = pl.BlockSpec(memory_space=pltpu.VMEM)
    return pl.pallas_call(
        functools.partial(
            relay_kernel, group_slices(width), blocks, lax.axis_size("blk"), offsets
        ),
        in_specs=[smem] * 3 + [vmem] * 5,
        out_specs=[vmem, vmem],
        out_shape=[out, out],
        compiler_params=params(),
        cost_estimate=cost(),
        name="relay_project",
    )(kv_index, here, placement, mine, theirs, wk, wv, gain)


def attend_kernel(inner, base, live_ref, depth_ref, q_ref, k_ref, v_ref, p0, p1, p2, p3, out):
    pages = (p0, p1, p2, p3)
    tokens, width = q_ref.shape
    live, depth = live_ref[0], depth_ref[0]
    lane = lax.broadcasted_iota(jnp.int32, (1, LANES), 1)
    row = lax.broadcasted_iota(jnp.int32, (PAGE, PAGE), 0)
    col = lax.broadcasted_iota(jnp.int32, (PAGE, PAGE), 1)
    causal = col <= row
    key_row = lax.broadcasted_iota(jnp.int32, (PAGE, LANES), 0)
    blocks = tokens // PAGE
    for start in range(0, width, LANES):
        cols = slice(start, start + LANES)
        firsts = (base,) + (inner,) * (PMAX - 1)
        page_cols = [slice(first + start, first + start + LANES) for first in firsts]
        keys, values = [], []
        for b in range(blocks):
            rows = slice(b * PAGE, (b + 1) * PAGE)
            keep = (key_row + b * PAGE) < live
            keys.append(k_ref[rows, cols])
            shown = jnp.where(keep, v_ref[rows, cols].astype(f32), 0.0).astype(bf16)
            ones = jnp.where(keep, 1.0, 0.0).astype(bf16)
            values.append(jnp.concatenate([shown, ones], axis=1))
        for p in range(PMAX):
            keep = jnp.where(p < depth, 1.0, 0.0).astype(bf16)
            keys.append(pages[p][0, :, page_cols[p]])
            ones = jnp.full((PAGE, LANES), 1.0, bf16) * keep
            values.append(jnp.concatenate([pages[p][1, :, page_cols[p]] * keep, ones], axis=1))
        for b in range(blocks):
            rows = slice(b * PAGE, (b + 1) * PAGE)
            q = q_ref[rows, cols]
            ratios = []
            for side in range(2):
                q_side = jnp.where((lane // HD) == side, q, jnp.zeros_like(q))
                acc = jnp.zeros((PAGE, 2 * LANES), f32)
                for j in list(range(b + 1)) + list(range(blocks, blocks + PMAX)):
                    scores = lax.dot_general(
                        q_side, keys[j], (((1,), (1,)), ((), ())), preferred_element_type=f32
                    )
                    weights = jnp.exp(scores)
                    if j == b:
                        weights = jnp.where(causal, weights, 0.0)
                    acc += jnp.dot(weights.astype(bf16), values[j], preferred_element_type=f32)
                ratios.append(acc[:, :LANES] / acc[:, LANES:])
            out[rows, cols] = jnp.where((lane // HD) == 0, ratios[0], ratios[1]).astype(bf16)


def attend(live, depth, q, k, v, pages, inner, base):
    tokens, width = q.shape
    heads = width // HD
    smem = pl.BlockSpec(memory_space=pltpu.SMEM)
    vmem = pl.BlockSpec(memory_space=pltpu.VMEM)
    keys = tokens + PMAX * PAGE
    return pl.pallas_call(
        functools.partial(attend_kernel, inner, base),
        in_specs=[smem, smem] + [vmem] * 7,
        out_specs=vmem,
        out_shape=jax.ShapeDtypeStruct((tokens, width), bf16),
        compiler_params=params(),
        cost_estimate=cost(),
        name="attend",
    )(live, depth, q, k, v, *pages)


def projected_heads(slices, rows, mine, theirs, w_mine, w_theirs):
    def half(parts, weights):
        total = None
        for part, (start, size) in zip(parts, slices):
            weight = weights[start : start + size, :]
            term = jnp.dot(part[rows, :], weight, preferred_element_type=f32)
            total = term if total is None else total + term
        return total

    return half(mine, w_mine) + half(theirs, w_theirs)


def partial_kernel(slices, w_mine, w_theirs, *refs):
    count = len(slices)
    mine, theirs, out = refs[:count], refs[count : 2 * count], refs[2 * count]
    for low in range(0, out.shape[0], PAGE):
        rows = slice(low, low + PAGE)
        out[rows, :] = projected_heads(slices, rows, mine, theirs, w_mine, w_theirs)


def partial_branch(slices, w_mine, w_theirs, mine, theirs):
    tokens, depth = mine[0].shape[0], w_mine.shape[1]
    vmem = pl.BlockSpec(memory_space=pltpu.VMEM)
    return pl.pallas_call(
        functools.partial(partial_kernel, slices),
        in_specs=[vmem] * (2 + 2 * len(slices)),
        out_specs=vmem,
        out_shape=jax.ShapeDtypeStruct((tokens, depth), f32),
        compiler_params=params(),
        cost_estimate=cost(),
        name="partial_branch",
    )(w_mine, w_theirs, *mine, *theirs)


def finish_kernel(slices, hidden, w_mine, w_theirs, rate, begun, *refs):
    count = len(slices)
    mine, theirs = refs[:count], refs[count : 2 * count]
    out, buf, sem = refs[2 * count :]
    step = buf.shape[1]
    copies = []
    for i in range(buf.shape[0]):
        rows = slice(i * step, (i + 1) * step)
        branch = begun[rows, :] + projected_heads(slices, rows, mine, theirs, w_mine, w_theirs)
        hidden_f = hidden[rows, :].astype(f32)
        mean = jnp.mean(hidden_f * hidden_f, axis=-1, keepdims=True)
        anchor = hidden_f * lax.rsqrt(mean + epsilon)
        mean = jnp.mean(branch * branch, axis=-1, keepdims=True)
        normed = branch * lax.rsqrt(mean + epsilon)
        updated = anchor + rate[...] * (normed - anchor)
        scale = lax.rsqrt(jnp.mean(updated * updated, axis=-1, keepdims=True) + epsilon)
        buf[i] = (updated * scale).astype(bf16)
        copy = pltpu.make_async_copy(buf.at[i], out.at[pl.ds(i * step, step)], sem.at[i])
        copy.start()
        copies.append(copy)
    for copy in copies:
        copy.wait()


def finish(slices, hidden_in, w_mine, w_theirs, rate, begun, mine, theirs):
    tokens, depth = hidden_in.shape
    steps = 4
    vmem = pl.BlockSpec(memory_space=pltpu.VMEM)
    return pl.pallas_call(
        functools.partial(finish_kernel, slices),
        in_specs=[vmem] * (5 + 2 * len(slices)),
        out_specs=pl.BlockSpec(memory_space=pltpu.HBM),
        out_shape=jax.ShapeDtypeStruct((tokens, depth), bf16),
        scratch_shapes=[
            pltpu.VMEM((steps, tokens // steps, depth), bf16),
            pltpu.SemaphoreType.DMA((steps,)),
        ],
        compiler_params=params(),
        cost_estimate=cost(),
        name="finish",
    )(hidden_in, w_mine, w_theirs, rate, begun, *mine, *theirs)


def body(
    hidden_in,
    w_query,
    w_key,
    w_value,
    w_out,
    head_gain,
    eigen_rate,
    pool_keys,
    pool_values,
    req_len,
    prefix_len,
    prefix_pages,
    placement,
):
    devices = lax.axis_size("blk")
    here = lax.axis_index("blk").astype(jnp.int32).reshape(1)
    kv_index = lax.axis_index("kv").astype(jnp.int32).reshape(1)
    blocks = hidden_in.shape[0] // PAGE
    gain = head_gain.reshape(1, -1)
    rate = eigen_rate.reshape(1, -1)
    page_offsets = [slot * devices // PMAX + 1 for slot in range(PMAX)]
    block_offsets = [(2 * b + 1) * devices // (2 * blocks) for b in range(blocks)]

    assert blocks == lax.axis_size("kv") == 2
    relay_send = split_rows(hidden_in, kv_index)
    near_send, far_send = pack(
        pool_keys, pool_values, prefix_pages.T, here, devices, page_offsets, relay_send
    )
    projected = project(hidden_in, w_query, w_key, w_value, gain)

    def fetch(block, slot):
        return over_blk(block, [devices - page_offsets[slot]] * 2)

    relay_mine = over_blk(relay_send, block_offsets)
    near = fetch(near_send, 0)
    first = {}
    for slot in SLOT_ORDER:
        block = far_send[0][slot - 1]
        if slot == SLOT_ORDER[-1]:
            block = after(block, projected[0][0], near, relay_mine)
        first[slot] = fetch(block, slot)
    arrived = [first[slot] for slot in SLOT_ORDER]
    second = {}
    for i, slot in enumerate(SLOT_ORDER):
        second[slot] = fetch(after(far_send[1][slot - 1], projected[0][0], relay_mine, *arrived[: i + 1]), slot)
    pages = [[near] + [got[slot] for slot in range(1, PMAX)] for got in (first, second)]
    w_theirs = from_behind(w_out, "kv", 1)
    relay_theirs = from_behind(after(relay_mine, w_theirs, *arrived), "kv", 1)
    new_keys, new_values = relay_project(
        relay_mine, relay_theirs, w_key, w_value, gain, kv_index, here, placement, block_offsets
    )

    mine, theirs, slices = [[], []], [[], []], [[], []]
    begun = None
    for (g, inner, start, size), (q, k, v) in zip(unit_slices(), projected):
        if g and begun is None:
            begun = partial_branch(slices[0], w_out, w_theirs, mine[0], theirs[0])
        if g:
            q = after(q, new_keys, begun)
        attended = attend(req_len, prefix_len, q, k, v, pages[g], inner, start)
        mine[g].append(attended)
        theirs[g].append(from_behind(attended, "kv", 1))
        slices[g].append((start, size))
    layer_out = finish(
        slices[1], hidden_in, w_out, w_theirs, rate, begun, mine[1], theirs[1]
    )
    return (layer_out, new_keys, new_values)


def solution(mesh):
    in_specs = (
        P("blk", None),
        P(None, "kv"),
        P(None, "kv"),
        P(None, "kv"),
        P("kv", None),
        P("kv"),
        P(),
        P("blk", None, "kv"),
        P("blk", None, "kv"),
        P("blk"),
        P("blk"),
        P(),
        P(),
    )
    out_specs = (P("blk", None), P("blk", None, "kv"), P("blk", None, "kv"))
    return jax.shard_map(body, mesh=mesh, in_specs=in_specs, out_specs=out_specs, check_vma=False)
```

```python
import functools
import math

import jax
import jax.numpy as jnp
from jax import lax
from jax.experimental import pallas as pl
from jax.experimental.pallas import tpu as pltpu
from jax.sharding import PartitionSpec as P

HD = 64
PAGE = 256
PMAX = 4
LANES = 128
GROUPS = (256, 384)
UNITS = ((256,), (128, 128, 128))
PARTS = 4
SLOT_ORDER = (2, 1, 3)
VMEM_LIMIT = 16 * 1024 * 1024
FIRST_LIMIT = 58 * 1024 * 1024

epsilon = 1e-06

f32 = jnp.float32
bf16 = jnp.bfloat16


def from_behind(block, axis, distance):
    devices = range(lax.axis_size(axis))
    route = [((i - distance) % len(devices), i) for i in devices]
    return lax.ppermute(block, axis, route)


def over_blk(block, distances):
    devices = lax.axis_size("blk")
    route = []
    for kv in range(lax.axis_size("kv")):
        for i in range(devices):
            route.append((kv * devices + (i - distances[kv]) % devices, kv * devices + i))
    return lax.ppermute(block, ("kv", "blk"), route)


def after(block, *others):
    return lax.optimization_barrier((block, *others))[0]


def group_slices(width):
    slices, start = [], 0
    for size in GROUPS:
        slices.append((start, size))
        start += size
    assert start == width
    return slices


def unit_slices():
    units, base = [], 0
    for g, sizes in enumerate(UNITS):
        inner = 0
        for size in sizes:
            units.append((g, inner, base + inner, size))
            inner += size
        base += inner
    return units


def params(limit=VMEM_LIMIT):
    return pltpu.CompilerParams(vmem_limit_bytes=limit)


def cost():
    return pl.CostEstimate(flops=1, bytes_accessed=1, transcendentals=0)


def split_kernel(kv_ref, hidden, out, sem):
    part = PAGE // PARTS
    copies = []
    for i in range(PARTS):
        rows = pl.ds(pl.multiple_of(kv_ref[0] * PAGE + i * part, part), part)
        target = out.at[pl.ds(i * part, part)]
        copies.append(pltpu.make_async_copy(hidden.at[rows], target, sem.at[i]))
    for copy in copies:
        copy.start()
    for copy in copies:
        copy.wait()


def split_rows(hidden_in, kv_index):
    return pl.pallas_call(
        split_kernel,
        in_specs=[pl.BlockSpec(memory_space=pltpu.SMEM), pl.BlockSpec(memory_space=pltpu.HBM)],
        out_specs=pl.BlockSpec(memory_space=pltpu.VMEM),
        out_shape=jax.ShapeDtypeStruct((PAGE, hidden_in.shape[1]), bf16),
        scratch_shapes=[pltpu.SemaphoreType.DMA((PARTS,))],
        compiler_params=params(FIRST_LIMIT),
        cost_estimate=cost(),
        name="split_rows",
    )(kv_index, hidden_in)


def pack_kernel(slices, devices, offsets, here_ref, table, keys, values, _, *rest):
    outs, (buf, sem) = rest[:-2], rest[-2:]
    copies = []
    for slot in range(PMAX):
        asker = lax.rem(here_ref[0] + (devices - offsets[slot]), devices)
        local = lax.rem(table[slot, asker], keys.shape[0])
        for side, pool in enumerate((keys, values)):
            index = 2 * slot + side
            copies.append(pltpu.make_async_copy(pool.at[local], buf.at[index], sem.at[index]))
    for copy in copies:
        copy.start()
    for slot in range(PMAX):
        for side in range(2):
            index = 2 * slot + side
            copies[index].wait()
            for g, (start, size) in enumerate(slices):
                outs[g * PMAX + slot][side] = buf[index, :, start : start + size]


def pack(pool_keys, pool_values, table, here, devices, offsets, first):
    width = pool_keys.shape[2]
    slices = group_slices(width)
    outs = []
    for _, size in slices:
        outs += [jax.ShapeDtypeStruct((2, PAGE, size), bf16)] * PMAX
    smem = pl.BlockSpec(memory_space=pltpu.SMEM)
    hbm = pl.BlockSpec(memory_space=pltpu.HBM)
    result = pl.pallas_call(
        functools.partial(pack_kernel, slices, devices, offsets),
        in_specs=[smem, smem, hbm, hbm, pl.BlockSpec(memory_space=pl.ANY)],
        out_specs=[pl.BlockSpec(memory_space=pltpu.VMEM)] * len(outs),
        out_shape=outs,
        scratch_shapes=[
            pltpu.VMEM((2 * PMAX, PAGE, width), bf16),
            pltpu.SemaphoreType.DMA((2 * PMAX,)),
        ],
        compiler_params=params(FIRST_LIMIT),
        cost_estimate=cost(),
        name="pack",
    )(here, table, pool_keys, pool_values, first)
    return [result[PMAX * g : PMAX * (g + 1)] for g in range(len(slices))]


def head_sum_matrix():
    rows = (lax.broadcasted_iota(jnp.int32, (2 * LANES, LANES), 0) % LANES) // HD
    cols = lax.broadcasted_iota(jnp.int32, (2 * LANES, LANES), 1) // HD
    return jnp.where(rows == cols, 1.0 / HD, 0.0).astype(bf16)


def head_norm(projected, gain, matrix):
    parts = []
    for start in range(0, projected.shape[1], LANES):
        part = projected[:, start : start + LANES]
        squares = part * part
        high = squares.astype(bf16)
        low = (squares - high.astype(f32)).astype(bf16)
        both = jnp.concatenate([high, low], axis=1)
        mean = jnp.dot(both, matrix, preferred_element_type=f32)
        parts.append(part * lax.rsqrt(mean + epsilon) * gain[:, start : start + LANES])
    return jnp.concatenate(parts, axis=1) if len(parts) > 1 else parts[0]


def row_scale_of(hidden):
    hidden_f = hidden.astype(f32)
    return lax.rsqrt(jnp.mean(hidden_f * hidden_f, axis=-1, keepdims=True) + epsilon)


def project_kernel(slices, hidden, wq, wk, wv, gain, *outs):
    matrix = head_sum_matrix()
    rows_all = hidden.shape[0]
    for low in range(0, rows_all, PAGE):
        rows = slice(low, low + PAGE)
        x = hidden[rows, :]
        scale = row_scale_of(x)
        for g, (start, size) in enumerate(slices):
            cols = slice(start, start + size)
            q = jnp.dot(x, wq[:, cols], preferred_element_type=f32)
            q = head_norm(q, gain[:, cols], matrix).astype(bf16)
            outs[3 * g][rows, :] = q * jnp.asarray(1.0 / math.sqrt(HD), bf16)
            k = jnp.dot(x, wk[:, cols], preferred_element_type=f32)
            outs[3 * g + 1][rows, :] = head_norm(k, gain[:, cols], matrix).astype(bf16)
            v = jnp.dot(x, wv[:, cols], preferred_element_type=f32)
            outs[3 * g + 2][rows, :] = (v * scale).astype(bf16)


def project(hidden_in, wq, wk, wv, gain):
    tokens, depth = hidden_in.shape
    width = wq.shape[1]
    slices = [(start, size) for _, _, start, size in unit_slices()]
    outs = []
    for _, size in slices:
        outs += [jax.ShapeDtypeStruct((tokens, size), bf16)] * 3
    flat = pl.pallas_call(
        functools.partial(project_kernel, slices),
        out_shape=outs,
        compiler_params=params(),
        cost_estimate=cost(),
        name="project",
    )(hidden_in, wq, wk, wv, gain)
    return [flat[3 * g : 3 * g + 3] for g in range(len(slices))]


def relay_kernel(slices, blocks, devices, offsets, kv_ref, here_ref, placement, *refs):
    mine, theirs, wk, wv, gain, key_out, value_out = refs
    matrix = head_sum_matrix()
    for rows_ref, block in ((mine, kv_ref[0]), (theirs, 1 - kv_ref[0])):
        x = rows_ref[...]
        scale = row_scale_of(x)
        offset = jnp.where(block == 0, offsets[0], offsets[1])
        source = lax.rem(here_ref[0] + (devices - offset), devices)
        slot = lax.rem(placement[source * blocks + block], blocks)
        for start, size in slices:
            cols = slice(start, start + size)
            k = jnp.dot(x, wk[:, cols], preferred_element_type=f32)
            key_out[slot, :, cols] = head_norm(k, gain[:, cols], matrix).astype(bf16)
            v = jnp.dot(x, wv[:, cols], preferred_element_type=f32)
            value_out[slot, :, cols] = (v * scale).astype(bf16)


def relay_project(mine, theirs, wk, wv, gain, kv_index, here, placement, offsets):
    blocks = len(offsets)
    depth, width = wk.shape
    out = jax.ShapeDtypeStruct((blocks, PAGE, width), bf16)
    smem = pl.BlockSpec(memory_space=pltpu.SMEM)
    vmem = pl.BlockSpec(memory_space=pltpu.VMEM)
    return pl.pallas_call(
        functools.partial(
            relay_kernel, group_slices(width), blocks, lax.axis_size("blk"), offsets
        ),
        in_specs=[smem] * 3 + [vmem] * 5,
        out_specs=[vmem, vmem],
        out_shape=[out, out],
        compiler_params=params(),
        cost_estimate=cost(),
        name="relay_project",
    )(kv_index, here, placement, mine, theirs, wk, wv, gain)


def attend_kernel(inner, live_ref, depth_ref, q_ref, k_ref, v_ref, p0, p1, p2, p3, out):
    pages = (p0, p1, p2, p3)
    tokens, width = q_ref.shape
    live, depth = live_ref[0], depth_ref[0]
    lane = lax.broadcasted_iota(jnp.int32, (1, LANES), 1)
    row = lax.broadcasted_iota(jnp.int32, (PAGE, PAGE), 0)
    col = lax.broadcasted_iota(jnp.int32, (PAGE, PAGE), 1)
    causal = col <= row
    key_row = lax.broadcasted_iota(jnp.int32, (PAGE, LANES), 0)
    blocks = tokens // PAGE
    for start in range(0, width, LANES):
        cols = slice(start, start + LANES)
        page_cols = slice(inner + start, inner + start + LANES)
        keys, values = [], []
        for b in range(blocks):
            rows = slice(b * PAGE, (b + 1) * PAGE)
            keep = (key_row + b * PAGE) < live
            keys.append(k_ref[rows, cols])
            shown = jnp.where(keep, v_ref[rows, cols].astype(f32), 0.0).astype(bf16)
            ones = jnp.where(keep, 1.0, 0.0).astype(bf16)
            values.append(jnp.concatenate([shown, ones], axis=1))
        for p in range(PMAX):
            keep = jnp.where(p < depth, 1.0, 0.0).astype(bf16)
            keys.append(pages[p][0, :, page_cols])
            ones = jnp.full((PAGE, LANES), 1.0, bf16) * keep
            values.append(jnp.concatenate([pages[p][1, :, page_cols] * keep, ones], axis=1))
        for b in range(blocks):
            rows = slice(b * PAGE, (b + 1) * PAGE)
            q = q_ref[rows, cols]
            ratios = []
            for side in range(2):
                q_side = jnp.where((lane // HD) == side, q, jnp.zeros_like(q))
                acc = jnp.zeros((PAGE, 2 * LANES), f32)
                for j in list(range(b + 1)) + list(range(blocks, blocks + PMAX)):
                    scores = lax.dot_general(
                        q_side, keys[j], (((1,), (1,)), ((), ())), preferred_element_type=f32
                    )
                    weights = jnp.exp(scores)
                    if j == b:
                        weights = jnp.where(causal, weights, 0.0)
                    acc += jnp.dot(weights.astype(bf16), values[j], preferred_element_type=f32)
                ratios.append(acc[:, :LANES] / acc[:, LANES:])
            out[rows, cols] = jnp.where((lane // HD) == 0, ratios[0], ratios[1]).astype(bf16)


def attend(live, depth, q, k, v, pages, inner):
    tokens, width = q.shape
    heads = width // HD
    smem = pl.BlockSpec(memory_space=pltpu.SMEM)
    vmem = pl.BlockSpec(memory_space=pltpu.VMEM)
    keys = tokens + PMAX * PAGE
    return pl.pallas_call(
        functools.partial(attend_kernel, inner),
        in_specs=[smem, smem] + [vmem] * 7,
        out_specs=vmem,
        out_shape=jax.ShapeDtypeStruct((tokens, width), bf16),
        compiler_params=params(),
        cost_estimate=cost(),
        name="attend",
    )(live, depth, q, k, v, *pages)


def projected_heads(slices, rows, mine, theirs, w_mine, w_theirs):
    def half(parts, weights):
        total = None
        for part, (start, size) in zip(parts, slices):
            weight = weights[start : start + size, :]
            term = jnp.dot(part[rows, :], weight, preferred_element_type=f32)
            total = term if total is None else total + term
        return total

    return half(mine, w_mine) + half(theirs, w_theirs)


def partial_kernel(slices, w_mine, w_theirs, *refs):
    count = len(slices)
    mine, theirs, out = refs[:count], refs[count : 2 * count], refs[2 * count]
    for low in range(0, out.shape[0], PAGE):
        rows = slice(low, low + PAGE)
        out[rows, :] = projected_heads(slices, rows, mine, theirs, w_mine, w_theirs)


def partial_branch(slices, w_mine, w_theirs, mine, theirs):
    tokens, depth = mine[0].shape[0], w_mine.shape[1]
    vmem = pl.BlockSpec(memory_space=pltpu.VMEM)
    return pl.pallas_call(
        functools.partial(partial_kernel, slices),
        in_specs=[vmem] * (2 + 2 * len(slices)),
        out_specs=vmem,
        out_shape=jax.ShapeDtypeStruct((tokens, depth), f32),
        compiler_params=params(),
        cost_estimate=cost(),
        name="partial_branch",
    )(w_mine, w_theirs, *mine, *theirs)


def finish_kernel(slices, hidden, w_mine, w_theirs, rate, begun, *refs):
    count = len(slices)
    mine, theirs = refs[:count], refs[count : 2 * count]
    out, buf, sem = refs[2 * count :]
    step = buf.shape[1]
    copies = []
    for i in range(buf.shape[0]):
        rows = slice(i * step, (i + 1) * step)
        branch = begun[rows, :] + projected_heads(slices, rows, mine, theirs, w_mine, w_theirs)
        hidden_f = hidden[rows, :].astype(f32)
        mean = jnp.mean(hidden_f * hidden_f, axis=-1, keepdims=True)
        anchor = hidden_f * lax.rsqrt(mean + epsilon)
        mean = jnp.mean(branch * branch, axis=-1, keepdims=True)
        normed = branch * lax.rsqrt(mean + epsilon)
        updated = anchor + rate[...] * (normed - anchor)
        scale = lax.rsqrt(jnp.mean(updated * updated, axis=-1, keepdims=True) + epsilon)
        buf[i] = (updated * scale).astype(bf16)
        copy = pltpu.make_async_copy(buf.at[i], out.at[pl.ds(i * step, step)], sem.at[i])
        copy.start()
        copies.append(copy)
    for copy in copies:
        copy.wait()


def finish(slices, hidden_in, w_mine, w_theirs, rate, begun, mine, theirs):
    tokens, depth = hidden_in.shape
    steps = 4
    vmem = pl.BlockSpec(memory_space=pltpu.VMEM)
    return pl.pallas_call(
        functools.partial(finish_kernel, slices),
        in_specs=[vmem] * (5 + 2 * len(slices)),
        out_specs=pl.BlockSpec(memory_space=pltpu.HBM),
        out_shape=jax.ShapeDtypeStruct((tokens, depth), bf16),
        scratch_shapes=[
            pltpu.VMEM((steps, tokens // steps, depth), bf16),
            pltpu.SemaphoreType.DMA((steps,)),
        ],
        compiler_params=params(),
        cost_estimate=cost(),
        name="finish",
    )(hidden_in, w_mine, w_theirs, rate, begun, *mine, *theirs)


def body(
    hidden_in,
    w_query,
    w_key,
    w_value,
    w_out,
    head_gain,
    eigen_rate,
    pool_keys,
    pool_values,
    req_len,
    prefix_len,
    prefix_pages,
    placement,
):
    devices = lax.axis_size("blk")
    here = lax.axis_index("blk").astype(jnp.int32).reshape(1)
    kv_index = lax.axis_index("kv").astype(jnp.int32).reshape(1)
    blocks = hidden_in.shape[0] // PAGE
    gain = head_gain.reshape(1, -1)
    rate = eigen_rate.reshape(1, -1)
    page_offsets = [slot * devices // PMAX + 1 for slot in range(PMAX)]
    block_offsets = [(2 * b + 1) * devices // (2 * blocks) for b in range(blocks)]

    assert blocks == lax.axis_size("kv") == 2
    relay_send = split_rows(hidden_in, kv_index)
    page_send = pack(
        pool_keys, pool_values, prefix_pages.T, here, devices, page_offsets, relay_send
    )
    projected = project(hidden_in, w_query, w_key, w_value, gain)

    def fetch(block, slot):
        return over_blk(block, [devices - page_offsets[slot]] * 2)

    relay_mine = over_blk(relay_send, block_offsets)
    ready = projected[0][0]
    first = {slot: fetch(page_send[0][slot], slot) for slot in SLOT_ORDER}
    first[0] = fetch(after(page_send[0][0], ready, relay_mine), 0)
    arrived = [first[slot] for slot in SLOT_ORDER]
    second = {0: fetch(after(page_send[1][0], ready, first[0], relay_mine), 0)}
    for i, slot in enumerate(SLOT_ORDER):
        gate = arrived[: i + 1]
        second[slot] = fetch(after(page_send[1][slot], ready, relay_mine, *gate), slot)
    pages = [[got[slot] for slot in range(PMAX)] for got in (first, second)]
    w_theirs = from_behind(w_out, "kv", 1)
    relay_theirs = from_behind(after(relay_mine, w_theirs, *arrived, first[0]), "kv", 1)
    new_keys, new_values = relay_project(
        relay_mine, relay_theirs, w_key, w_value, gain, kv_index, here, placement, block_offsets
    )

    mine, theirs, slices = [[], []], [[], []], [[], []]
    begun = None
    for (g, inner, start, size), (q, k, v) in zip(unit_slices(), projected):
        if g and begun is None:
            begun = partial_branch(
                slices[0], w_out, after(w_theirs, new_keys), mine[0], theirs[0]
            )
        if g:
            q = after(q, new_keys, begun)
        attended = attend(req_len, prefix_len, q, k, v, pages[g], inner)
        mine[g].append(attended)
        theirs[g].append(from_behind(attended, "kv", 1))
        slices[g].append((start, size))
    layer_out = finish(
        slices[1], hidden_in, w_out, w_theirs, rate, begun, mine[1], theirs[1]
    )
    return (layer_out, new_keys, new_values)


def solution(mesh):
    in_specs = (
        P("blk", None),
        P(None, "kv"),
        P(None, "kv"),
        P(None, "kv"),
        P("kv", None),
        P("kv"),
        P(),
        P("blk", None, "kv"),
        P("blk", None, "kv"),
        P("blk"),
        P("blk"),
        P(),
        P(),
    )
    out_specs = (P("blk", None), P("blk", None, "kv"), P("blk", None, "kv"))
    return jax.shard_map(body, mesh=mesh, in_specs=in_specs, out_specs=out_specs, check_vma=False)
```

```python
import functools
import math

import jax
import jax.numpy as jnp
from jax import lax
from jax.experimental import pallas as pl
from jax.experimental.pallas import tpu as pltpu
from jax.sharding import PartitionSpec as P

HD = 64
PAGE = 256
PMAX = 4
LANES = 128
GROUPS = (256, 384)
UNITS = ((256,), (128, 128, 128))
PARTS = 4
SLOT_ORDER = (2, 1, 3)
PAGE_ORDER = (2, 1, 3, 0)
VMEM_LIMIT = 16 * 1024 * 1024
FIRST_LIMIT = 58 * 1024 * 1024

epsilon = 1e-06

f32 = jnp.float32
bf16 = jnp.bfloat16


def from_behind(block, axis, distance):
    devices = range(lax.axis_size(axis))
    route = [((i - distance) % len(devices), i) for i in devices]
    return lax.ppermute(block, axis, route)


def over_blk(block, distances):
    devices = lax.axis_size("blk")
    route = []
    for kv in range(lax.axis_size("kv")):
        for i in range(devices):
            route.append((kv * devices + (i - distances[kv]) % devices, kv * devices + i))
    return lax.ppermute(block, ("kv", "blk"), route)


def after(block, *others):
    return lax.optimization_barrier((block, *others))[0]


def group_slices(width):
    slices, start = [], 0
    for size in GROUPS:
        slices.append((start, size))
        start += size
    assert start == width
    return slices


def unit_slices():
    units, base = [], 0
    for g, sizes in enumerate(UNITS):
        inner = 0
        for size in sizes:
            units.append((g, inner, base + inner, size))
            inner += size
        base += inner
    return units


def params(limit=VMEM_LIMIT):
    return pltpu.CompilerParams(vmem_limit_bytes=limit)


def cost():
    return pl.CostEstimate(flops=1, bytes_accessed=1, transcendentals=0)


def split_kernel(kv_ref, hidden, out, sem):
    part = PAGE // PARTS
    copies = []
    for i in range(PARTS):
        rows = pl.ds(pl.multiple_of(kv_ref[0] * PAGE + i * part, part), part)
        target = out.at[pl.ds(i * part, part)]
        copies.append(pltpu.make_async_copy(hidden.at[rows], target, sem.at[i]))
    for copy in copies:
        copy.start()
    for copy in copies:
        copy.wait()


def split_rows(hidden_in, kv_index):
    return pl.pallas_call(
        split_kernel,
        in_specs=[pl.BlockSpec(memory_space=pltpu.SMEM), pl.BlockSpec(memory_space=pltpu.HBM)],
        out_specs=pl.BlockSpec(memory_space=pltpu.VMEM),
        out_shape=jax.ShapeDtypeStruct((PAGE, hidden_in.shape[1]), bf16),
        scratch_shapes=[pltpu.SemaphoreType.DMA((PARTS,))],
        compiler_params=params(FIRST_LIMIT),
        cost_estimate=cost(),
        name="split_rows",
    )(kv_index, hidden_in)


def pack_kernel(slices, devices, offsets, here_ref, table, keys, values, _, *rest):
    outs, (buf, sem) = rest[:-2], rest[-2:]
    copies = []
    for slot in range(PMAX):
        asker = lax.rem(here_ref[0] + (devices - offsets[slot]), devices)
        local = lax.rem(table[slot, asker], keys.shape[0])
        for side, pool in enumerate((keys, values)):
            index = 2 * slot + side
            copies.append(pltpu.make_async_copy(pool.at[local], buf.at[index], sem.at[index]))
    for copy in copies:
        copy.start()
    for slot in range(PMAX):
        for side in range(2):
            index = 2 * slot + side
            copies[index].wait()
            for g, (start, size) in enumerate(slices):
                outs[g * PMAX + slot][side] = buf[index, :, start : start + size]


def pack(pool_keys, pool_values, table, here, devices, offsets, first):
    width = pool_keys.shape[2]
    slices = group_slices(width)
    outs = []
    for _, size in slices:
        outs += [jax.ShapeDtypeStruct((2, PAGE, size), bf16)] * PMAX
    smem = pl.BlockSpec(memory_space=pltpu.SMEM)
    hbm = pl.BlockSpec(memory_space=pltpu.HBM)
    result = pl.pallas_call(
        functools.partial(pack_kernel, slices, devices, offsets),
        in_specs=[smem, smem, hbm, hbm, pl.BlockSpec(memory_space=pl.ANY)],
        out_specs=[pl.BlockSpec(memory_space=pltpu.VMEM)] * len(outs),
        out_shape=outs,
        scratch_shapes=[
            pltpu.VMEM((2 * PMAX, PAGE, width), bf16),
            pltpu.SemaphoreType.DMA((2 * PMAX,)),
        ],
        compiler_params=params(FIRST_LIMIT),
        cost_estimate=cost(),
        name="pack",
    )(here, table, pool_keys, pool_values, first)
    return [result[PMAX * g : PMAX * (g + 1)] for g in range(len(slices))]


def head_sum_matrix():
    rows = (lax.broadcasted_iota(jnp.int32, (2 * LANES, LANES), 0) % LANES) // HD
    cols = lax.broadcasted_iota(jnp.int32, (2 * LANES, LANES), 1) // HD
    return jnp.where(rows == cols, 1.0 / HD, 0.0).astype(bf16)


def head_norm(projected, gain, matrix):
    parts = []
    for start in range(0, projected.shape[1], LANES):
        part = projected[:, start : start + LANES]
        squares = part * part
        high = squares.astype(bf16)
        low = (squares - high.astype(f32)).astype(bf16)
        both = jnp.concatenate([high, low], axis=1)
        mean = jnp.dot(both, matrix, preferred_element_type=f32)
        parts.append(part * lax.rsqrt(mean + epsilon) * gain[:, start : start + LANES])
    return jnp.concatenate(parts, axis=1) if len(parts) > 1 else parts[0]


def row_scale_of(hidden):
    hidden_f = hidden.astype(f32)
    return lax.rsqrt(jnp.mean(hidden_f * hidden_f, axis=-1, keepdims=True) + epsilon)


def project_kernel(slices, hidden, wq, wk, wv, gain, *outs):
    matrix = head_sum_matrix()
    rows_all = hidden.shape[0]
    for low in range(0, rows_all, PAGE):
        rows = slice(low, low + PAGE)
        x = hidden[rows, :]
        scale = row_scale_of(x)
        for g, (start, size) in enumerate(slices):
            cols = slice(start, start + size)
            q = jnp.dot(x, wq[:, cols], preferred_element_type=f32)
            q = head_norm(q, gain[:, cols], matrix).astype(bf16)
            outs[3 * g][rows, :] = q * jnp.asarray(1.0 / math.sqrt(HD), bf16)
            k = jnp.dot(x, wk[:, cols], preferred_element_type=f32)
            outs[3 * g + 1][rows, :] = head_norm(k, gain[:, cols], matrix).astype(bf16)
            v = jnp.dot(x, wv[:, cols], preferred_element_type=f32)
            outs[3 * g + 2][rows, :] = (v * scale).astype(bf16)


def project(hidden_in, wq, wk, wv, gain):
    tokens, depth = hidden_in.shape
    width = wq.shape[1]
    slices = [(start, size) for _, _, start, size in unit_slices()]
    outs = []
    for _, size in slices:
        outs += [jax.ShapeDtypeStruct((tokens, size), bf16)] * 3
    flat = pl.pallas_call(
        functools.partial(project_kernel, slices),
        out_shape=outs,
        compiler_params=params(),
        cost_estimate=cost(),
        name="project",
    )(hidden_in, wq, wk, wv, gain)
    return [flat[3 * g : 3 * g + 3] for g in range(len(slices))]


def relay_kernel(slices, blocks, devices, offsets, kv_ref, here_ref, placement, *refs):
    mine, theirs, wk, wv, gain, key_out, value_out = refs
    matrix = head_sum_matrix()
    for rows_ref, block in ((mine, kv_ref[0]), (theirs, 1 - kv_ref[0])):
        x = rows_ref[...]
        scale = row_scale_of(x)
        offset = jnp.where(block == 0, offsets[0], offsets[1])
        source = lax.rem(here_ref[0] + (devices - offset), devices)
        slot = lax.rem(placement[source * blocks + block], blocks)
        for start, size in slices:
            cols = slice(start, start + size)
            k = jnp.dot(x, wk[:, cols], preferred_element_type=f32)
            key_out[slot, :, cols] = head_norm(k, gain[:, cols], matrix).astype(bf16)
            v = jnp.dot(x, wv[:, cols], preferred_element_type=f32)
            value_out[slot, :, cols] = (v * scale).astype(bf16)


def relay_project(mine, theirs, wk, wv, gain, kv_index, here, placement, offsets):
    blocks = len(offsets)
    depth, width = wk.shape
    out = jax.ShapeDtypeStruct((blocks, PAGE, width), bf16)
    smem = pl.BlockSpec(memory_space=pltpu.SMEM)
    vmem = pl.BlockSpec(memory_space=pltpu.VMEM)
    return pl.pallas_call(
        functools.partial(
            relay_kernel, group_slices(width), blocks, lax.axis_size("blk"), offsets
        ),
        in_specs=[smem] * 3 + [vmem] * 5,
        out_specs=[vmem, vmem],
        out_shape=[out, out],
        compiler_params=params(),
        cost_estimate=cost(),
        name="relay_project",
    )(kv_index, here, placement, mine, theirs, wk, wv, gain)


def attend_kernel(inner, live_ref, depth_ref, q_ref, k_ref, v_ref, p0, p1, p2, p3, out):
    pages = (p0, p1, p2, p3)
    tokens, width = q_ref.shape
    live, depth = live_ref[0], depth_ref[0]
    lane = lax.broadcasted_iota(jnp.int32, (1, LANES), 1)
    row = lax.broadcasted_iota(jnp.int32, (PAGE, PAGE), 0)
    col = lax.broadcasted_iota(jnp.int32, (PAGE, PAGE), 1)
    causal = col <= row
    key_row = lax.broadcasted_iota(jnp.int32, (PAGE, LANES), 0)
    blocks = tokens // PAGE
    for start in range(0, width, LANES):
        cols = slice(start, start + LANES)
        page_cols = slice(inner + start, inner + start + LANES)
        keys, values = [], []
        for b in range(blocks):
            rows = slice(b * PAGE, (b + 1) * PAGE)
            keep = (key_row + b * PAGE) < live
            keys.append(k_ref[rows, cols])
            shown = jnp.where(keep, v_ref[rows, cols].astype(f32), 0.0).astype(bf16)
            ones = jnp.where(keep, 1.0, 0.0).astype(bf16)
            values.append(jnp.concatenate([shown, ones], axis=1))
        for p in range(PMAX):
            keep = jnp.where(PAGE_ORDER[p] < depth, 1.0, 0.0).astype(bf16)
            keys.append(pages[p][0, :, page_cols])
            ones = jnp.full((PAGE, LANES), 1.0, bf16) * keep
            values.append(jnp.concatenate([pages[p][1, :, page_cols] * keep, ones], axis=1))
        for b in range(blocks):
            rows = slice(b * PAGE, (b + 1) * PAGE)
            q = q_ref[rows, cols]
            ratios = []
            for side in range(2):
                q_side = jnp.where((lane // HD) == side, q, jnp.zeros_like(q))
                acc = jnp.zeros((PAGE, 2 * LANES), f32)
                for j in list(range(b + 1)) + list(range(blocks, blocks + PMAX)):
                    scores = lax.dot_general(
                        q_side, keys[j], (((1,), (1,)), ((), ())), preferred_element_type=f32
                    )
                    weights = jnp.exp(scores)
                    if j == b:
                        weights = jnp.where(causal, weights, 0.0)
                    acc += jnp.dot(weights.astype(bf16), values[j], preferred_element_type=f32)
                ratios.append(acc[:, :LANES] / acc[:, LANES:])
            out[rows, cols] = jnp.where((lane // HD) == 0, ratios[0], ratios[1]).astype(bf16)


def attend(live, depth, q, k, v, pages, inner):
    tokens, width = q.shape
    heads = width // HD
    smem = pl.BlockSpec(memory_space=pltpu.SMEM)
    vmem = pl.BlockSpec(memory_space=pltpu.VMEM)
    keys = tokens + PMAX * PAGE
    return pl.pallas_call(
        functools.partial(attend_kernel, inner),
        in_specs=[smem, smem] + [vmem] * 7,
        out_specs=vmem,
        out_shape=jax.ShapeDtypeStruct((tokens, width), bf16),
        compiler_params=params(),
        cost_estimate=cost(),
        name="attend",
    )(live, depth, q, k, v, *pages)


def projected_heads(slices, rows, mine, theirs, w_mine, w_theirs):
    def half(parts, weights):
        total = None
        for part, (start, size) in zip(parts, slices):
            weight = weights[start : start + size, :]
            term = jnp.dot(part[rows, :], weight, preferred_element_type=f32)
            total = term if total is None else total + term
        return total

    return half(mine, w_mine) + half(theirs, w_theirs)


def partial_kernel(slices, hidden, rate, w_mine, w_theirs, *refs):
    count = len(slices)
    mine, theirs = refs[:count], refs[count : 2 * count]
    base, out = refs[2 * count :]
    for low in range(0, out.shape[0], PAGE):
        rows = slice(low, low + PAGE)
        out[rows, :] = projected_heads(slices, rows, mine, theirs, w_mine, w_theirs)
        anchor = hidden[rows, :].astype(f32) * row_scale_of(hidden[rows, :])
        base[rows, :] = anchor - rate[...] * anchor


def partial_branch(slices, hidden_in, rate, w_mine, w_theirs, mine, theirs):
    out = jax.ShapeDtypeStruct(hidden_in.shape, f32)
    vmem = pl.BlockSpec(memory_space=pltpu.VMEM)
    return pl.pallas_call(
        functools.partial(partial_kernel, slices),
        in_specs=[vmem] * (4 + 2 * len(slices)),
        out_specs=[vmem] * 2,
        out_shape=[out, out],
        compiler_params=params(),
        cost_estimate=cost(),
        name="partial_branch",
    )(hidden_in, rate, w_mine, w_theirs, *mine, *theirs)


def add_kernel(slices, begun, w_mine, w_theirs, *refs):
    count = len(slices)
    mine, theirs, out = refs[:count], refs[count : 2 * count], refs[2 * count]
    for low in range(0, out.shape[0], PAGE):
        rows = slice(low, low + PAGE)
        term = projected_heads(slices, rows, mine, theirs, w_mine, w_theirs)
        out[rows, :] = begun[rows, :] + term


def add_branch(slices, begun, w_mine, w_theirs, mine, theirs):
    vmem = pl.BlockSpec(memory_space=pltpu.VMEM)
    return pl.pallas_call(
        functools.partial(add_kernel, slices),
        in_specs=[vmem] * (3 + 2 * len(slices)),
        out_specs=vmem,
        out_shape=jax.ShapeDtypeStruct(begun.shape, f32),
        compiler_params=params(),
        cost_estimate=cost(),
        name="add_branch",
    )(begun, w_mine, w_theirs, *mine, *theirs)


def finish_kernel(slices, base, w_mine, w_theirs, rate, begun, *refs):
    count = len(slices)
    mine, theirs = refs[:count], refs[count : 2 * count]
    out, buf, sem = refs[2 * count :]
    step = buf.shape[1]
    copies = []
    for i in range(buf.shape[0]):
        rows = slice(i * step, (i + 1) * step)
        branch = begun[rows, :] + projected_heads(slices, rows, mine, theirs, w_mine, w_theirs)
        mean = jnp.mean(branch * branch, axis=-1, keepdims=True)
        updated = base[rows, :] + rate[...] * (branch * lax.rsqrt(mean + epsilon))
        scale = lax.rsqrt(jnp.mean(updated * updated, axis=-1, keepdims=True) + epsilon)
        buf[i] = (updated * scale).astype(bf16)
        copy = pltpu.make_async_copy(buf.at[i], out.at[pl.ds(i * step, step)], sem.at[i])
        copy.start()
        copies.append(copy)
    for copy in copies:
        copy.wait()


def finish(slices, base, w_mine, w_theirs, rate, begun, mine, theirs):
    tokens, depth = base.shape
    steps = 4
    vmem = pl.BlockSpec(memory_space=pltpu.VMEM)
    return pl.pallas_call(
        functools.partial(finish_kernel, slices),
        in_specs=[vmem] * (5 + 2 * len(slices)),
        out_specs=pl.BlockSpec(memory_space=pltpu.HBM),
        out_shape=jax.ShapeDtypeStruct((tokens, depth), bf16),
        scratch_shapes=[
            pltpu.VMEM((steps, tokens // steps, depth), bf16),
            pltpu.SemaphoreType.DMA((steps,)),
        ],
        compiler_params=params(),
        cost_estimate=cost(),
        name="finish",
    )(base, w_mine, w_theirs, rate, begun, *mine, *theirs)


def body(
    hidden_in,
    w_query,
    w_key,
    w_value,
    w_out,
    head_gain,
    eigen_rate,
    pool_keys,
    pool_values,
    req_len,
    prefix_len,
    prefix_pages,
    placement,
):
    devices = lax.axis_size("blk")
    here = lax.axis_index("blk").astype(jnp.int32).reshape(1)
    kv_index = lax.axis_index("kv").astype(jnp.int32).reshape(1)
    blocks = hidden_in.shape[0] // PAGE
    gain = head_gain.reshape(1, -1)
    rate = eigen_rate.reshape(1, -1)
    page_offsets = [slot * devices // PMAX + 1 for slot in range(PMAX)]
    block_offsets = [(2 * b + 1) * devices // (2 * blocks) for b in range(blocks)]

    assert blocks == lax.axis_size("kv") == 2
    relay_send = split_rows(hidden_in, kv_index)
    page_send = pack(
        pool_keys, pool_values, prefix_pages.T, here, devices, page_offsets, relay_send
    )
    projected = project(hidden_in, w_query, w_key, w_value, gain)

    def fetch(block, slot):
        return over_blk(block, [devices - page_offsets[slot]] * 2)

    relay_mine = over_blk(relay_send, block_offsets)
    ready = projected[0][0]
    first = {slot: fetch(page_send[0][slot], slot) for slot in SLOT_ORDER}
    first[0] = fetch(after(page_send[0][0], ready, relay_mine), 0)
    arrived = [first[slot] for slot in SLOT_ORDER]
    second = {}
    for slot in PAGE_ORDER:
        gate = (ready, relay_mine, *arrived, first[0])
        second[slot] = fetch(after(page_send[1][slot], *gate), slot)
    pages = [[got[slot] for slot in PAGE_ORDER] for got in (first, second)]
    w_theirs = from_behind(w_out, "kv", 1)
    relay_theirs = from_behind(after(relay_mine, w_theirs, *arrived, first[0]), "kv", 1)
    new_keys, new_values = relay_project(
        relay_mine, relay_theirs, w_key, w_value, gain, kv_index, here, placement, block_offsets
    )

    mine, theirs, slices = [[], []], [[], []], [[], []]
    begun = None
    for (g, inner, start, size), (q, k, v) in zip(unit_slices(), projected):
        if g and begun is None:
            base, begun = partial_branch(
                slices[0], hidden_in, rate, w_out, after(w_theirs, new_keys), mine[0], theirs[0]
            )
        if g:
            q = after(q, new_keys, begun)
        attended = attend(req_len, prefix_len, q, k, v, pages[g], inner)
        mine[g].append(attended)
        theirs[g].append(from_behind(attended, "kv", 1))
        slices[g].append((start, size))
    begun = add_branch(slices[1][:-1], begun, w_out, w_theirs, mine[1][:-1], theirs[1][:-1])
    layer_out = finish(
        slices[1][-1:], base, w_out, w_theirs, rate, begun, mine[1][-1:], theirs[1][-1:]
    )
    return (layer_out, new_keys, new_values)


def solution(mesh):
    in_specs = (
        P("blk", None),
        P(None, "kv"),
        P(None, "kv"),
        P(None, "kv"),
        P("kv", None),
        P("kv"),
        P(),
        P("blk", None, "kv"),
        P("blk", None, "kv"),
        P("blk"),
        P("blk"),
        P(),
        P(),
    )
    out_specs = (P("blk", None), P("blk", None, "kv"), P("blk", None, "kv"))
    return jax.shard_map(body, mesh=mesh, in_specs=in_specs, out_specs=out_specs, check_vma=False)
```

```python
import functools
import math

import jax
import jax.numpy as jnp
from jax import lax
from jax.experimental import pallas as pl
from jax.experimental.pallas import tpu as pltpu
from jax.sharding import PartitionSpec as P

HD = 64
PAGE = 256
PMAX = 4
LANES = 128
GROUPS = (256, 384)
UNITS = ((256,), (128, 128, 128))
PARTS = 4
SLOT_ORDER = (2, 1, 3)
PAGE_ORDER = (2, 1, 3, 0)
EARLY = 2
VMEM_LIMIT = 16 * 1024 * 1024
FIRST_LIMIT = 58 * 1024 * 1024

epsilon = 1e-06

f32 = jnp.float32
bf16 = jnp.bfloat16


def from_behind(block, axis, distance):
    devices = range(lax.axis_size(axis))
    route = [((i - distance) % len(devices), i) for i in devices]
    return lax.ppermute(block, axis, route)


def over_blk(block, distances):
    devices = lax.axis_size("blk")
    route = []
    for kv in range(lax.axis_size("kv")):
        for i in range(devices):
            route.append((kv * devices + (i - distances[kv]) % devices, kv * devices + i))
    return lax.ppermute(block, ("kv", "blk"), route)


def after(block, *others):
    return lax.optimization_barrier((block, *others))[0]


def group_slices(width):
    slices, start = [], 0
    for size in GROUPS:
        slices.append((start, size))
        start += size
    assert start == width
    return slices


def unit_slices():
    units, base = [], 0
    for g, sizes in enumerate(UNITS):
        inner = 0
        for size in sizes:
            units.append((g, inner, base + inner, size))
            inner += size
        base += inner
    return units


def params(limit=VMEM_LIMIT):
    return pltpu.CompilerParams(vmem_limit_bytes=limit)


def cost():
    return pl.CostEstimate(flops=1, bytes_accessed=1, transcendentals=0)


def split_kernel(kv_ref, hidden, out, sem):
    part = PAGE // PARTS
    copies = []
    for i in range(PARTS):
        rows = pl.ds(pl.multiple_of(kv_ref[0] * PAGE + i * part, part), part)
        target = out.at[pl.ds(i * part, part)]
        copies.append(pltpu.make_async_copy(hidden.at[rows], target, sem.at[i]))
    for copy in copies:
        copy.start()
    for copy in copies:
        copy.wait()


def split_rows(hidden_in, kv_index):
    return pl.pallas_call(
        split_kernel,
        in_specs=[pl.BlockSpec(memory_space=pltpu.SMEM), pl.BlockSpec(memory_space=pltpu.HBM)],
        out_specs=pl.BlockSpec(memory_space=pltpu.VMEM),
        out_shape=jax.ShapeDtypeStruct((PAGE, hidden_in.shape[1]), bf16),
        scratch_shapes=[pltpu.SemaphoreType.DMA((PARTS,))],
        compiler_params=params(FIRST_LIMIT),
        cost_estimate=cost(),
        name="split_rows",
    )(kv_index, hidden_in)


def pack_kernel(slices, devices, offsets, here_ref, table, keys, values, _, *rest):
    outs, (buf, sem) = rest[:-2], rest[-2:]
    copies = []
    for slot in range(PMAX):
        asker = lax.rem(here_ref[0] + (devices - offsets[slot]), devices)
        local = lax.rem(table[slot, asker], keys.shape[0])
        for side, pool in enumerate((keys, values)):
            index = 2 * slot + side
            copies.append(pltpu.make_async_copy(pool.at[local], buf.at[index], sem.at[index]))
    for copy in copies:
        copy.start()
    for slot in range(PMAX):
        for side in range(2):
            index = 2 * slot + side
            copies[index].wait()
            for g, (start, size) in enumerate(slices):
                outs[g * PMAX + slot][side] = buf[index, :, start : start + size]


def pack(pool_keys, pool_values, table, here, devices, offsets, first):
    width = pool_keys.shape[2]
    slices = group_slices(width)
    outs = []
    for _, size in slices:
        outs += [jax.ShapeDtypeStruct((2, PAGE, size), bf16)] * PMAX
    smem = pl.BlockSpec(memory_space=pltpu.SMEM)
    hbm = pl.BlockSpec(memory_space=pltpu.HBM)
    result = pl.pallas_call(
        functools.partial(pack_kernel, slices, devices, offsets),
        in_specs=[smem, smem, hbm, hbm, pl.BlockSpec(memory_space=pl.ANY)],
        out_specs=[pl.BlockSpec(memory_space=pltpu.VMEM)] * len(outs),
        out_shape=outs,
        scratch_shapes=[
            pltpu.VMEM((2 * PMAX, PAGE, width), bf16),
            pltpu.SemaphoreType.DMA((2 * PMAX,)),
        ],
        compiler_params=params(FIRST_LIMIT),
        cost_estimate=cost(),
        name="pack",
    )(here, table, pool_keys, pool_values, first)
    return [result[PMAX * g : PMAX * (g + 1)] for g in range(len(slices))]


def head_sum_matrix():
    rows = (lax.broadcasted_iota(jnp.int32, (2 * LANES, LANES), 0) % LANES) // HD
    cols = lax.broadcasted_iota(jnp.int32, (2 * LANES, LANES), 1) // HD
    return jnp.where(rows == cols, 1.0 / HD, 0.0).astype(bf16)


def head_norm(projected, gain, matrix):
    parts = []
    for start in range(0, projected.shape[1], LANES):
        part = projected[:, start : start + LANES]
        squares = part * part
        high = squares.astype(bf16)
        low = (squares - high.astype(f32)).astype(bf16)
        both = jnp.concatenate([high, low], axis=1)
        mean = jnp.dot(both, matrix, preferred_element_type=f32)
        parts.append(part * lax.rsqrt(mean + epsilon) * gain[:, start : start + LANES])
    return jnp.concatenate(parts, axis=1) if len(parts) > 1 else parts[0]


def row_scale_of(hidden):
    hidden_f = hidden.astype(f32)
    return lax.rsqrt(jnp.mean(hidden_f * hidden_f, axis=-1, keepdims=True) + epsilon)


def project_kernel(slices, hidden, wq, wk, wv, gain, *outs):
    matrix = head_sum_matrix()
    rows_all = hidden.shape[0]
    for low in range(0, rows_all, PAGE):
        rows = slice(low, low + PAGE)
        x = hidden[rows, :]
        scale = row_scale_of(x)
        for g, (start, size) in enumerate(slices):
            cols = slice(start, start + size)
            q = jnp.dot(x, wq[:, cols], preferred_element_type=f32)
            q = head_norm(q, gain[:, cols], matrix).astype(bf16)
            outs[3 * g][rows, :] = q * jnp.asarray(1.0 / math.sqrt(HD), bf16)
            k = jnp.dot(x, wk[:, cols], preferred_element_type=f32)
            outs[3 * g + 1][rows, :] = head_norm(k, gain[:, cols], matrix).astype(bf16)
            v = jnp.dot(x, wv[:, cols], preferred_element_type=f32)
            outs[3 * g + 2][rows, :] = (v * scale).astype(bf16)


def project(hidden_in, wq, wk, wv, gain):
    tokens, depth = hidden_in.shape
    width = wq.shape[1]
    slices = [(start, size) for _, _, start, size in unit_slices()]
    outs = []
    for _, size in slices:
        outs += [jax.ShapeDtypeStruct((tokens, size), bf16)] * 3
    flat = pl.pallas_call(
        functools.partial(project_kernel, slices),
        out_shape=outs,
        compiler_params=params(),
        cost_estimate=cost(),
        name="project",
    )(hidden_in, wq, wk, wv, gain)
    return [flat[3 * g : 3 * g + 3] for g in range(len(slices))]


def relay_kernel(slices, blocks, devices, offsets, kv_ref, here_ref, placement, *refs):
    mine, theirs, wk, wv, gain, key_out, value_out = refs
    matrix = head_sum_matrix()
    for rows_ref, block in ((mine, kv_ref[0]), (theirs, 1 - kv_ref[0])):
        x = rows_ref[...]
        scale = row_scale_of(x)
        offset = jnp.where(block == 0, offsets[0], offsets[1])
        source = lax.rem(here_ref[0] + (devices - offset), devices)
        slot = lax.rem(placement[source * blocks + block], blocks)
        for start, size in slices:
            cols = slice(start, start + size)
            k = jnp.dot(x, wk[:, cols], preferred_element_type=f32)
            key_out[slot, :, cols] = head_norm(k, gain[:, cols], matrix).astype(bf16)
            v = jnp.dot(x, wv[:, cols], preferred_element_type=f32)
            value_out[slot, :, cols] = (v * scale).astype(bf16)


def relay_project(mine, theirs, wk, wv, gain, kv_index, here, placement, offsets):
    blocks = len(offsets)
    depth, width = wk.shape
    out = jax.ShapeDtypeStruct((blocks, PAGE, width), bf16)
    smem = pl.BlockSpec(memory_space=pltpu.SMEM)
    vmem = pl.BlockSpec(memory_space=pltpu.VMEM)
    return pl.pallas_call(
        functools.partial(
            relay_kernel, group_slices(width), blocks, lax.axis_size("blk"), offsets
        ),
        in_specs=[smem] * 3 + [vmem] * 5,
        out_specs=[vmem, vmem],
        out_shape=[out, out],
        compiler_params=params(),
        cost_estimate=cost(),
        name="relay_project",
    )(kv_index, here, placement, mine, theirs, wk, wv, gain)


def weighted(q, blocks):
    lane = lax.broadcasted_iota(jnp.int32, (1, LANES), 1) // HD
    sums = []
    for side in range(2):
        q_side = jnp.where(lane == side, q, jnp.zeros_like(q))
        acc = jnp.zeros((q.shape[0], 2 * LANES), f32)
        for keys, values, visible in blocks:
            scores = lax.dot_general(
                q_side, keys, (((1,), (1,)), ((), ())), preferred_element_type=f32
            )
            weights = jnp.exp(scores)
            if visible is not None:
                weights = jnp.where(visible, weights, 0.0)
            acc += jnp.dot(weights.astype(bf16), values, preferred_element_type=f32)
        sums.append(acc)
    mixed = jnp.where(lane == 0, sums[0][:, :LANES], sums[1][:, :LANES])
    totals = jnp.where(lane == 0, sums[0][:, LANES:], sums[1][:, LANES:])
    return mixed, totals


def own_blocks(k_ref, v_ref, live, cols):
    row = lax.broadcasted_iota(jnp.int32, (PAGE, PAGE), 0)
    col = lax.broadcasted_iota(jnp.int32, (PAGE, PAGE), 1)
    key_row = lax.broadcasted_iota(jnp.int32, (PAGE, LANES), 0)
    blocks = []
    for b in range(k_ref.shape[0] // PAGE):
        rows = slice(b * PAGE, (b + 1) * PAGE)
        keep = (key_row + b * PAGE) < live
        shown = jnp.where(keep, v_ref[rows, cols].astype(f32), 0.0).astype(bf16)
        ones = jnp.where(keep, 1.0, 0.0).astype(bf16)
        blocks.append((k_ref[rows, cols], jnp.concatenate([shown, ones], axis=1)))
    return blocks, col <= row


def page_blocks(pages, slots, depth, cols):
    blocks = []
    for page, slot in zip(pages, slots):
        keep = jnp.where(slot < depth, 1.0, 0.0).astype(bf16)
        ones = jnp.full((PAGE, LANES), 1.0, bf16) * keep
        values = jnp.concatenate([page[1, :, cols] * keep, ones], axis=1)
        blocks.append((page[0, :, cols], values, None))
    return blocks


def attend_kernel(inner, slots, live_ref, depth_ref, q_ref, k_ref, v_ref, *refs):
    pages, outs = refs[: len(slots)], refs[len(slots) :]
    tokens, width = q_ref.shape
    for start in range(0, width, LANES):
        cols = slice(start, start + LANES)
        own, causal = own_blocks(k_ref, v_ref, live_ref[0], cols)
        page_cols = slice(inner + start, inner + start + LANES)
        cached = page_blocks(pages, slots, depth_ref[0], page_cols)
        for b in range(tokens // PAGE):
            rows = slice(b * PAGE, (b + 1) * PAGE)
            blocks = [own[j] + (causal if j == b else None,) for j in range(b + 1)]
            mixed, totals = weighted(q_ref[rows, cols], blocks + cached)
            if len(outs) == 1:
                outs[0][rows, cols] = (mixed / totals).astype(bf16)
            else:
                outs[0][rows, cols] = mixed
                outs[1][rows, cols] = totals


def attend(live, depth, q, k, v, pages, slots, inner):
    smem = pl.BlockSpec(memory_space=pltpu.SMEM)
    vmem = pl.BlockSpec(memory_space=pltpu.VMEM)
    if len(slots) == PMAX:
        out = [jax.ShapeDtypeStruct(q.shape, bf16)]
    else:
        out = [jax.ShapeDtypeStruct(q.shape, f32)] * 2
    result = pl.pallas_call(
        functools.partial(attend_kernel, inner, slots),
        in_specs=[smem, smem] + [vmem] * (3 + len(slots)),
        out_specs=[vmem] * len(out),
        out_shape=out,
        compiler_params=params(),
        cost_estimate=cost(),
        name="attend",
    )(live, depth, q, k, v, *pages)
    return result[0] if len(out) == 1 else result


def attend_rest_kernel(inner, slots, depth_ref, q_ref, mixed_ref, totals_ref, *refs):
    pages, out = refs[: len(slots)], refs[len(slots)]
    tokens, width = q_ref.shape
    for start in range(0, width, LANES):
        cols = slice(start, start + LANES)
        page_cols = slice(inner + start, inner + start + LANES)
        cached = page_blocks(pages, slots, depth_ref[0], page_cols)
        for b in range(tokens // PAGE):
            rows = slice(b * PAGE, (b + 1) * PAGE)
            mixed, totals = weighted(q_ref[rows, cols], cached)
            mixed += mixed_ref[rows, cols]
            totals += totals_ref[rows, cols]
            out[rows, cols] = (mixed / totals).astype(bf16)


def attend_rest(depth, q, mixed, totals, pages, slots, inner):
    smem = pl.BlockSpec(memory_space=pltpu.SMEM)
    vmem = pl.BlockSpec(memory_space=pltpu.VMEM)
    return pl.pallas_call(
        functools.partial(attend_rest_kernel, inner, slots),
        in_specs=[smem] + [vmem] * (3 + len(slots)),
        out_specs=vmem,
        out_shape=jax.ShapeDtypeStruct(q.shape, bf16),
        compiler_params=params(),
        cost_estimate=cost(),
        name="attend_rest",
    )(depth, q, mixed, totals, *pages)


def projected_heads(slices, rows, mine, theirs, w_mine, w_theirs):
    def half(parts, weights):
        total = None
        for part, (start, size) in zip(parts, slices):
            weight = weights[start : start + size, :]
            term = jnp.dot(part[rows, :], weight, preferred_element_type=f32)
            total = term if total is None else total + term
        return total

    return half(mine, w_mine) + half(theirs, w_theirs)


def partial_kernel(slices, hidden, rate, w_mine, w_theirs, *refs):
    count = len(slices)
    mine, theirs = refs[:count], refs[count : 2 * count]
    base, out = refs[2 * count :]
    for low in range(0, out.shape[0], PAGE):
        rows = slice(low, low + PAGE)
        out[rows, :] = projected_heads(slices, rows, mine, theirs, w_mine, w_theirs)
        anchor = hidden[rows, :].astype(f32) * row_scale_of(hidden[rows, :])
        base[rows, :] = anchor - rate[...] * anchor


def partial_branch(slices, hidden_in, rate, w_mine, w_theirs, mine, theirs):
    out = jax.ShapeDtypeStruct(hidden_in.shape, f32)
    vmem = pl.BlockSpec(memory_space=pltpu.VMEM)
    return pl.pallas_call(
        functools.partial(partial_kernel, slices),
        in_specs=[vmem] * (4 + 2 * len(slices)),
        out_specs=[vmem] * 2,
        out_shape=[out, out],
        compiler_params=params(),
        cost_estimate=cost(),
        name="partial_branch",
    )(hidden_in, rate, w_mine, w_theirs, *mine, *theirs)


def add_kernel(slices, begun, w_mine, w_theirs, *refs):
    count = len(slices)
    mine, theirs, out = refs[:count], refs[count : 2 * count], refs[2 * count]
    for low in range(0, out.shape[0], PAGE):
        rows = slice(low, low + PAGE)
        term = projected_heads(slices, rows, mine, theirs, w_mine, w_theirs)
        out[rows, :] = begun[rows, :] + term


def add_branch(slices, begun, w_mine, w_theirs, mine, theirs):
    vmem = pl.BlockSpec(memory_space=pltpu.VMEM)
    return pl.pallas_call(
        functools.partial(add_kernel, slices),
        in_specs=[vmem] * (3 + 2 * len(slices)),
        out_specs=vmem,
        out_shape=jax.ShapeDtypeStruct(begun.shape, f32),
        compiler_params=params(),
        cost_estimate=cost(),
        name="add_branch",
    )(begun, w_mine, w_theirs, *mine, *theirs)


def finish_kernel(slices, base, w_mine, w_theirs, rate, begun, *refs):
    count = len(slices)
    mine, theirs = refs[:count], refs[count : 2 * count]
    out, buf, sem = refs[2 * count :]
    step = buf.shape[1]
    copies = []
    for i in range(buf.shape[0]):
        rows = slice(i * step, (i + 1) * step)
        branch = begun[rows, :] + projected_heads(slices, rows, mine, theirs, w_mine, w_theirs)
        mean = jnp.mean(branch * branch, axis=-1, keepdims=True)
        updated = base[rows, :] + rate[...] * (branch * lax.rsqrt(mean + epsilon))
        scale = lax.rsqrt(jnp.mean(updated * updated, axis=-1, keepdims=True) + epsilon)
        buf[i] = (updated * scale).astype(bf16)
        copy = pltpu.make_async_copy(buf.at[i], out.at[pl.ds(i * step, step)], sem.at[i])
        copy.start()
        copies.append(copy)
    for copy in copies:
        copy.wait()


def finish(slices, base, w_mine, w_theirs, rate, begun, mine, theirs):
    tokens, depth = base.shape
    steps = 4
    vmem = pl.BlockSpec(memory_space=pltpu.VMEM)
    return pl.pallas_call(
        functools.partial(finish_kernel, slices),
        in_specs=[vmem] * (5 + 2 * len(slices)),
        out_specs=pl.BlockSpec(memory_space=pltpu.HBM),
        out_shape=jax.ShapeDtypeStruct((tokens, depth), bf16),
        scratch_shapes=[
            pltpu.VMEM((steps, tokens // steps, depth), bf16),
            pltpu.SemaphoreType.DMA((steps,)),
        ],
        compiler_params=params(),
        cost_estimate=cost(),
        name="finish",
    )(base, w_mine, w_theirs, rate, begun, *mine, *theirs)


def body(
    hidden_in,
    w_query,
    w_key,
    w_value,
    w_out,
    head_gain,
    eigen_rate,
    pool_keys,
    pool_values,
    req_len,
    prefix_len,
    prefix_pages,
    placement,
):
    devices = lax.axis_size("blk")
    here = lax.axis_index("blk").astype(jnp.int32).reshape(1)
    kv_index = lax.axis_index("kv").astype(jnp.int32).reshape(1)
    blocks = hidden_in.shape[0] // PAGE
    gain = head_gain.reshape(1, -1)
    rate = eigen_rate.reshape(1, -1)
    page_offsets = [slot * devices // PMAX + 1 for slot in range(PMAX)]
    block_offsets = [(2 * b + 1) * devices // (2 * blocks) for b in range(blocks)]

    assert blocks == lax.axis_size("kv") == 2
    relay_send = split_rows(hidden_in, kv_index)
    page_send = pack(
        pool_keys, pool_values, prefix_pages.T, here, devices, page_offsets, relay_send
    )
    projected = project(hidden_in, w_query, w_key, w_value, gain)

    def fetch(block, slot):
        return over_blk(block, [devices - page_offsets[slot]] * 2)

    relay_mine = over_blk(relay_send, block_offsets)
    ready = projected[0][0]
    first = {slot: fetch(page_send[0][slot], slot) for slot in SLOT_ORDER}
    first[0] = fetch(after(page_send[0][0], ready, relay_mine), 0)
    arrived = [first[slot] for slot in SLOT_ORDER]
    second = {}
    for slot in PAGE_ORDER:
        gate = (ready, relay_mine, *arrived, first[0])
        second[slot] = fetch(after(page_send[1][slot], *gate), slot)
    pages = [[got[slot] for slot in PAGE_ORDER] for got in (first, second)]
    w_theirs = from_behind(w_out, "kv", 1)
    relay_theirs = from_behind(after(relay_mine, w_theirs, *arrived, first[0]), "kv", 1)
    new_keys, new_values = relay_project(
        relay_mine, relay_theirs, w_key, w_value, gain, kv_index, here, placement, block_offsets
    )

    mine, theirs, slices = [[], []], [[], []], [[], []]
    units = list(zip(unit_slices(), projected))

    def swap(g, start, size, attended):
        mine[g].append(attended)
        theirs[g].append(from_behind(attended, "kv", 1))
        slices[g].append((start, size))

    for (g, inner, start, size), (q, k, v) in units:
        if g == 0:
            swap(g, start, size, attend(req_len, prefix_len, q, k, v, pages[0], PAGE_ORDER, inner))
    base, begun = partial_branch(
        slices[0], hidden_in, rate, w_out, after(w_theirs, new_keys), mine[0], theirs[0]
    )
    early, late = PAGE_ORDER[:EARLY], PAGE_ORDER[EARLY:]
    sums = []
    for (g, inner, _, _), (q, k, v) in units:
        if g:
            q = after(q, new_keys, begun)
            sums.append(attend(req_len, prefix_len, q, k, v, pages[g][:EARLY], early, inner))
    rest = [unit for unit in units if unit[0][0]]
    for ((g, inner, start, size), (q, _, _)), (mixed, totals) in zip(rest, sums):
        q = after(q, *[total for _, total in sums])
        swap(g, start, size, attend_rest(prefix_len, q, mixed, totals, pages[g][EARLY:], late, inner))
    begun = add_branch(slices[1][:-1], begun, w_out, w_theirs, mine[1][:-1], theirs[1][:-1])
    layer_out = finish(
        slices[1][-1:], base, w_out, w_theirs, rate, begun, mine[1][-1:], theirs[1][-1:]
    )
    return (layer_out, new_keys, new_values)


def solution(mesh):
    in_specs = (
        P("blk", None),
        P(None, "kv"),
        P(None, "kv"),
        P(None, "kv"),
        P("kv", None),
        P("kv"),
        P(),
        P("blk", None, "kv"),
        P("blk", None, "kv"),
        P("blk"),
        P("blk"),
        P(),
        P(),
    )
    out_specs = (P("blk", None), P("blk", None, "kv"), P("blk", None, "kv"))
    return jax.shard_map(body, mesh=mesh, in_specs=in_specs, out_specs=out_specs, check_vma=False)
```

```python
import functools
import math

import jax
import jax.numpy as jnp
from jax import lax
from jax.experimental import pallas as pl
from jax.experimental.pallas import tpu as pltpu
from jax.sharding import PartitionSpec as P

HD = 64
PAGE = 256
PMAX = 4
LANES = 128
GROUPS = (256, 384)
UNITS = ((256,), (128, 128, 128))
PARTS = 4
SLOT_ORDER = (2, 1, 3)
PAGE_ORDER = (2, 1, 3, 0)
EARLY = 1
VMEM_LIMIT = 16 * 1024 * 1024
FIRST_LIMIT = 58 * 1024 * 1024

epsilon = 1e-06

f32 = jnp.float32
bf16 = jnp.bfloat16


def from_behind(block, axis, distance):
    devices = range(lax.axis_size(axis))
    route = [((i - distance) % len(devices), i) for i in devices]
    return lax.ppermute(block, axis, route)


def over_blk(block, distances):
    devices = lax.axis_size("blk")
    route = []
    for kv in range(lax.axis_size("kv")):
        for i in range(devices):
            route.append((kv * devices + (i - distances[kv]) % devices, kv * devices + i))
    return lax.ppermute(block, ("kv", "blk"), route)


def after(block, *others):
    return lax.optimization_barrier((block, *others))[0]


def group_slices(width):
    slices, start = [], 0
    for size in GROUPS:
        slices.append((start, size))
        start += size
    assert start == width
    return slices


def unit_slices():
    units, base = [], 0
    for g, sizes in enumerate(UNITS):
        inner = 0
        for size in sizes:
            units.append((g, inner, base + inner, size))
            inner += size
        base += inner
    return units


def params(limit=VMEM_LIMIT):
    return pltpu.CompilerParams(vmem_limit_bytes=limit)


def cost():
    return pl.CostEstimate(flops=1, bytes_accessed=1, transcendentals=0)


def split_kernel(kv_ref, hidden, out, sem):
    part = PAGE // PARTS
    copies = []
    for i in range(PARTS):
        rows = pl.ds(pl.multiple_of(kv_ref[0] * PAGE + i * part, part), part)
        target = out.at[pl.ds(i * part, part)]
        copies.append(pltpu.make_async_copy(hidden.at[rows], target, sem.at[i]))
    for copy in copies:
        copy.start()
    for copy in copies:
        copy.wait()


def split_rows(hidden_in, kv_index):
    return pl.pallas_call(
        split_kernel,
        in_specs=[pl.BlockSpec(memory_space=pltpu.SMEM), pl.BlockSpec(memory_space=pltpu.HBM)],
        out_specs=pl.BlockSpec(memory_space=pltpu.VMEM),
        out_shape=jax.ShapeDtypeStruct((PAGE, hidden_in.shape[1]), bf16),
        scratch_shapes=[pltpu.SemaphoreType.DMA((PARTS,))],
        compiler_params=params(FIRST_LIMIT),
        cost_estimate=cost(),
        name="split_rows",
    )(kv_index, hidden_in)


def pack_kernel(slices, devices, offsets, here_ref, table, keys, values, _, *rest):
    outs, (buf, sem) = rest[:-2], rest[-2:]
    copies = []
    for slot in range(PMAX):
        asker = lax.rem(here_ref[0] + (devices - offsets[slot]), devices)
        local = lax.rem(table[slot, asker], keys.shape[0])
        for side, pool in enumerate((keys, values)):
            index = 2 * slot + side
            copies.append(pltpu.make_async_copy(pool.at[local], buf.at[index], sem.at[index]))
    for copy in copies:
        copy.start()
    for slot in range(PMAX):
        for side in range(2):
            index = 2 * slot + side
            copies[index].wait()
            for g, (start, size) in enumerate(slices):
                outs[g * PMAX + slot][side] = buf[index, :, start : start + size]


def pack(pool_keys, pool_values, table, here, devices, offsets, first):
    width = pool_keys.shape[2]
    slices = group_slices(width)
    outs = []
    for _, size in slices:
        outs += [jax.ShapeDtypeStruct((2, PAGE, size), bf16)] * PMAX
    smem = pl.BlockSpec(memory_space=pltpu.SMEM)
    hbm = pl.BlockSpec(memory_space=pltpu.HBM)
    result = pl.pallas_call(
        functools.partial(pack_kernel, slices, devices, offsets),
        in_specs=[smem, smem, hbm, hbm, pl.BlockSpec(memory_space=pl.ANY)],
        out_specs=[pl.BlockSpec(memory_space=pltpu.VMEM)] * len(outs),
        out_shape=outs,
        scratch_shapes=[
            pltpu.VMEM((2 * PMAX, PAGE, width), bf16),
            pltpu.SemaphoreType.DMA((2 * PMAX,)),
        ],
        compiler_params=params(FIRST_LIMIT),
        cost_estimate=cost(),
        name="pack",
    )(here, table, pool_keys, pool_values, first)
    return [result[PMAX * g : PMAX * (g + 1)] for g in range(len(slices))]


def head_sum_matrix():
    rows = (lax.broadcasted_iota(jnp.int32, (2 * LANES, LANES), 0) % LANES) // HD
    cols = lax.broadcasted_iota(jnp.int32, (2 * LANES, LANES), 1) // HD
    return jnp.where(rows == cols, 1.0 / HD, 0.0).astype(bf16)


def head_norm(projected, gain, matrix):
    parts = []
    for start in range(0, projected.shape[1], LANES):
        part = projected[:, start : start + LANES]
        squares = part * part
        high = squares.astype(bf16)
        low = (squares - high.astype(f32)).astype(bf16)
        both = jnp.concatenate([high, low], axis=1)
        mean = jnp.dot(both, matrix, preferred_element_type=f32)
        parts.append(part * lax.rsqrt(mean + epsilon) * gain[:, start : start + LANES])
    return jnp.concatenate(parts, axis=1) if len(parts) > 1 else parts[0]


def row_scale_of(hidden):
    hidden_f = hidden.astype(f32)
    return lax.rsqrt(jnp.mean(hidden_f * hidden_f, axis=-1, keepdims=True) + epsilon)


def project_kernel(slices, hidden, wq, wk, wv, gain, *outs):
    matrix = head_sum_matrix()
    rows_all = hidden.shape[0]
    for low in range(0, rows_all, PAGE):
        rows = slice(low, low + PAGE)
        x = hidden[rows, :]
        scale = row_scale_of(x)
        for g, (start, size) in enumerate(slices):
            cols = slice(start, start + size)
            q = jnp.dot(x, wq[:, cols], preferred_element_type=f32)
            q = head_norm(q, gain[:, cols], matrix).astype(bf16)
            outs[3 * g][rows, :] = q * jnp.asarray(1.0 / math.sqrt(HD), bf16)
            k = jnp.dot(x, wk[:, cols], preferred_element_type=f32)
            outs[3 * g + 1][rows, :] = head_norm(k, gain[:, cols], matrix).astype(bf16)
            v = jnp.dot(x, wv[:, cols], preferred_element_type=f32)
            outs[3 * g + 2][rows, :] = (v * scale).astype(bf16)


def project(hidden_in, wq, wk, wv, gain):
    tokens, depth = hidden_in.shape
    width = wq.shape[1]
    slices = [(start, size) for _, _, start, size in unit_slices()]
    outs = []
    for _, size in slices:
        outs += [jax.ShapeDtypeStruct((tokens, size), bf16)] * 3
    flat = pl.pallas_call(
        functools.partial(project_kernel, slices),
        out_shape=outs,
        compiler_params=params(),
        cost_estimate=cost(),
        name="project",
    )(hidden_in, wq, wk, wv, gain)
    return [flat[3 * g : 3 * g + 3] for g in range(len(slices))]


def relay_kernel(slices, blocks, devices, offsets, kv_ref, here_ref, placement, *refs):
    mine, theirs, wk, wv, gain, key_out, value_out = refs
    matrix = head_sum_matrix()
    for rows_ref, block in ((mine, kv_ref[0]), (theirs, 1 - kv_ref[0])):
        x = rows_ref[...]
        scale = row_scale_of(x)
        offset = jnp.where(block == 0, offsets[0], offsets[1])
        source = lax.rem(here_ref[0] + (devices - offset), devices)
        slot = lax.rem(placement[source * blocks + block], blocks)
        for start, size in slices:
            cols = slice(start, start + size)
            k = jnp.dot(x, wk[:, cols], preferred_element_type=f32)
            key_out[slot, :, cols] = head_norm(k, gain[:, cols], matrix).astype(bf16)
            v = jnp.dot(x, wv[:, cols], preferred_element_type=f32)
            value_out[slot, :, cols] = (v * scale).astype(bf16)


def relay_project(mine, theirs, wk, wv, gain, kv_index, here, placement, offsets):
    blocks = len(offsets)
    depth, width = wk.shape
    out = jax.ShapeDtypeStruct((blocks, PAGE, width), bf16)
    smem = pl.BlockSpec(memory_space=pltpu.SMEM)
    vmem = pl.BlockSpec(memory_space=pltpu.VMEM)
    return pl.pallas_call(
        functools.partial(
            relay_kernel, group_slices(width), blocks, lax.axis_size("blk"), offsets
        ),
        in_specs=[smem] * 3 + [vmem] * 5,
        out_specs=[vmem, vmem],
        out_shape=[out, out],
        compiler_params=params(),
        cost_estimate=cost(),
        name="relay_project",
    )(kv_index, here, placement, mine, theirs, wk, wv, gain)


def weighted(q, blocks):
    lane = lax.broadcasted_iota(jnp.int32, (1, LANES), 1) // HD
    sums = []
    for side in range(2):
        q_side = jnp.where(lane == side, q, jnp.zeros_like(q))
        acc = jnp.zeros((q.shape[0], 2 * LANES), f32)
        for keys, values, visible in blocks:
            scores = lax.dot_general(
                q_side, keys, (((1,), (1,)), ((), ())), preferred_element_type=f32
            )
            weights = jnp.exp(scores)
            if visible is not None:
                weights = jnp.where(visible, weights, 0.0)
            acc += jnp.dot(weights.astype(bf16), values, preferred_element_type=f32)
        sums.append(acc)
    mixed = jnp.where(lane == 0, sums[0][:, :LANES], sums[1][:, :LANES])
    totals = jnp.where(lane == 0, sums[0][:, LANES:], sums[1][:, LANES:])
    return mixed, totals


def own_blocks(k_ref, v_ref, live, cols):
    row = lax.broadcasted_iota(jnp.int32, (PAGE, PAGE), 0)
    col = lax.broadcasted_iota(jnp.int32, (PAGE, PAGE), 1)
    key_row = lax.broadcasted_iota(jnp.int32, (PAGE, LANES), 0)
    blocks = []
    for b in range(k_ref.shape[0] // PAGE):
        rows = slice(b * PAGE, (b + 1) * PAGE)
        keep = (key_row + b * PAGE) < live
        shown = jnp.where(keep, v_ref[rows, cols].astype(f32), 0.0).astype(bf16)
        ones = jnp.where(keep, 1.0, 0.0).astype(bf16)
        blocks.append((k_ref[rows, cols], jnp.concatenate([shown, ones], axis=1)))
    return blocks, col <= row


def page_blocks(pages, slots, depth, cols):
    blocks = []
    for page, slot in zip(pages, slots):
        keep = jnp.where(slot < depth, 1.0, 0.0).astype(bf16)
        ones = jnp.full((PAGE, LANES), 1.0, bf16) * keep
        values = jnp.concatenate([page[1, :, cols] * keep, ones], axis=1)
        blocks.append((page[0, :, cols], values, None))
    return blocks


def attend_kernel(inner, slots, live_ref, depth_ref, q_ref, k_ref, v_ref, *refs):
    pages, outs = refs[: len(slots)], refs[len(slots) :]
    tokens, width = q_ref.shape
    for start in range(0, width, LANES):
        cols = slice(start, start + LANES)
        own, causal = own_blocks(k_ref, v_ref, live_ref[0], cols)
        page_cols = slice(inner + start, inner + start + LANES)
        cached = page_blocks(pages, slots, depth_ref[0], page_cols)
        for b in range(tokens // PAGE):
            rows = slice(b * PAGE, (b + 1) * PAGE)
            blocks = [own[j] + (causal if j == b else None,) for j in range(b + 1)]
            mixed, totals = weighted(q_ref[rows, cols], blocks + cached)
            if len(outs) == 1:
                outs[0][rows, cols] = (mixed / totals).astype(bf16)
            else:
                outs[0][rows, cols] = mixed
                outs[1][rows, cols] = totals


def attend(live, depth, q, k, v, pages, slots, inner):
    smem = pl.BlockSpec(memory_space=pltpu.SMEM)
    vmem = pl.BlockSpec(memory_space=pltpu.VMEM)
    if len(slots) == PMAX:
        out = [jax.ShapeDtypeStruct(q.shape, bf16)]
    else:
        out = [jax.ShapeDtypeStruct(q.shape, f32)] * 2
    result = pl.pallas_call(
        functools.partial(attend_kernel, inner, slots),
        in_specs=[smem, smem] + [vmem] * (3 + len(slots)),
        out_specs=[vmem] * len(out),
        out_shape=out,
        compiler_params=params(),
        cost_estimate=cost(),
        name="attend",
    )(live, depth, q, k, v, *pages)
    return result[0] if len(out) == 1 else result


def attend_rest_kernel(inner, slots, depth_ref, q_ref, mixed_ref, totals_ref, *refs):
    pages, out = refs[: len(slots)], refs[len(slots)]
    tokens, width = q_ref.shape
    for start in range(0, width, LANES):
        cols = slice(start, start + LANES)
        page_cols = slice(inner + start, inner + start + LANES)
        cached = page_blocks(pages, slots, depth_ref[0], page_cols)
        for b in range(tokens // PAGE):
            rows = slice(b * PAGE, (b + 1) * PAGE)
            mixed, totals = weighted(q_ref[rows, cols], cached)
            mixed += mixed_ref[rows, cols]
            totals += totals_ref[rows, cols]
            out[rows, cols] = (mixed / totals).astype(bf16)


def attend_rest(depth, q, mixed, totals, pages, slots, inner):
    smem = pl.BlockSpec(memory_space=pltpu.SMEM)
    vmem = pl.BlockSpec(memory_space=pltpu.VMEM)
    return pl.pallas_call(
        functools.partial(attend_rest_kernel, inner, slots),
        in_specs=[smem] + [vmem] * (3 + len(slots)),
        out_specs=vmem,
        out_shape=jax.ShapeDtypeStruct(q.shape, bf16),
        compiler_params=params(),
        cost_estimate=cost(),
        name="attend_rest",
    )(depth, q, mixed, totals, *pages)


def projected_heads(slices, rows, mine, theirs, w_mine, w_theirs):
    def half(parts, weights):
        total = None
        for part, (start, size) in zip(parts, slices):
            weight = weights[start : start + size, :]
            term = jnp.dot(part[rows, :], weight, preferred_element_type=f32)
            total = term if total is None else total + term
        return total

    return half(mine, w_mine) + half(theirs, w_theirs)


def partial_kernel(slices, hidden, rate, w_mine, w_theirs, *refs):
    count = len(slices)
    mine, theirs = refs[:count], refs[count : 2 * count]
    base, out = refs[2 * count :]
    for low in range(0, out.shape[0], PAGE):
        rows = slice(low, low + PAGE)
        out[rows, :] = projected_heads(slices, rows, mine, theirs, w_mine, w_theirs)
        anchor = hidden[rows, :].astype(f32) * row_scale_of(hidden[rows, :])
        base[rows, :] = anchor - rate[...] * anchor


def partial_branch(slices, hidden_in, rate, w_mine, w_theirs, mine, theirs):
    out = jax.ShapeDtypeStruct(hidden_in.shape, f32)
    vmem = pl.BlockSpec(memory_space=pltpu.VMEM)
    return pl.pallas_call(
        functools.partial(partial_kernel, slices),
        in_specs=[vmem] * (4 + 2 * len(slices)),
        out_specs=[vmem] * 2,
        out_shape=[out, out],
        compiler_params=params(),
        cost_estimate=cost(),
        name="partial_branch",
    )(hidden_in, rate, w_mine, w_theirs, *mine, *theirs)


def add_kernel(slices, begun, w_mine, w_theirs, *refs):
    count = len(slices)
    mine, theirs, out = refs[:count], refs[count : 2 * count], refs[2 * count]
    for low in range(0, out.shape[0], PAGE):
        rows = slice(low, low + PAGE)
        term = projected_heads(slices, rows, mine, theirs, w_mine, w_theirs)
        out[rows, :] = begun[rows, :] + term


def add_branch(slices, begun, w_mine, w_theirs, mine, theirs):
    vmem = pl.BlockSpec(memory_space=pltpu.VMEM)
    return pl.pallas_call(
        functools.partial(add_kernel, slices),
        in_specs=[vmem] * (3 + 2 * len(slices)),
        out_specs=vmem,
        out_shape=jax.ShapeDtypeStruct(begun.shape, f32),
        compiler_params=params(),
        cost_estimate=cost(),
        name="add_branch",
    )(begun, w_mine, w_theirs, *mine, *theirs)


def finish_kernel(slices, base, w_mine, w_theirs, rate, begun, *refs):
    count = len(slices)
    mine, theirs = refs[:count], refs[count : 2 * count]
    out, buf, sem = refs[2 * count :]
    step = buf.shape[1]
    copies = []
    for i in range(buf.shape[0]):
        rows = slice(i * step, (i + 1) * step)
        branch = begun[rows, :] + projected_heads(slices, rows, mine, theirs, w_mine, w_theirs)
        mean = jnp.mean(branch * branch, axis=-1, keepdims=True)
        updated = base[rows, :] + rate[...] * (branch * lax.rsqrt(mean + epsilon))
        scale = lax.rsqrt(jnp.mean(updated * updated, axis=-1, keepdims=True) + epsilon)
        buf[i] = (updated * scale).astype(bf16)
        copy = pltpu.make_async_copy(buf.at[i], out.at[pl.ds(i * step, step)], sem.at[i])
        copy.start()
        copies.append(copy)
    for copy in copies:
        copy.wait()


def finish(slices, base, w_mine, w_theirs, rate, begun, mine, theirs):
    tokens, depth = base.shape
    steps = 4
    vmem = pl.BlockSpec(memory_space=pltpu.VMEM)
    return pl.pallas_call(
        functools.partial(finish_kernel, slices),
        in_specs=[vmem] * (5 + 2 * len(slices)),
        out_specs=pl.BlockSpec(memory_space=pltpu.HBM),
        out_shape=jax.ShapeDtypeStruct((tokens, depth), bf16),
        scratch_shapes=[
            pltpu.VMEM((steps, tokens // steps, depth), bf16),
            pltpu.SemaphoreType.DMA((steps,)),
        ],
        compiler_params=params(),
        cost_estimate=cost(),
        name="finish",
    )(base, w_mine, w_theirs, rate, begun, *mine, *theirs)


def body(
    hidden_in,
    w_query,
    w_key,
    w_value,
    w_out,
    head_gain,
    eigen_rate,
    pool_keys,
    pool_values,
    req_len,
    prefix_len,
    prefix_pages,
    placement,
):
    devices = lax.axis_size("blk")
    here = lax.axis_index("blk").astype(jnp.int32).reshape(1)
    kv_index = lax.axis_index("kv").astype(jnp.int32).reshape(1)
    blocks = hidden_in.shape[0] // PAGE
    gain = head_gain.reshape(1, -1)
    rate = eigen_rate.reshape(1, -1)
    page_offsets = [slot * devices // PMAX + 1 for slot in range(PMAX)]
    block_offsets = [(2 * b + 1) * devices // (2 * blocks) for b in range(blocks)]

    assert blocks == lax.axis_size("kv") == 2
    relay_send = split_rows(hidden_in, kv_index)
    page_send = pack(
        pool_keys, pool_values, prefix_pages.T, here, devices, page_offsets, relay_send
    )
    projected = project(hidden_in, w_query, w_key, w_value, gain)

    def fetch(block, slot):
        return over_blk(block, [devices - page_offsets[slot]] * 2)

    relay_mine = over_blk(relay_send, block_offsets)
    ready = projected[0][0]
    first = {slot: fetch(page_send[0][slot], slot) for slot in SLOT_ORDER}
    first[0] = fetch(after(page_send[0][0], ready, relay_mine), 0)
    arrived = [first[slot] for slot in SLOT_ORDER]
    second = {}
    for slot in PAGE_ORDER:
        gate = (ready, relay_mine, *arrived, first[0])
        second[slot] = fetch(after(page_send[1][slot], *gate), slot)
    pages = [[got[slot] for slot in PAGE_ORDER] for got in (first, second)]
    w_theirs = from_behind(w_out, "kv", 1)
    relay_theirs = from_behind(after(relay_mine, w_theirs, *arrived, first[0]), "kv", 1)
    new_keys, new_values = relay_project(
        relay_mine, relay_theirs, w_key, w_value, gain, kv_index, here, placement, block_offsets
    )

    mine, theirs, slices = [[], []], [[], []], [[], []]
    units = list(zip(unit_slices(), projected))

    def swap(g, start, size, attended):
        mine[g].append(attended)
        theirs[g].append(from_behind(attended, "kv", 1))
        slices[g].append((start, size))

    for (g, inner, start, size), (q, k, v) in units:
        if g == 0:
            swap(g, start, size, attend(req_len, prefix_len, q, k, v, pages[0], PAGE_ORDER, inner))
    base, begun = partial_branch(
        slices[0], hidden_in, rate, w_out, after(w_theirs, new_keys), mine[0], theirs[0]
    )
    early, late = PAGE_ORDER[:EARLY], PAGE_ORDER[EARLY:]
    sums = []
    for (g, inner, _, _), (q, k, v) in units:
        if g:
            q = after(q, new_keys, begun)
            sums.append(attend(req_len, prefix_len, q, k, v, pages[g][:EARLY], early, inner))
    rest = [unit for unit in units if unit[0][0]]
    for ((g, inner, start, size), (q, _, _)), (mixed, totals) in zip(rest, sums):
        q = after(q, *[total for _, total in sums])
        swap(g, start, size, attend_rest(prefix_len, q, mixed, totals, pages[g][EARLY:], late, inner))
    begun = add_branch(slices[1][:-1], begun, w_out, w_theirs, mine[1][:-1], theirs[1][:-1])
    layer_out = finish(
        slices[1][-1:], base, w_out, w_theirs, rate, begun, mine[1][-1:], theirs[1][-1:]
    )
    return (layer_out, new_keys, new_values)


def solution(mesh):
    in_specs = (
        P("blk", None),
        P(None, "kv"),
        P(None, "kv"),
        P(None, "kv"),
        P("kv", None),
        P("kv"),
        P(),
        P("blk", None, "kv"),
        P("blk", None, "kv"),
        P("blk"),
        P("blk"),
        P(),
        P(),
    )
    out_specs = (P("blk", None), P("blk", None, "kv"), P("blk", None, "kv"))
    return jax.shard_map(body, mesh=mesh, in_specs=in_specs, out_specs=out_specs, check_vma=False)
```

```python
import functools
import math

import jax
import jax.numpy as jnp
from jax import lax
from jax.experimental import pallas as pl
from jax.experimental.pallas import tpu as pltpu
from jax.sharding import PartitionSpec as P

HD = 64
PAGE = 256
PMAX = 4
LANES = 128
GROUPS = (384, 256)
UNITS = ((128, 256), (128, 128))
PARTS = 4
SLOT_ORDER = (2, 1, 3)
PAGE_ORDER = (2, 1, 3, 0)
EARLY = 1
VMEM_LIMIT = 16 * 1024 * 1024
FIRST_LIMIT = 58 * 1024 * 1024

epsilon = 1e-06

f32 = jnp.float32
bf16 = jnp.bfloat16


def from_behind(block, axis, distance):
    devices = range(lax.axis_size(axis))
    route = [((i - distance) % len(devices), i) for i in devices]
    return lax.ppermute(block, axis, route)


def over_blk(block, distances):
    devices = lax.axis_size("blk")
    route = []
    for kv in range(lax.axis_size("kv")):
        for i in range(devices):
            route.append((kv * devices + (i - distances[kv]) % devices, kv * devices + i))
    return lax.ppermute(block, ("kv", "blk"), route)


def after(block, *others):
    return lax.optimization_barrier((block, *others))[0]


def group_slices(width):
    slices, start = [], 0
    for size in GROUPS:
        slices.append((start, size))
        start += size
    assert start == width
    return slices


def unit_slices():
    units, base = [], 0
    for g, sizes in enumerate(UNITS):
        inner = 0
        for size in sizes:
            units.append((g, inner, base + inner, size))
            inner += size
        base += inner
    return units


def params(limit=VMEM_LIMIT):
    return pltpu.CompilerParams(vmem_limit_bytes=limit)


def cost():
    return pl.CostEstimate(flops=1, bytes_accessed=1, transcendentals=0)


def split_kernel(kv_ref, hidden, out, sem):
    part = PAGE // PARTS
    copies = []
    for i in range(PARTS):
        rows = pl.ds(pl.multiple_of(kv_ref[0] * PAGE + i * part, part), part)
        target = out.at[pl.ds(i * part, part)]
        copies.append(pltpu.make_async_copy(hidden.at[rows], target, sem.at[i]))
    for copy in copies:
        copy.start()
    for copy in copies:
        copy.wait()


def split_rows(hidden_in, kv_index):
    return pl.pallas_call(
        split_kernel,
        in_specs=[pl.BlockSpec(memory_space=pltpu.SMEM), pl.BlockSpec(memory_space=pltpu.HBM)],
        out_specs=pl.BlockSpec(memory_space=pltpu.VMEM),
        out_shape=jax.ShapeDtypeStruct((PAGE, hidden_in.shape[1]), bf16),
        scratch_shapes=[pltpu.SemaphoreType.DMA((PARTS,))],
        compiler_params=params(FIRST_LIMIT),
        cost_estimate=cost(),
        name="split_rows",
    )(kv_index, hidden_in)


def pack_kernel(slices, devices, offsets, here_ref, table, keys, values, _, *rest):
    outs, (buf, sem) = rest[:-2], rest[-2:]
    copies = []
    for slot in range(PMAX):
        asker = lax.rem(here_ref[0] + (devices - offsets[slot]), devices)
        local = lax.rem(table[slot, asker], keys.shape[0])
        for side, pool in enumerate((keys, values)):
            index = 2 * slot + side
            copies.append(pltpu.make_async_copy(pool.at[local], buf.at[index], sem.at[index]))
    for copy in copies:
        copy.start()
    for slot in range(PMAX):
        for side in range(2):
            index = 2 * slot + side
            copies[index].wait()
            for g, (start, size) in enumerate(slices):
                outs[g * PMAX + slot][side] = buf[index, :, start : start + size]


def pack(pool_keys, pool_values, table, here, devices, offsets, first):
    width = pool_keys.shape[2]
    slices = group_slices(width)
    outs = []
    for _, size in slices:
        outs += [jax.ShapeDtypeStruct((2, PAGE, size), bf16)] * PMAX
    smem = pl.BlockSpec(memory_space=pltpu.SMEM)
    hbm = pl.BlockSpec(memory_space=pltpu.HBM)
    result = pl.pallas_call(
        functools.partial(pack_kernel, slices, devices, offsets),
        in_specs=[smem, smem, hbm, hbm, pl.BlockSpec(memory_space=pl.ANY)],
        out_specs=[pl.BlockSpec(memory_space=pltpu.VMEM)] * len(outs),
        out_shape=outs,
        scratch_shapes=[
            pltpu.VMEM((2 * PMAX, PAGE, width), bf16),
            pltpu.SemaphoreType.DMA((2 * PMAX,)),
        ],
        compiler_params=params(FIRST_LIMIT),
        cost_estimate=cost(),
        name="pack",
    )(here, table, pool_keys, pool_values, first)
    return [result[PMAX * g : PMAX * (g + 1)] for g in range(len(slices))]


def head_sum_matrix():
    rows = (lax.broadcasted_iota(jnp.int32, (2 * LANES, LANES), 0) % LANES) // HD
    cols = lax.broadcasted_iota(jnp.int32, (2 * LANES, LANES), 1) // HD
    return jnp.where(rows == cols, 1.0 / HD, 0.0).astype(bf16)


def head_norm(projected, gain, matrix):
    parts = []
    for start in range(0, projected.shape[1], LANES):
        part = projected[:, start : start + LANES]
        squares = part * part
        high = squares.astype(bf16)
        low = (squares - high.astype(f32)).astype(bf16)
        both = jnp.concatenate([high, low], axis=1)
        mean = jnp.dot(both, matrix, preferred_element_type=f32)
        parts.append(part * lax.rsqrt(mean + epsilon) * gain[:, start : start + LANES])
    return jnp.concatenate(parts, axis=1) if len(parts) > 1 else parts[0]


def row_scale_of(hidden):
    hidden_f = hidden.astype(f32)
    return lax.rsqrt(jnp.mean(hidden_f * hidden_f, axis=-1, keepdims=True) + epsilon)


def project_kernel(slices, hidden, wq, wk, wv, gain, *outs):
    matrix = head_sum_matrix()
    rows_all = hidden.shape[0]
    for low in range(0, rows_all, PAGE):
        rows = slice(low, low + PAGE)
        x = hidden[rows, :]
        scale = row_scale_of(x)
        for g, (start, size) in enumerate(slices):
            cols = slice(start, start + size)
            q = jnp.dot(x, wq[:, cols], preferred_element_type=f32)
            q = head_norm(q, gain[:, cols], matrix).astype(bf16)
            outs[3 * g][rows, :] = q * jnp.asarray(1.0 / math.sqrt(HD), bf16)
            k = jnp.dot(x, wk[:, cols], preferred_element_type=f32)
            outs[3 * g + 1][rows, :] = head_norm(k, gain[:, cols], matrix).astype(bf16)
            v = jnp.dot(x, wv[:, cols], preferred_element_type=f32)
            outs[3 * g + 2][rows, :] = (v * scale).astype(bf16)


def project(hidden_in, wq, wk, wv, gain):
    tokens, depth = hidden_in.shape
    width = wq.shape[1]
    slices = [(start, size) for _, _, start, size in unit_slices()]
    outs = []
    for _, size in slices:
        outs += [jax.ShapeDtypeStruct((tokens, size), bf16)] * 3
    flat = pl.pallas_call(
        functools.partial(project_kernel, slices),
        out_shape=outs,
        compiler_params=params(),
        cost_estimate=cost(),
        name="project",
    )(hidden_in, wq, wk, wv, gain)
    return [flat[3 * g : 3 * g + 3] for g in range(len(slices))]


def relay_kernel(slices, blocks, devices, offsets, kv_ref, here_ref, placement, *refs):
    mine, theirs, wk, wv, gain, key_out, value_out = refs
    matrix = head_sum_matrix()
    for rows_ref, block in ((mine, kv_ref[0]), (theirs, 1 - kv_ref[0])):
        x = rows_ref[...]
        scale = row_scale_of(x)
        offset = jnp.where(block == 0, offsets[0], offsets[1])
        source = lax.rem(here_ref[0] + (devices - offset), devices)
        slot = lax.rem(placement[source * blocks + block], blocks)
        for start, size in slices:
            cols = slice(start, start + size)
            k = jnp.dot(x, wk[:, cols], preferred_element_type=f32)
            key_out[slot, :, cols] = head_norm(k, gain[:, cols], matrix).astype(bf16)
            v = jnp.dot(x, wv[:, cols], preferred_element_type=f32)
            value_out[slot, :, cols] = (v * scale).astype(bf16)


def relay_project(mine, theirs, wk, wv, gain, kv_index, here, placement, offsets):
    blocks = len(offsets)
    depth, width = wk.shape
    out = jax.ShapeDtypeStruct((blocks, PAGE, width), bf16)
    smem = pl.BlockSpec(memory_space=pltpu.SMEM)
    vmem = pl.BlockSpec(memory_space=pltpu.VMEM)
    return pl.pallas_call(
        functools.partial(
            relay_kernel, group_slices(width), blocks, lax.axis_size("blk"), offsets
        ),
        in_specs=[smem] * 3 + [vmem] * 5,
        out_specs=[vmem, vmem],
        out_shape=[out, out],
        compiler_params=params(),
        cost_estimate=cost(),
        name="relay_project",
    )(kv_index, here, placement, mine, theirs, wk, wv, gain)


def weighted(q, blocks):
    lane = lax.broadcasted_iota(jnp.int32, (1, LANES), 1) // HD
    sums = []
    for side in range(2):
        q_side = jnp.where(lane == side, q, jnp.zeros_like(q))
        acc = jnp.zeros((q.shape[0], 2 * LANES), f32)
        for keys, values, visible in blocks:
            scores = lax.dot_general(
                q_side, keys, (((1,), (1,)), ((), ())), preferred_element_type=f32
            )
            weights = jnp.exp(scores)
            if visible is not None:
                weights = jnp.where(visible, weights, 0.0)
            acc += jnp.dot(weights.astype(bf16), values, preferred_element_type=f32)
        sums.append(acc)
    mixed = jnp.where(lane == 0, sums[0][:, :LANES], sums[1][:, :LANES])
    totals = jnp.where(lane == 0, sums[0][:, LANES:], sums[1][:, LANES:])
    return mixed, totals


def own_blocks(k_ref, v_ref, live, cols):
    row = lax.broadcasted_iota(jnp.int32, (PAGE, PAGE), 0)
    col = lax.broadcasted_iota(jnp.int32, (PAGE, PAGE), 1)
    key_row = lax.broadcasted_iota(jnp.int32, (PAGE, LANES), 0)
    blocks = []
    for b in range(k_ref.shape[0] // PAGE):
        rows = slice(b * PAGE, (b + 1) * PAGE)
        keep = (key_row + b * PAGE) < live
        shown = jnp.where(keep, v_ref[rows, cols].astype(f32), 0.0).astype(bf16)
        ones = jnp.where(keep, 1.0, 0.0).astype(bf16)
        blocks.append((k_ref[rows, cols], jnp.concatenate([shown, ones], axis=1)))
    return blocks, col <= row


def page_blocks(pages, slots, depth, cols):
    blocks = []
    for page, slot in zip(pages, slots):
        keep = jnp.where(slot < depth, 1.0, 0.0).astype(bf16)
        ones = jnp.full((PAGE, LANES), 1.0, bf16) * keep
        values = jnp.concatenate([page[1, :, cols] * keep, ones], axis=1)
        blocks.append((page[0, :, cols], values, None))
    return blocks


def attend_kernel(inner, slots, live_ref, depth_ref, q_ref, k_ref, v_ref, *refs):
    pages, outs = refs[: len(slots)], refs[len(slots) :]
    tokens, width = q_ref.shape
    for start in range(0, width, LANES):
        cols = slice(start, start + LANES)
        own, causal = own_blocks(k_ref, v_ref, live_ref[0], cols)
        page_cols = slice(inner + start, inner + start + LANES)
        cached = page_blocks(pages, slots, depth_ref[0], page_cols)
        for b in range(tokens // PAGE):
            rows = slice(b * PAGE, (b + 1) * PAGE)
            blocks = [own[j] + (causal if j == b else None,) for j in range(b + 1)]
            mixed, totals = weighted(q_ref[rows, cols], blocks + cached)
            if len(outs) == 1:
                outs[0][rows, cols] = (mixed / totals).astype(bf16)
            else:
                outs[0][rows, cols] = mixed
                outs[1][rows, cols] = totals


def attend(live, depth, q, k, v, pages, slots, inner):
    smem = pl.BlockSpec(memory_space=pltpu.SMEM)
    vmem = pl.BlockSpec(memory_space=pltpu.VMEM)
    if len(slots) == PMAX:
        out = [jax.ShapeDtypeStruct(q.shape, bf16)]
    else:
        out = [jax.ShapeDtypeStruct(q.shape, f32)] * 2
    result = pl.pallas_call(
        functools.partial(attend_kernel, inner, slots),
        in_specs=[smem, smem] + [vmem] * (3 + len(slots)),
        out_specs=[vmem] * len(out),
        out_shape=out,
        compiler_params=params(),
        cost_estimate=cost(),
        name="attend",
    )(live, depth, q, k, v, *pages)
    return result[0] if len(out) == 1 else result


def attend_rest_kernel(inner, slots, depth_ref, q_ref, mixed_ref, totals_ref, *refs):
    pages, out = refs[: len(slots)], refs[len(slots)]
    tokens, width = q_ref.shape
    for start in range(0, width, LANES):
        cols = slice(start, start + LANES)
        page_cols = slice(inner + start, inner + start + LANES)
        cached = page_blocks(pages, slots, depth_ref[0], page_cols)
        for b in range(tokens // PAGE):
            rows = slice(b * PAGE, (b + 1) * PAGE)
            mixed, totals = weighted(q_ref[rows, cols], cached)
            mixed += mixed_ref[rows, cols]
            totals += totals_ref[rows, cols]
            out[rows, cols] = (mixed / totals).astype(bf16)


def attend_rest(depth, q, mixed, totals, pages, slots, inner):
    smem = pl.BlockSpec(memory_space=pltpu.SMEM)
    vmem = pl.BlockSpec(memory_space=pltpu.VMEM)
    return pl.pallas_call(
        functools.partial(attend_rest_kernel, inner, slots),
        in_specs=[smem] + [vmem] * (3 + len(slots)),
        out_specs=vmem,
        out_shape=jax.ShapeDtypeStruct(q.shape, bf16),
        compiler_params=params(),
        cost_estimate=cost(),
        name="attend_rest",
    )(depth, q, mixed, totals, *pages)


def projected_heads(slices, rows, mine, theirs, w_mine, w_theirs):
    def half(parts, weights):
        total = None
        for part, (start, size) in zip(parts, slices):
            weight = weights[start : start + size, :]
            term = jnp.dot(part[rows, :], weight, preferred_element_type=f32)
            total = term if total is None else total + term
        return total

    return half(mine, w_mine) + half(theirs, w_theirs)


def partial_kernel(slices, hidden, rate, w_mine, w_theirs, *refs):
    count = len(slices)
    mine, theirs = refs[:count], refs[count : 2 * count]
    base, out = refs[2 * count :]
    for low in range(0, out.shape[0], PAGE):
        rows = slice(low, low + PAGE)
        out[rows, :] = projected_heads(slices, rows, mine, theirs, w_mine, w_theirs)
        anchor = hidden[rows, :].astype(f32) * row_scale_of(hidden[rows, :])
        base[rows, :] = anchor - rate[...] * anchor


def partial_branch(slices, hidden_in, rate, w_mine, w_theirs, mine, theirs):
    out = jax.ShapeDtypeStruct(hidden_in.shape, f32)
    vmem = pl.BlockSpec(memory_space=pltpu.VMEM)
    return pl.pallas_call(
        functools.partial(partial_kernel, slices),
        in_specs=[vmem] * (4 + 2 * len(slices)),
        out_specs=[vmem] * 2,
        out_shape=[out, out],
        compiler_params=params(),
        cost_estimate=cost(),
        name="partial_branch",
    )(hidden_in, rate, w_mine, w_theirs, *mine, *theirs)


def add_kernel(slices, begun, w_mine, w_theirs, *refs):
    count = len(slices)
    mine, theirs, out = refs[:count], refs[count : 2 * count], refs[2 * count]
    for low in range(0, out.shape[0], PAGE):
        rows = slice(low, low + PAGE)
        term = projected_heads(slices, rows, mine, theirs, w_mine, w_theirs)
        out[rows, :] = begun[rows, :] + term


def add_branch(slices, begun, w_mine, w_theirs, mine, theirs):
    vmem = pl.BlockSpec(memory_space=pltpu.VMEM)
    return pl.pallas_call(
        functools.partial(add_kernel, slices),
        in_specs=[vmem] * (3 + 2 * len(slices)),
        out_specs=vmem,
        out_shape=jax.ShapeDtypeStruct(begun.shape, f32),
        compiler_params=params(),
        cost_estimate=cost(),
        name="add_branch",
    )(begun, w_mine, w_theirs, *mine, *theirs)


def finish_kernel(slices, base, w_mine, w_theirs, rate, begun, *refs):
    count = len(slices)
    mine, theirs = refs[:count], refs[count : 2 * count]
    out, buf, sem = refs[2 * count :]
    step = buf.shape[1]
    copies = []
    for i in range(buf.shape[0]):
        rows = slice(i * step, (i + 1) * step)
        branch = begun[rows, :] + projected_heads(slices, rows, mine, theirs, w_mine, w_theirs)
        mean = jnp.mean(branch * branch, axis=-1, keepdims=True)
        updated = base[rows, :] + rate[...] * (branch * lax.rsqrt(mean + epsilon))
        scale = lax.rsqrt(jnp.mean(updated * updated, axis=-1, keepdims=True) + epsilon)
        buf[i] = (updated * scale).astype(bf16)
        copy = pltpu.make_async_copy(buf.at[i], out.at[pl.ds(i * step, step)], sem.at[i])
        copy.start()
        copies.append(copy)
    for copy in copies:
        copy.wait()


def finish(slices, base, w_mine, w_theirs, rate, begun, mine, theirs):
    tokens, depth = base.shape
    steps = 4
    vmem = pl.BlockSpec(memory_space=pltpu.VMEM)
    return pl.pallas_call(
        functools.partial(finish_kernel, slices),
        in_specs=[vmem] * (5 + 2 * len(slices)),
        out_specs=pl.BlockSpec(memory_space=pltpu.HBM),
        out_shape=jax.ShapeDtypeStruct((tokens, depth), bf16),
        scratch_shapes=[
            pltpu.VMEM((steps, tokens // steps, depth), bf16),
            pltpu.SemaphoreType.DMA((steps,)),
        ],
        compiler_params=params(),
        cost_estimate=cost(),
        name="finish",
    )(base, w_mine, w_theirs, rate, begun, *mine, *theirs)


def body(
    hidden_in,
    w_query,
    w_key,
    w_value,
    w_out,
    head_gain,
    eigen_rate,
    pool_keys,
    pool_values,
    req_len,
    prefix_len,
    prefix_pages,
    placement,
):
    devices = lax.axis_size("blk")
    here = lax.axis_index("blk").astype(jnp.int32).reshape(1)
    kv_index = lax.axis_index("kv").astype(jnp.int32).reshape(1)
    blocks = hidden_in.shape[0] // PAGE
    gain = head_gain.reshape(1, -1)
    rate = eigen_rate.reshape(1, -1)
    page_offsets = [slot * devices // PMAX + 1 for slot in range(PMAX)]
    block_offsets = [(2 * b + 1) * devices // (2 * blocks) for b in range(blocks)]

    assert blocks == lax.axis_size("kv") == 2
    relay_send = split_rows(hidden_in, kv_index)
    page_send = pack(
        pool_keys, pool_values, prefix_pages.T, here, devices, page_offsets, relay_send
    )
    projected = project(hidden_in, w_query, w_key, w_value, gain)

    def fetch(block, slot):
        return over_blk(block, [devices - page_offsets[slot]] * 2)

    relay_mine = over_blk(relay_send, block_offsets)
    ready = projected[0][0]
    first = {slot: fetch(page_send[0][slot], slot) for slot in SLOT_ORDER}
    first[0] = fetch(after(page_send[0][0], ready, relay_mine), 0)
    arrived = [first[slot] for slot in SLOT_ORDER]
    second = {}
    for slot in PAGE_ORDER:
        gate = (ready, relay_mine, *arrived, first[0])
        second[slot] = fetch(after(page_send[1][slot], *gate), slot)
    pages = [[got[slot] for slot in PAGE_ORDER] for got in (first, second)]
    w_theirs = from_behind(w_out, "kv", 1)
    relay_theirs = from_behind(after(relay_mine, w_theirs, *arrived, first[0]), "kv", 1)
    mine, theirs, slices = [[], []], [[], []], [[], []]
    units = list(zip(unit_slices(), projected))

    def swap(g, start, size, attended):
        mine[g].append(attended)
        theirs[g].append(from_behind(attended, "kv", 1))
        slices[g].append((start, size))

    (g, inner, start, size), (q, k, v) = units[0]
    swap(0, start, size, attend(req_len, prefix_len, q, k, v, pages[0], PAGE_ORDER, inner))
    (g, inner, start, size), (q, k, v) = units[1]
    q = after(q, theirs[0][0])
    swap(1, start, size, attend(req_len, prefix_len, q, k, v, pages[0], PAGE_ORDER, inner))
    new_keys, new_values = relay_project(
        after(relay_mine, mine[1][0]), relay_theirs, w_key, w_value, gain, kv_index, here, placement, block_offsets
    )
    base, begun = partial_branch(
        slices[0], hidden_in, rate, w_out, after(w_theirs, new_keys), mine[0], theirs[0]
    )
    early, late = PAGE_ORDER[:EARLY], PAGE_ORDER[EARLY:]
    sums = []
    for (g, inner, _, _), (q, k, v) in units:
        if g:
            q = after(q, new_keys, begun)
            sums.append(attend(req_len, prefix_len, q, k, v, pages[g][:EARLY], early, inner))
    rest = [unit for unit in units if unit[0][0]]
    for ((g, inner, start, size), (q, _, _)), (mixed, totals) in zip(rest, sums):
        q = after(q, *[total for _, total in sums])
        swap(g, start, size, attend_rest(prefix_len, q, mixed, totals, pages[g][EARLY:], late, inner))
    begun = add_branch(slices[1][:-1], begun, w_out, w_theirs, mine[1][:-1], theirs[1][:-1])
    layer_out = finish(
        slices[1][-1:], base, w_out, w_theirs, rate, begun, mine[1][-1:], theirs[1][-1:]
    )
    return (layer_out, new_keys, new_values)


def solution(mesh):
    in_specs = (
        P("blk", None),
        P(None, "kv"),
        P(None, "kv"),
        P(None, "kv"),
        P("kv", None),
        P("kv"),
        P(),
        P("blk", None, "kv"),
        P("blk", None, "kv"),
        P("blk"),
        P("blk"),
        P(),
        P(),
    )
    out_specs = (P("blk", None), P("blk", None, "kv"), P("blk", None, "kv"))
    return jax.shard_map(body, mesh=mesh, in_specs=in_specs, out_specs=out_specs, check_vma=False)
```

```python
import functools
import math

import jax
import jax.numpy as jnp
from jax import lax
from jax.experimental import pallas as pl
from jax.experimental.pallas import tpu as pltpu
from jax.sharding import PartitionSpec as P

HD = 64
PAGE = 256
PMAX = 4
LANES = 128
GROUPS = (256, 384)
UNITS = ((256,), (128, 128, 128))
PARTS = 4
SLOT_ORDER = (2, 1, 3)
PAGE_ORDER = (2, 1, 3, 0)
EARLY = 1
VMEM_LIMIT = 16 * 1024 * 1024
FIRST_LIMIT = 58 * 1024 * 1024

epsilon = 1e-06

f32 = jnp.float32
bf16 = jnp.bfloat16


def from_behind(block, axis, distance):
    devices = range(lax.axis_size(axis))
    route = [((i - distance) % len(devices), i) for i in devices]
    return lax.ppermute(block, axis, route)


def over_blk(block, distances):
    devices = lax.axis_size("blk")
    route = []
    for kv in range(lax.axis_size("kv")):
        for i in range(devices):
            route.append((kv * devices + (i - distances[kv]) % devices, kv * devices + i))
    return lax.ppermute(block, ("kv", "blk"), route)


def after(block, *others):
    return lax.optimization_barrier((block, *others))[0]


def group_slices(width):
    slices, start = [], 0
    for size in GROUPS:
        slices.append((start, size))
        start += size
    assert start == width
    return slices


def unit_slices():
    units, base = [], 0
    for g, sizes in enumerate(UNITS):
        inner = 0
        for size in sizes:
            units.append((g, inner, base + inner, size))
            inner += size
        base += inner
    return units


def params(limit=VMEM_LIMIT):
    return pltpu.CompilerParams(vmem_limit_bytes=limit)


def cost():
    return pl.CostEstimate(flops=1, bytes_accessed=1, transcendentals=0)


def pack_kernel(slices, devices, offsets, here_ref, table, keys, values, _, *rest):
    outs, (buf, sem) = rest[:-2], rest[-2:]
    copies = []
    for slot in range(PMAX):
        asker = lax.rem(here_ref[0] + (devices - offsets[slot]), devices)
        local = lax.rem(table[slot, asker], keys.shape[0])
        for side, pool in enumerate((keys, values)):
            index = 2 * slot + side
            copies.append(pltpu.make_async_copy(pool.at[local], buf.at[index], sem.at[index]))
    for copy in copies:
        copy.start()
    for slot in range(PMAX):
        for side in range(2):
            index = 2 * slot + side
            copies[index].wait()
            for g, (start, size) in enumerate(slices):
                outs[g * PMAX + slot][side] = buf[index, :, start : start + size]


def pack(pool_keys, pool_values, table, here, devices, offsets, first):
    width = pool_keys.shape[2]
    slices = group_slices(width)
    outs = []
    for _, size in slices:
        outs += [jax.ShapeDtypeStruct((2, PAGE, size), bf16)] * PMAX
    smem = pl.BlockSpec(memory_space=pltpu.SMEM)
    hbm = pl.BlockSpec(memory_space=pltpu.HBM)
    result = pl.pallas_call(
        functools.partial(pack_kernel, slices, devices, offsets),
        in_specs=[smem, smem, hbm, hbm, pl.BlockSpec(memory_space=pl.ANY)],
        out_specs=[pl.BlockSpec(memory_space=pltpu.VMEM)] * len(outs),
        out_shape=outs,
        scratch_shapes=[
            pltpu.VMEM((2 * PMAX, PAGE, width), bf16),
            pltpu.SemaphoreType.DMA((2 * PMAX,)),
        ],
        compiler_params=params(FIRST_LIMIT),
        cost_estimate=cost(),
        name="pack",
    )(here, table, pool_keys, pool_values, first)
    return [result[PMAX * g : PMAX * (g + 1)] for g in range(len(slices))]


def head_sum_matrix():
    rows = (lax.broadcasted_iota(jnp.int32, (2 * LANES, LANES), 0) % LANES) // HD
    cols = lax.broadcasted_iota(jnp.int32, (2 * LANES, LANES), 1) // HD
    return jnp.where(rows == cols, 1.0 / HD, 0.0).astype(bf16)


def head_norm(projected, gain, matrix):
    parts = []
    for start in range(0, projected.shape[1], LANES):
        part = projected[:, start : start + LANES]
        squares = part * part
        high = squares.astype(bf16)
        low = (squares - high.astype(f32)).astype(bf16)
        both = jnp.concatenate([high, low], axis=1)
        mean = jnp.dot(both, matrix, preferred_element_type=f32)
        parts.append(part * lax.rsqrt(mean + epsilon) * gain[:, start : start + LANES])
    return jnp.concatenate(parts, axis=1) if len(parts) > 1 else parts[0]


def row_scale_of(hidden):
    hidden_f = hidden.astype(f32)
    return lax.rsqrt(jnp.mean(hidden_f * hidden_f, axis=-1, keepdims=True) + epsilon)


def project_kernel(slices, hidden, wq, wk, wv, gain, *outs):
    matrix = head_sum_matrix()
    rows_all = hidden.shape[0]
    for low in range(0, rows_all, PAGE):
        rows = slice(low, low + PAGE)
        x = hidden[rows, :]
        scale = row_scale_of(x)
        for g, (start, size) in enumerate(slices):
            cols = slice(start, start + size)
            q = jnp.dot(x, wq[:, cols], preferred_element_type=f32)
            q = head_norm(q, gain[:, cols], matrix).astype(bf16)
            outs[3 * g][rows, :] = q * jnp.asarray(1.0 / math.sqrt(HD), bf16)
            k = jnp.dot(x, wk[:, cols], preferred_element_type=f32)
            outs[3 * g + 1][rows, :] = head_norm(k, gain[:, cols], matrix).astype(bf16)
            v = jnp.dot(x, wv[:, cols], preferred_element_type=f32)
            outs[3 * g + 2][rows, :] = (v * scale).astype(bf16)


def project(hidden_in, wq, wk, wv, gain):
    tokens, depth = hidden_in.shape
    width = wq.shape[1]
    slices = [(start, size) for _, _, start, size in unit_slices()]
    outs = []
    for _, size in slices:
        outs += [jax.ShapeDtypeStruct((tokens, size), bf16)] * 3
    flat = pl.pallas_call(
        functools.partial(project_kernel, slices),
        out_shape=outs,
        compiler_params=params(),
        cost_estimate=cost(),
        name="project",
    )(hidden_in, wq, wk, wv, gain)
    return [flat[3 * g : 3 * g + 3] for g in range(len(slices))]


def relay_kernel(slices, blocks, devices, offsets, kv_ref, here_ref, placement, *refs):
    mine, theirs, wk, wv, gain, key_out, value_out = refs
    matrix = head_sum_matrix()
    for rows_ref, block in ((mine, kv_ref[0]), (theirs, 1 - kv_ref[0])):
        x = rows_ref[...]
        scale = row_scale_of(x)
        offset = jnp.where(block == 0, offsets[0], offsets[1])
        source = lax.rem(here_ref[0] + (devices - offset), devices)
        slot = lax.rem(placement[source * blocks + block], blocks)
        for start, size in slices:
            cols = slice(start, start + size)
            k = jnp.dot(x, wk[:, cols], preferred_element_type=f32)
            key_out[slot, :, cols] = head_norm(k, gain[:, cols], matrix).astype(bf16)
            v = jnp.dot(x, wv[:, cols], preferred_element_type=f32)
            value_out[slot, :, cols] = (v * scale).astype(bf16)


def relay_project(mine, theirs, wk, wv, gain, kv_index, here, placement, offsets):
    blocks = len(offsets)
    depth, width = wk.shape
    out = jax.ShapeDtypeStruct((blocks, PAGE, width), bf16)
    smem = pl.BlockSpec(memory_space=pltpu.SMEM)
    vmem = pl.BlockSpec(memory_space=pltpu.VMEM)
    return pl.pallas_call(
        functools.partial(
            relay_kernel, group_slices(width), blocks, lax.axis_size("blk"), offsets
        ),
        in_specs=[smem] * 3 + [vmem] * 5,
        out_specs=[vmem, vmem],
        out_shape=[out, out],
        compiler_params=params(),
        cost_estimate=cost(),
        name="relay_project",
    )(kv_index, here, placement, mine, theirs, wk, wv, gain)


def weighted(q, blocks):
    lane = lax.broadcasted_iota(jnp.int32, (1, LANES), 1) // HD
    sums = []
    for side in range(2):
        q_side = jnp.where(lane == side, q, jnp.zeros_like(q))
        acc = jnp.zeros((q.shape[0], 2 * LANES), f32)
        for keys, values, visible in blocks:
            scores = lax.dot_general(
                q_side, keys, (((1,), (1,)), ((), ())), preferred_element_type=f32
            )
            weights = jnp.exp(scores)
            if visible is not None:
                weights = jnp.where(visible, weights, 0.0)
            acc += jnp.dot(weights.astype(bf16), values, preferred_element_type=f32)
        sums.append(acc)
    mixed = jnp.where(lane == 0, sums[0][:, :LANES], sums[1][:, :LANES])
    totals = jnp.where(lane == 0, sums[0][:, LANES:], sums[1][:, LANES:])
    return mixed, totals


def own_blocks(k_ref, v_ref, live, cols):
    row = lax.broadcasted_iota(jnp.int32, (PAGE, PAGE), 0)
    col = lax.broadcasted_iota(jnp.int32, (PAGE, PAGE), 1)
    key_row = lax.broadcasted_iota(jnp.int32, (PAGE, LANES), 0)
    blocks = []
    for b in range(k_ref.shape[0] // PAGE):
        rows = slice(b * PAGE, (b + 1) * PAGE)
        keep = (key_row + b * PAGE) < live
        shown = jnp.where(keep, v_ref[rows, cols].astype(f32), 0.0).astype(bf16)
        ones = jnp.where(keep, 1.0, 0.0).astype(bf16)
        blocks.append((k_ref[rows, cols], jnp.concatenate([shown, ones], axis=1)))
    return blocks, col <= row


def page_blocks(pages, slots, depth, cols):
    blocks = []
    for page, slot in zip(pages, slots):
        keep = jnp.where(slot < depth, 1.0, 0.0).astype(bf16)
        ones = jnp.full((PAGE, LANES), 1.0, bf16) * keep
        values = jnp.concatenate([page[1, :, cols] * keep, ones], axis=1)
        blocks.append((page[0, :, cols], values, None))
    return blocks


def attend_kernel(inner, slots, live_ref, depth_ref, q_ref, k_ref, v_ref, *refs):
    pages, outs = refs[: len(slots)], refs[len(slots) :]
    tokens, width = q_ref.shape
    for start in range(0, width, LANES):
        cols = slice(start, start + LANES)
        own, causal = own_blocks(k_ref, v_ref, live_ref[0], cols)
        page_cols = slice(inner + start, inner + start + LANES)
        cached = page_blocks(pages, slots, depth_ref[0], page_cols)
        for b in range(tokens // PAGE):
            rows = slice(b * PAGE, (b + 1) * PAGE)
            blocks = [own[j] + (causal if j == b else None,) for j in range(b + 1)]
            mixed, totals = weighted(q_ref[rows, cols], blocks + cached)
            if len(outs) == 1:
                outs[0][rows, cols] = (mixed / totals).astype(bf16)
            else:
                outs[0][rows, cols] = mixed
                outs[1][rows, cols] = totals


def attend(live, depth, q, k, v, pages, slots, inner):
    smem = pl.BlockSpec(memory_space=pltpu.SMEM)
    vmem = pl.BlockSpec(memory_space=pltpu.VMEM)
    if len(slots) == PMAX:
        out = [jax.ShapeDtypeStruct(q.shape, bf16)]
    else:
        out = [jax.ShapeDtypeStruct(q.shape, f32)] * 2
    result = pl.pallas_call(
        functools.partial(attend_kernel, inner, slots),
        in_specs=[smem, smem] + [vmem] * (3 + len(slots)),
        out_specs=[vmem] * len(out),
        out_shape=out,
        compiler_params=params(),
        cost_estimate=cost(),
        name="attend",
    )(live, depth, q, k, v, *pages)
    return result[0] if len(out) == 1 else result


def attend_rest_kernel(inner, slots, depth_ref, q_ref, mixed_ref, totals_ref, *refs):
    pages, out = refs[: len(slots)], refs[len(slots)]
    tokens, width = q_ref.shape
    for start in range(0, width, LANES):
        cols = slice(start, start + LANES)
        page_cols = slice(inner + start, inner + start + LANES)
        cached = page_blocks(pages, slots, depth_ref[0], page_cols)
        for b in range(tokens // PAGE):
            rows = slice(b * PAGE, (b + 1) * PAGE)
            mixed, totals = weighted(q_ref[rows, cols], cached)
            mixed += mixed_ref[rows, cols]
            totals += totals_ref[rows, cols]
            out[rows, cols] = (mixed / totals).astype(bf16)


def attend_rest(depth, q, mixed, totals, pages, slots, inner):
    smem = pl.BlockSpec(memory_space=pltpu.SMEM)
    vmem = pl.BlockSpec(memory_space=pltpu.VMEM)
    return pl.pallas_call(
        functools.partial(attend_rest_kernel, inner, slots),
        in_specs=[smem] + [vmem] * (3 + len(slots)),
        out_specs=vmem,
        out_shape=jax.ShapeDtypeStruct(q.shape, bf16),
        compiler_params=params(),
        cost_estimate=cost(),
        name="attend_rest",
    )(depth, q, mixed, totals, *pages)


def projected_heads(slices, rows, mine, theirs, w_mine, w_theirs):
    def half(parts, weights):
        total = None
        for part, (start, size) in zip(parts, slices):
            weight = weights[start : start + size, :]
            term = jnp.dot(part[rows, :], weight, preferred_element_type=f32)
            total = term if total is None else total + term
        return total

    return half(mine, w_mine) + half(theirs, w_theirs)


def partial_kernel(slices, hidden, rate, w_mine, w_theirs, *refs):
    count = len(slices)
    mine, theirs = refs[:count], refs[count : 2 * count]
    base, out = refs[2 * count :]
    for low in range(0, out.shape[0], PAGE):
        rows = slice(low, low + PAGE)
        out[rows, :] = projected_heads(slices, rows, mine, theirs, w_mine, w_theirs)
        anchor = hidden[rows, :].astype(f32) * row_scale_of(hidden[rows, :])
        base[rows, :] = anchor - rate[...] * anchor


def partial_branch(slices, hidden_in, rate, w_mine, w_theirs, mine, theirs):
    out = jax.ShapeDtypeStruct(hidden_in.shape, f32)
    vmem = pl.BlockSpec(memory_space=pltpu.VMEM)
    return pl.pallas_call(
        functools.partial(partial_kernel, slices),
        in_specs=[vmem] * (4 + 2 * len(slices)),
        out_specs=[vmem] * 2,
        out_shape=[out, out],
        compiler_params=params(),
        cost_estimate=cost(),
        name="partial_branch",
    )(hidden_in, rate, w_mine, w_theirs, *mine, *theirs)


def add_kernel(slices, begun, w_mine, w_theirs, *refs):
    count = len(slices)
    mine, theirs, out = refs[:count], refs[count : 2 * count], refs[2 * count]
    for low in range(0, out.shape[0], PAGE):
        rows = slice(low, low + PAGE)
        term = projected_heads(slices, rows, mine, theirs, w_mine, w_theirs)
        out[rows, :] = begun[rows, :] + term


def add_branch(slices, begun, w_mine, w_theirs, mine, theirs):
    vmem = pl.BlockSpec(memory_space=pltpu.VMEM)
    return pl.pallas_call(
        functools.partial(add_kernel, slices),
        in_specs=[vmem] * (3 + 2 * len(slices)),
        out_specs=vmem,
        out_shape=jax.ShapeDtypeStruct(begun.shape, f32),
        compiler_params=params(),
        cost_estimate=cost(),
        name="add_branch",
    )(begun, w_mine, w_theirs, *mine, *theirs)


def finish_kernel(slices, base, w_mine, w_theirs, rate, begun, *refs):
    count = len(slices)
    mine, theirs = refs[:count], refs[count : 2 * count]
    out, buf, sem = refs[2 * count :]
    step = buf.shape[1]
    copies = []
    for i in range(buf.shape[0]):
        rows = slice(i * step, (i + 1) * step)
        branch = begun[rows, :] + projected_heads(slices, rows, mine, theirs, w_mine, w_theirs)
        mean = jnp.mean(branch * branch, axis=-1, keepdims=True)
        updated = base[rows, :] + rate[...] * (branch * lax.rsqrt(mean + epsilon))
        scale = lax.rsqrt(jnp.mean(updated * updated, axis=-1, keepdims=True) + epsilon)
        buf[i] = (updated * scale).astype(bf16)
        copy = pltpu.make_async_copy(buf.at[i], out.at[pl.ds(i * step, step)], sem.at[i])
        copy.start()
        copies.append(copy)
    for copy in copies:
        copy.wait()


def finish(slices, base, w_mine, w_theirs, rate, begun, mine, theirs):
    tokens, depth = base.shape
    steps = 4
    vmem = pl.BlockSpec(memory_space=pltpu.VMEM)
    return pl.pallas_call(
        functools.partial(finish_kernel, slices),
        in_specs=[vmem] * (5 + 2 * len(slices)),
        out_specs=pl.BlockSpec(memory_space=pltpu.HBM),
        out_shape=jax.ShapeDtypeStruct((tokens, depth), bf16),
        scratch_shapes=[
            pltpu.VMEM((steps, tokens // steps, depth), bf16),
            pltpu.SemaphoreType.DMA((steps,)),
        ],
        compiler_params=params(),
        cost_estimate=cost(),
        name="finish",
    )(base, w_mine, w_theirs, rate, begun, *mine, *theirs)


def body(
    hidden_in,
    w_query,
    w_key,
    w_value,
    w_out,
    head_gain,
    eigen_rate,
    pool_keys,
    pool_values,
    req_len,
    prefix_len,
    prefix_pages,
    placement,
):
    devices = lax.axis_size("blk")
    here = lax.axis_index("blk").astype(jnp.int32).reshape(1)
    kv_index = lax.axis_index("kv").astype(jnp.int32).reshape(1)
    blocks = hidden_in.shape[0] // PAGE
    gain = head_gain.reshape(1, -1)
    rate = eigen_rate.reshape(1, -1)
    page_offsets = [slot * devices // PMAX + 1 for slot in range(PMAX)]
    block_offsets = [(2 * b + 1) * devices // (2 * blocks) for b in range(blocks)]

    assert blocks == lax.axis_size("kv") == 2
    relay_send = lax.dynamic_slice_in_dim(hidden_in, lax.axis_index("kv") * PAGE, PAGE, axis=0)
    page_send = pack(
        pool_keys, pool_values, prefix_pages.T, here, devices, page_offsets, relay_send
    )
    projected = project(hidden_in, w_query, w_key, w_value, gain)

    def fetch(block, slot):
        return over_blk(block, [devices - page_offsets[slot]] * 2)

    relay_mine = over_blk(relay_send, block_offsets)
    ready = projected[0][0]
    first = {slot: fetch(page_send[0][slot], slot) for slot in SLOT_ORDER}
    first[0] = fetch(after(page_send[0][0], ready, relay_mine), 0)
    arrived = [first[slot] for slot in SLOT_ORDER]
    second = {}
    for slot in PAGE_ORDER:
        gate = (ready, relay_mine, *arrived, first[0])
        second[slot] = fetch(after(page_send[1][slot], *gate), slot)
    pages = [[got[slot] for slot in PAGE_ORDER] for got in (first, second)]
    w_theirs = from_behind(w_out, "kv", 1)
    relay_theirs = from_behind(after(relay_mine, w_theirs, *arrived, first[0]), "kv", 1)
    new_keys, new_values = relay_project(
        relay_mine, relay_theirs, w_key, w_value, gain, kv_index, here, placement, block_offsets
    )

    mine, theirs, slices = [[], []], [[], []], [[], []]
    units = list(zip(unit_slices(), projected))

    def swap(g, start, size, attended):
        mine[g].append(attended)
        theirs[g].append(from_behind(attended, "kv", 1))
        slices[g].append((start, size))

    for (g, inner, start, size), (q, k, v) in units:
        if g == 0:
            swap(g, start, size, attend(req_len, prefix_len, q, k, v, pages[0], PAGE_ORDER, inner))
    base, begun = partial_branch(
        slices[0], hidden_in, rate, w_out, after(w_theirs, new_keys), mine[0], theirs[0]
    )
    early, late = PAGE_ORDER[:EARLY], PAGE_ORDER[EARLY:]
    sums = []
    for (g, inner, _, _), (q, k, v) in units:
        if g:
            q = after(q, new_keys, begun)
            sums.append(attend(req_len, prefix_len, q, k, v, pages[g][:EARLY], early, inner))
    rest = [unit for unit in units if unit[0][0]]
    for ((g, inner, start, size), (q, _, _)), (mixed, totals) in zip(rest, sums):
        q = after(q, *[total for _, total in sums])
        swap(g, start, size, attend_rest(prefix_len, q, mixed, totals, pages[g][EARLY:], late, inner))
    begun = add_branch(slices[1][:-1], begun, w_out, w_theirs, mine[1][:-1], theirs[1][:-1])
    layer_out = finish(
        slices[1][-1:], base, w_out, w_theirs, rate, begun, mine[1][-1:], theirs[1][-1:]
    )
    return (layer_out, new_keys, new_values)


def solution(mesh):
    in_specs = (
        P("blk", None),
        P(None, "kv"),
        P(None, "kv"),
        P(None, "kv"),
        P("kv", None),
        P("kv"),
        P(),
        P("blk", None, "kv"),
        P("blk", None, "kv"),
        P("blk"),
        P("blk"),
        P(),
        P(),
    )
    out_specs = (P("blk", None), P("blk", None, "kv"), P("blk", None, "kv"))
    return jax.shard_map(body, mesh=mesh, in_specs=in_specs, out_specs=out_specs, check_vma=False)
```

```python
import functools
import math

import jax
import jax.numpy as jnp
from jax import lax
from jax.experimental import pallas as pl
from jax.experimental.pallas import tpu as pltpu
from jax.sharding import PartitionSpec as P

HD = 64
PAGE = 256
PMAX = 4
LANES = 128
GROUPS = (256, 384)
UNITS = ((256,), (128, 128, 128))
PARTS = 4
SLOT_ORDER = (2, 1, 3)
PAGE_ORDER = (2, 1, 3, 0)
EARLY = 1
VMEM_LIMIT = 16 * 1024 * 1024
FIRST_LIMIT = 58 * 1024 * 1024

epsilon = 1e-06

f32 = jnp.float32
bf16 = jnp.bfloat16


def from_behind(block, axis, distance):
    devices = range(lax.axis_size(axis))
    route = [((i - distance) % len(devices), i) for i in devices]
    return lax.ppermute(block, axis, route)


def over_blk(block, distances):
    devices = lax.axis_size("blk")
    route = []
    for kv in range(lax.axis_size("kv")):
        for i in range(devices):
            route.append((kv * devices + (i - distances[kv]) % devices, kv * devices + i))
    return lax.ppermute(block, ("kv", "blk"), route)


def after(block, *others):
    return lax.optimization_barrier((block, *others))[0]


def group_slices(width):
    slices, start = [], 0
    for size in GROUPS:
        slices.append((start, size))
        start += size
    assert start == width
    return slices


def unit_slices():
    units, base = [], 0
    for g, sizes in enumerate(UNITS):
        inner = 0
        for size in sizes:
            units.append((g, inner, base + inner, size))
            inner += size
        base += inner
    return units


def params(limit=VMEM_LIMIT):
    return pltpu.CompilerParams(vmem_limit_bytes=limit)


def cost():
    return pl.CostEstimate(flops=1, bytes_accessed=1, transcendentals=0)


def split_kernel(kv_ref, hidden, out, sem):
    part = PAGE // PARTS
    copies = []
    for i in range(PARTS):
        rows = pl.ds(pl.multiple_of(kv_ref[0] * PAGE + i * part, part), part)
        target = out.at[pl.ds(i * part, part)]
        copies.append(pltpu.make_async_copy(hidden.at[rows], target, sem.at[i]))
    for copy in copies:
        copy.start()
    for copy in copies:
        copy.wait()


def split_rows(hidden_in, kv_index):
    return pl.pallas_call(
        split_kernel,
        in_specs=[pl.BlockSpec(memory_space=pltpu.SMEM), pl.BlockSpec(memory_space=pltpu.HBM)],
        out_specs=pl.BlockSpec(memory_space=pltpu.VMEM),
        out_shape=jax.ShapeDtypeStruct((PAGE, hidden_in.shape[1]), bf16),
        scratch_shapes=[pltpu.SemaphoreType.DMA((PARTS,))],
        compiler_params=params(FIRST_LIMIT),
        cost_estimate=cost(),
        name="split_rows",
    )(kv_index, hidden_in)


def pack_kernel(slices, devices, offsets, here_ref, table, keys, values, _, *rest):
    outs, (buf, sem) = rest[:-2], rest[-2:]
    copies = []
    for slot in range(PMAX):
        asker = lax.rem(here_ref[0] + (devices - offsets[slot]), devices)
        local = lax.rem(table[slot, asker], keys.shape[0])
        for side, pool in enumerate((keys, values)):
            index = 2 * slot + side
            copies.append(pltpu.make_async_copy(pool.at[local], buf.at[index], sem.at[index]))
    for copy in copies:
        copy.start()
    for slot in range(PMAX):
        for side in range(2):
            index = 2 * slot + side
            copies[index].wait()
            for g, (start, size) in enumerate(slices):
                outs[g * PMAX + slot][side] = buf[index, :, start : start + size]


def pack(pool_keys, pool_values, table, here, devices, offsets, first):
    width = pool_keys.shape[2]
    slices = group_slices(width)
    outs = []
    for _, size in slices:
        outs += [jax.ShapeDtypeStruct((2, PAGE, size), bf16)] * PMAX
    smem = pl.BlockSpec(memory_space=pltpu.SMEM)
    hbm = pl.BlockSpec(memory_space=pltpu.HBM)
    result = pl.pallas_call(
        functools.partial(pack_kernel, slices, devices, offsets),
        in_specs=[smem, smem, hbm, hbm, pl.BlockSpec(memory_space=pl.ANY)],
        out_specs=[pl.BlockSpec(memory_space=pltpu.VMEM)] * len(outs),
        out_shape=outs,
        scratch_shapes=[
            pltpu.VMEM((2 * PMAX, PAGE, width), bf16),
            pltpu.SemaphoreType.DMA((2 * PMAX,)),
        ],
        compiler_params=params(FIRST_LIMIT),
        cost_estimate=cost(),
        name="pack",
    )(here, table, pool_keys, pool_values, first)
    return [result[PMAX * g : PMAX * (g + 1)] for g in range(len(slices))]


def head_sum_matrix():
    rows = (lax.broadcasted_iota(jnp.int32, (2 * LANES, LANES), 0) % LANES) // HD
    cols = lax.broadcasted_iota(jnp.int32, (2 * LANES, LANES), 1) // HD
    return jnp.where(rows == cols, 1.0 / HD, 0.0).astype(bf16)


def head_norm(projected, gain, matrix):
    parts = []
    for start in range(0, projected.shape[1], LANES):
        part = projected[:, start : start + LANES]
        squares = part * part
        high = squares.astype(bf16)
        low = (squares - high.astype(f32)).astype(bf16)
        both = jnp.concatenate([high, low], axis=1)
        mean = jnp.dot(both, matrix, preferred_element_type=f32)
        parts.append(part * lax.rsqrt(mean + epsilon) * gain[:, start : start + LANES])
    return jnp.concatenate(parts, axis=1) if len(parts) > 1 else parts[0]


def row_scale_of(hidden):
    hidden_f = hidden.astype(f32)
    return lax.rsqrt(jnp.mean(hidden_f * hidden_f, axis=-1, keepdims=True) + epsilon)


def project_kernel(slices, hidden, wq, wk, wv, gain, *outs):
    matrix = head_sum_matrix()
    rows_all = hidden.shape[0]
    for low in range(0, rows_all, PAGE):
        rows = slice(low, low + PAGE)
        x = hidden[rows, :]
        scale = row_scale_of(x)
        for g, (start, size) in enumerate(slices):
            cols = slice(start, start + size)
            q = jnp.dot(x, wq[:, cols], preferred_element_type=f32)
            q = head_norm(q, gain[:, cols], matrix).astype(bf16)
            outs[3 * g][rows, :] = q * jnp.asarray(1.0 / math.sqrt(HD), bf16)
            k = jnp.dot(x, wk[:, cols], preferred_element_type=f32)
            outs[3 * g + 1][rows, :] = head_norm(k, gain[:, cols], matrix).astype(bf16)
            v = jnp.dot(x, wv[:, cols], preferred_element_type=f32)
            outs[3 * g + 2][rows, :] = (v * scale).astype(bf16)


def project(hidden_in, wq, wk, wv, gain):
    tokens, depth = hidden_in.shape
    width = wq.shape[1]
    slices = [(start, size) for _, _, start, size in unit_slices()]
    outs = []
    for _, size in slices:
        outs += [jax.ShapeDtypeStruct((tokens, size), bf16)] * 3
    flat = pl.pallas_call(
        functools.partial(project_kernel, slices),
        out_shape=outs,
        compiler_params=params(),
        cost_estimate=cost(),
        name="project",
    )(hidden_in, wq, wk, wv, gain)
    return [flat[3 * g : 3 * g + 3] for g in range(len(slices))]


def relay_kernel(slices, blocks, devices, offsets, kv_ref, here_ref, placement, *refs):
    mine, theirs, wk, wv, gain, key_out, value_out = refs
    matrix = head_sum_matrix()
    for rows_ref, block in ((mine, kv_ref[0]), (theirs, 1 - kv_ref[0])):
        x = rows_ref[...]
        scale = row_scale_of(x)
        offset = jnp.where(block == 0, offsets[0], offsets[1])
        source = lax.rem(here_ref[0] + (devices - offset), devices)
        slot = lax.rem(placement[source * blocks + block], blocks)
        for start, size in slices:
            cols = slice(start, start + size)
            k = jnp.dot(x, wk[:, cols], preferred_element_type=f32)
            key_out[slot, :, cols] = head_norm(k, gain[:, cols], matrix).astype(bf16)
            v = jnp.dot(x, wv[:, cols], preferred_element_type=f32)
            value_out[slot, :, cols] = (v * scale).astype(bf16)


def relay_project(mine, theirs, wk, wv, gain, kv_index, here, placement, offsets):
    blocks = len(offsets)
    depth, width = wk.shape
    out = jax.ShapeDtypeStruct((blocks, PAGE, width), bf16)
    smem = pl.BlockSpec(memory_space=pltpu.SMEM)
    vmem = pl.BlockSpec(memory_space=pltpu.VMEM)
    return pl.pallas_call(
        functools.partial(
            relay_kernel, group_slices(width), blocks, lax.axis_size("blk"), offsets
        ),
        in_specs=[smem] * 3 + [vmem] * 5,
        out_specs=[vmem, vmem],
        out_shape=[out, out],
        compiler_params=params(),
        cost_estimate=cost(),
        name="relay_project",
    )(kv_index, here, placement, mine, theirs, wk, wv, gain)


def weighted(q, blocks):
    lane = lax.broadcasted_iota(jnp.int32, (1, LANES), 1) // HD
    sums = []
    for side in range(2):
        q_side = jnp.where(lane == side, q, jnp.zeros_like(q))
        acc = jnp.zeros((q.shape[0], 2 * LANES), f32)
        for keys, values, visible in blocks:
            scores = lax.dot_general(
                q_side, keys, (((1,), (1,)), ((), ())), preferred_element_type=f32
            )
            weights = jnp.exp(scores)
            if visible is not None:
                weights = jnp.where(visible, weights, 0.0)
            acc += jnp.dot(weights.astype(bf16), values, preferred_element_type=f32)
        sums.append(acc)
    mixed = jnp.where(lane == 0, sums[0][:, :LANES], sums[1][:, :LANES])
    totals = jnp.where(lane == 0, sums[0][:, LANES:], sums[1][:, LANES:])
    return mixed, totals


def own_blocks(k_ref, v_ref, live, cols):
    row = lax.broadcasted_iota(jnp.int32, (PAGE, PAGE), 0)
    col = lax.broadcasted_iota(jnp.int32, (PAGE, PAGE), 1)
    key_row = lax.broadcasted_iota(jnp.int32, (PAGE, LANES), 0)
    blocks = []
    for b in range(k_ref.shape[0] // PAGE):
        rows = slice(b * PAGE, (b + 1) * PAGE)
        keep = (key_row + b * PAGE) < live
        shown = jnp.where(keep, v_ref[rows, cols].astype(f32), 0.0).astype(bf16)
        ones = jnp.where(keep, 1.0, 0.0).astype(bf16)
        blocks.append((k_ref[rows, cols], jnp.concatenate([shown, ones], axis=1)))
    return blocks, col <= row


def page_blocks(pages, slots, depth, cols):
    blocks = []
    for page, slot in zip(pages, slots):
        keep = jnp.where(slot < depth, 1.0, 0.0).astype(bf16)
        ones = jnp.full((PAGE, LANES), 1.0, bf16) * keep
        values = jnp.concatenate([page[1, :, cols] * keep, ones], axis=1)
        blocks.append((page[0, :, cols], values, None))
    return blocks


def attend_kernel(inner, slots, live_ref, depth_ref, q_ref, k_ref, v_ref, *refs):
    pages, outs = refs[: len(slots)], refs[len(slots) :]
    tokens, width = q_ref.shape
    for start in range(0, width, LANES):
        cols = slice(start, start + LANES)
        own, causal = own_blocks(k_ref, v_ref, live_ref[0], cols)
        page_cols = slice(inner + start, inner + start + LANES)
        cached = page_blocks(pages, slots, depth_ref[0], page_cols)
        for b in range(tokens // PAGE):
            rows = slice(b * PAGE, (b + 1) * PAGE)
            blocks = [own[j] + (causal if j == b else None,) for j in range(b + 1)]
            mixed, totals = weighted(q_ref[rows, cols], blocks + cached)
            if len(outs) == 1:
                outs[0][rows, cols] = (mixed / totals).astype(bf16)
            else:
                outs[0][rows, cols] = mixed
                outs[1][rows, cols] = totals


def attend(live, depth, q, k, v, pages, slots, inner):
    smem = pl.BlockSpec(memory_space=pltpu.SMEM)
    vmem = pl.BlockSpec(memory_space=pltpu.VMEM)
    if len(slots) == PMAX:
        out = [jax.ShapeDtypeStruct(q.shape, bf16)]
    else:
        out = [jax.ShapeDtypeStruct(q.shape, f32)] * 2
    result = pl.pallas_call(
        functools.partial(attend_kernel, inner, slots),
        in_specs=[smem, smem] + [vmem] * (3 + len(slots)),
        out_specs=[vmem] * len(out),
        out_shape=out,
        compiler_params=params(),
        cost_estimate=cost(),
        name="attend",
    )(live, depth, q, k, v, *pages)
    return result[0] if len(out) == 1 else result


def attend_rest_kernel(inner, slots, depth_ref, q_ref, mixed_ref, totals_ref, *refs):
    pages, out = refs[: len(slots)], refs[len(slots)]
    tokens, width = q_ref.shape
    for start in range(0, width, LANES):
        cols = slice(start, start + LANES)
        page_cols = slice(inner + start, inner + start + LANES)
        cached = page_blocks(pages, slots, depth_ref[0], page_cols)
        for b in range(tokens // PAGE):
            rows = slice(b * PAGE, (b + 1) * PAGE)
            mixed, totals = weighted(q_ref[rows, cols], cached)
            mixed += mixed_ref[rows, cols]
            totals += totals_ref[rows, cols]
            out[rows, cols] = (mixed / totals).astype(bf16)


def attend_rest(depth, q, mixed, totals, pages, slots, inner):
    smem = pl.BlockSpec(memory_space=pltpu.SMEM)
    vmem = pl.BlockSpec(memory_space=pltpu.VMEM)
    return pl.pallas_call(
        functools.partial(attend_rest_kernel, inner, slots),
        in_specs=[smem] + [vmem] * (3 + len(slots)),
        out_specs=vmem,
        out_shape=jax.ShapeDtypeStruct(q.shape, bf16),
        compiler_params=params(),
        cost_estimate=cost(),
        name="attend_rest",
    )(depth, q, mixed, totals, *pages)


def projected_heads(slices, rows, mine, theirs, w_mine, w_theirs):
    def half(parts, weights):
        total = None
        for part, (start, size) in zip(parts, slices):
            weight = weights[start : start + size, :]
            term = jnp.dot(part[rows, :], weight, preferred_element_type=f32)
            total = term if total is None else total + term
        return total

    return half(mine, w_mine) + half(theirs, w_theirs)


def partial_kernel(slices, hidden, rate, w_mine, w_theirs, *refs):
    count = len(slices)
    mine, theirs = refs[:count], refs[count : 2 * count]
    base, out = refs[2 * count :]
    for low in range(0, out.shape[0], PAGE):
        rows = slice(low, low + PAGE)
        out[rows, :] = projected_heads(slices, rows, mine, theirs, w_mine, w_theirs)
        anchor = hidden[rows, :].astype(f32) * row_scale_of(hidden[rows, :])
        base[rows, :] = anchor - rate[...] * anchor


def partial_branch(slices, hidden_in, rate, w_mine, w_theirs, mine, theirs):
    out = jax.ShapeDtypeStruct(hidden_in.shape, f32)
    vmem = pl.BlockSpec(memory_space=pltpu.VMEM)
    return pl.pallas_call(
        functools.partial(partial_kernel, slices),
        in_specs=[vmem] * (4 + 2 * len(slices)),
        out_specs=[vmem] * 2,
        out_shape=[out, out],
        compiler_params=params(),
        cost_estimate=cost(),
        name="partial_branch",
    )(hidden_in, rate, w_mine, w_theirs, *mine, *theirs)


def add_kernel(slices, begun, w_mine, w_theirs, *refs):
    count = len(slices)
    mine, theirs, out = refs[:count], refs[count : 2 * count], refs[2 * count]
    for low in range(0, out.shape[0], PAGE):
        rows = slice(low, low + PAGE)
        term = projected_heads(slices, rows, mine, theirs, w_mine, w_theirs)
        out[rows, :] = begun[rows, :] + term


def add_branch(slices, begun, w_mine, w_theirs, mine, theirs):
    vmem = pl.BlockSpec(memory_space=pltpu.VMEM)
    return pl.pallas_call(
        functools.partial(add_kernel, slices),
        in_specs=[vmem] * (3 + 2 * len(slices)),
        out_specs=vmem,
        out_shape=jax.ShapeDtypeStruct(begun.shape, f32),
        compiler_params=params(),
        cost_estimate=cost(),
        name="add_branch",
    )(begun, w_mine, w_theirs, *mine, *theirs)


def finish_kernel(slices, base, w_mine, w_theirs, rate, begun, *refs):
    count = len(slices)
    mine, theirs = refs[:count], refs[count : 2 * count]
    out, buf, sem = refs[2 * count :]
    step = buf.shape[1]
    copies = []
    for low in range(0, base.shape[0], PAGE):
        rows = slice(low, low + PAGE)
        whole = begun[rows, :] + projected_heads(slices, rows, mine, theirs, w_mine, w_theirs)
        for inner in range(0, PAGE, step):
            i = (low + inner) // step
            rows = slice(i * step, (i + 1) * step)
            branch = whole[inner : inner + step, :]
            mean = jnp.mean(branch * branch, axis=-1, keepdims=True)
            updated = base[rows, :] + rate[...] * (branch * lax.rsqrt(mean + epsilon))
            scale = lax.rsqrt(jnp.mean(updated * updated, axis=-1, keepdims=True) + epsilon)
            buf[i] = (updated * scale).astype(bf16)
            copy = pltpu.make_async_copy(buf.at[i], out.at[pl.ds(i * step, step)], sem.at[i])
            copy.start()
            copies.append(copy)
    for copy in copies:
        copy.wait()


def finish(slices, base, w_mine, w_theirs, rate, begun, mine, theirs):
    tokens, depth = base.shape
    steps = 8
    vmem = pl.BlockSpec(memory_space=pltpu.VMEM)
    return pl.pallas_call(
        functools.partial(finish_kernel, slices),
        in_specs=[vmem] * (5 + 2 * len(slices)),
        out_specs=pl.BlockSpec(memory_space=pltpu.HBM),
        out_shape=jax.ShapeDtypeStruct((tokens, depth), bf16),
        scratch_shapes=[
            pltpu.VMEM((steps, tokens // steps, depth), bf16),
            pltpu.SemaphoreType.DMA((steps,)),
        ],
        compiler_params=params(),
        cost_estimate=cost(),
        name="finish",
    )(base, w_mine, w_theirs, rate, begun, *mine, *theirs)


def body(
    hidden_in,
    w_query,
    w_key,
    w_value,
    w_out,
    head_gain,
    eigen_rate,
    pool_keys,
    pool_values,
    req_len,
    prefix_len,
    prefix_pages,
    placement,
):
    devices = lax.axis_size("blk")
    here = lax.axis_index("blk").astype(jnp.int32).reshape(1)
    kv_index = lax.axis_index("kv").astype(jnp.int32).reshape(1)
    blocks = hidden_in.shape[0] // PAGE
    gain = head_gain.reshape(1, -1)
    rate = eigen_rate.reshape(1, -1)
    page_offsets = [slot * devices // PMAX + 1 for slot in range(PMAX)]
    block_offsets = [(2 * b + 1) * devices // (2 * blocks) for b in range(blocks)]

    assert blocks == lax.axis_size("kv") == 2
    relay_send = split_rows(hidden_in, kv_index)
    page_send = pack(
        pool_keys, pool_values, prefix_pages.T, here, devices, page_offsets, relay_send
    )
    projected = project(hidden_in, w_query, w_key, w_value, gain)

    def fetch(block, slot):
        return over_blk(block, [devices - page_offsets[slot]] * 2)

    relay_mine = over_blk(relay_send, block_offsets)
    ready = projected[0][0]
    first = {slot: fetch(page_send[0][slot], slot) for slot in SLOT_ORDER}
    first[0] = fetch(after(page_send[0][0], ready, relay_mine), 0)
    arrived = [first[slot] for slot in SLOT_ORDER]
    second = {}
    for slot in PAGE_ORDER:
        gate = (ready, relay_mine, *arrived, first[0])
        second[slot] = fetch(after(page_send[1][slot], *gate), slot)
    pages = [[got[slot] for slot in PAGE_ORDER] for got in (first, second)]
    w_theirs = from_behind(w_out, "kv", 1)
    relay_theirs = from_behind(after(relay_mine, w_theirs, *arrived, first[0]), "kv", 1)
    new_keys, new_values = relay_project(
        relay_mine, relay_theirs, w_key, w_value, gain, kv_index, here, placement, block_offsets
    )

    mine, theirs, slices = [[], []], [[], []], [[], []]
    units = list(zip(unit_slices(), projected))

    def swap(g, start, size, attended):
        mine[g].append(attended)
        theirs[g].append(from_behind(attended, "kv", 1))
        slices[g].append((start, size))

    for (g, inner, start, size), (q, k, v) in units:
        if g == 0:
            swap(g, start, size, attend(req_len, prefix_len, q, k, v, pages[0], PAGE_ORDER, inner))
    base, begun = partial_branch(
        slices[0], hidden_in, rate, w_out, after(w_theirs, new_keys), mine[0], theirs[0]
    )
    early, late = PAGE_ORDER[:EARLY], PAGE_ORDER[EARLY:]
    sums = []
    for (g, inner, _, _), (q, k, v) in units:
        if g:
            q = after(q, new_keys, begun)
            sums.append(attend(req_len, prefix_len, q, k, v, pages[g][:EARLY], early, inner))
    rest = [unit for unit in units if unit[0][0]]
    for ((g, inner, start, size), (q, _, _)), (mixed, totals) in zip(rest, sums):
        q = after(q, *[total for _, total in sums])
        swap(g, start, size, attend_rest(prefix_len, q, mixed, totals, pages[g][EARLY:], late, inner))
    begun = add_branch(slices[1][:-1], begun, w_out, w_theirs, mine[1][:-1], theirs[1][:-1])
    layer_out = finish(
        slices[1][-1:], base, w_out, w_theirs, rate, begun, mine[1][-1:], theirs[1][-1:]
    )
    return (layer_out, new_keys, new_values)


def solution(mesh):
    in_specs = (
        P("blk", None),
        P(None, "kv"),
        P(None, "kv"),
        P(None, "kv"),
        P("kv", None),
        P("kv"),
        P(),
        P("blk", None, "kv"),
        P("blk", None, "kv"),
        P("blk"),
        P("blk"),
        P(),
        P(),
    )
    out_specs = (P("blk", None), P("blk", None, "kv"), P("blk", None, "kv"))
    return jax.shard_map(body, mesh=mesh, in_specs=in_specs, out_specs=out_specs, check_vma=False)
```
